32 devices in a mesh: dp: 8 (over y, x, core), vocab: 4 (over z).
Axes of the slice: x: 2, y: 2, z: 4, core: 2. Of those that a mesh axis runs over, the one named last changes fastest.
Arguments:
- tokens: int32 [64, 512], P(('dp', 'vocab')), may hold values from 5 to 4100
- picks: int32 [64, 120], P(('dp', 'vocab')), may hold values from 0 to 512, as said below
- species: int32 [64], P(('dp', 'vocab')), may hold values from 0 to 7
- table: float32 [4104, 768], P('vocab', 'dp')
- table_m: float32 [4104, 768], P('vocab', 'dp'), may hold values from -1.9073486e-05 to 1.9073486e-05
- table_v: float32 [4104, 768], P('vocab', 'dp'), may hold values from 9.233324e-12 to 3.6933297e-11
- qkv_w: float32 [768, 2304], P(('dp', 'vocab')), may hold values from -0.21875 to 0.21875
- qkv_m: float32 [768, 2304], P(('dp', 'vocab')), may hold values from -1.9073486e-05 to 1.9073486e-05
- qkv_v: float32 [768, 2304], P(('dp', 'vocab')), may hold values from 9.233324e-12 to 3.6933297e-11
- out_w: float32 [768, 768], P(('dp', 'vocab')), may hold values from -1.75 to 1.75
- out_m: float32 [768, 768], P(('dp', 'vocab')), may hold values from -1.9073486e-05 to 1.9073486e-05
- out_v: float32 [768, 768], P(('dp', 'vocab')), may hold values from 9.233324e-12 to 3.6933297e-11
- up_w: float32 [768, 3072], P(('dp', 'vocab')), may hold values from -0.21875 to 0.21875
- up_m: float32 [768, 3072], P(('dp', 'vocab')), may hold values from -1.9073486e-05 to 1.9073486e-05
- up_v: float32 [768, 3072], P(('dp', 'vocab')), may hold values from 9.233324e-12 to 3.6933297e-11
- down_w: float32 [3072, 768], P(('dp', 'vocab')), may hold values from -0.109375 to 0.109375
- down_m: float32 [3072, 768], P(('dp', 'vocab')), may hold values from -1.9073486e-05 to 1.9073486e-05
- down_v: float32 [3072, 768], P(('dp', 'vocab')), may hold values from 9.233324e-12 to 3.6933297e-11
- trans_w: float32 [768, 768], P(('dp', 'vocab')), may hold values from -0.21875 to 0.21875
- trans_m: float32 [768, 768], P(('dp', 'vocab')), may hold values from -1.9073486e-05 to 1.9073486e-05
- trans_v: float32 [768, 768], P(('dp', 'vocab')), may hold values from 9.233324e-12 to 3.6933297e-11
- vectors: float32 [768, 14], P(('dp', 'vocab'))
- vectors_m: float32 [768, 14], P(('dp', 'vocab')), may hold values from -7.6293945e-05 to 7.6293945e-05
- vectors_v: float32 [768, 14], P(('dp', 'vocab')), may hold values from 1.4773319e-10 to 5.9093275e-10
Outputs:
- table_first: float32 [4104, 768], P('vocab', 'dp')
- table_second: float32 [4104, 768], P('vocab', 'dp')
- table_new: float32 [4104, 768], P('vocab', 'dp')
- table_copy: bfloat16 [4104, 768], P('vocab', 'dp')
- qkv_first: float32 [768, 2304], P(('dp', 'vocab'))
- qkv_second: float32 [768, 2304], P(('dp', 'vocab'))
- qkv_new: float32 [768, 2304], P(('dp', 'vocab'))
- qkv_copy: bfloat16 [768, 2304], P(('dp', 'vocab'))
- out_first: float32 [768, 768], P(('dp', 'vocab'))
- out_second: float32 [768, 768], P(('dp', 'vocab'))
- out_new: float32 [768, 768], P(('dp', 'vocab'))
- out_copy: bfloat16 [768, 768], P(('dp', 'vocab'))
- up_first: float32 [768, 3072], P(('dp', 'vocab'))
- up_second: float32 [768, 3072], P(('dp', 'vocab'))
- up_new: float32 [768, 3072], P(('dp', 'vocab'))
- up_copy: bfloat16 [768, 3072], P(('dp', 'vocab'))
- down_first: float32 [3072, 768], P(('dp', 'vocab'))
- down_second: float32 [3072, 768], P(('dp', 'vocab'))
- down_new: float32 [3072, 768], P(('dp', 'vocab'))
- down_copy: bfloat16 [3072, 768], P(('dp', 'vocab'))
- trans_first: float32 [768, 768], P(('dp', 'vocab'))
- trans_second: float32 [768, 768], P(('dp', 'vocab'))
- trans_new: float32 [768, 768], P(('dp', 'vocab'))
- trans_copy: bfloat16 [768, 768], P(('dp', 'vocab'))
- vectors_first: float32 [768, 14], P(('dp', 'vocab'))
- vectors_second: float32 [768, 14], P(('dp', 'vocab'))
- vectors_new: float32 [768, 14], P(('dp', 'vocab'))
- loss_sum: float32 [], replicated
- present: float32 [], replicated
- grad_norm: float32 [], replicated
The draws below stay inside these ranges and needn't reach their ends.
Inputs may be any that keep to these rules, and one draw needn't show every extreme that they name: `picks`: each sequence's row lists whole masked spans of 6 consecutive positions (span starts are multiples of 6, spans disjoint), 6 entries a span, then 512 in every unused slot; some sequence fills all 120 slots.
All inputs are finite; a program needn't handle non-finite values.
Results may differ from the reference program's by a relative error of at most 0.018.
Values may be sent and summed in bfloat16 or wider, within the bound.
A program may use at most 192 MiB of HBM per device.

```python
import math
import jax
import jax.numpy as jnp
from jax import lax

D = 768
HEADS = 12
HD = 64
FF = 3072
VOCAB = 4104
L = 512
SEQ_DEV = 2
SPANS_MAX = 20
NSPEC = 8
NVEC = 14
STEP = 10
SEQS = 64
PICKS = 120
VREAL = 4101
NPARAM = 10830336
N_DP = 8
N_VOCAB = 4


def draw_table(key, part):
    key = jax.random.fold_in(key, 11)
    rows = jnp.arange(VOCAB, dtype=jnp.float32)[:, None] / VOCAB
    base = jax.random.normal(key, (VOCAB, D), jnp.float32)
    scale = 1.0 + 2.0 * rows
    return base * scale * D ** (-0.5)


def draw_vectors(key, part):
    key = jax.random.fold_in(key, 12)
    key_gain, key_shift, key_mask = jax.random.split(key, 3)
    across = jnp.arange(D, dtype=jnp.float32)[:, None] / D
    gains = (0.5 + across) * jax.random.uniform(key_gain, (D, 4), jnp.float32, 0.8, 1.25)
    shifts = 0.1 * jax.random.normal(key_shift, (D, 9), jnp.float32)
    mask_column = jax.random.normal(key_mask, (D,), jnp.float32)
    columns = [gains[:, 0], shifts[:, 0], gains[:, 1], shifts[:, 1], gains[:, 2], shifts[:, 2], gains[:, 3], shifts[:, 3]]
    columns = columns + [shifts[:, index] for index in range(4, 9)] + [mask_column * D ** (-0.5)]
    return jnp.stack(columns, axis=1)


def draw_picks(key, part):
    key = jax.random.fold_in(key, 13)
    key_jitter, key_full, key_order = jax.random.split(key, 3)
    slots = L // 6
    seq = jnp.arange(SEQS, dtype=jnp.int32)
    device = seq // SEQ_DEV
    data_pos = device // N_VOCAB
    vocab_pos = device % N_VOCAB
    numer = data_pos * max(N_VOCAB - 1, 1) + vocab_pos * max(N_DP - 1, 1)
    denom = 2 * max(N_DP - 1, 1) * max(N_VOCAB - 1, 1)
    least = max(SPANS_MAX // 3, 1)
    count = least + (SPANS_MAX - least) * numer // denom - jax.random.randint(key_jitter, (SEQS,), 0, 2)
    count = jnp.clip(count, 1, SPANS_MAX)
    full = jax.random.randint(key_full, (), 0, SEQS)
    count = jnp.where(seq == full, SPANS_MAX, count)
    scores = jax.random.randint(key_order, (SEQS, slots), 0, 1 << 20) * slots + jnp.arange(slots, dtype=jnp.int32)[None, :]
    order = jnp.argsort(scores, axis=1)[:, :SPANS_MAX]
    starts = order * 6
    spots = starts[:, :, None] + jnp.arange(6, dtype=jnp.int32)[None, None, :]
    used = jnp.arange(SPANS_MAX, dtype=jnp.int32)[None, :, None] < count[:, None, None]
    return jnp.where(used, spots, L).reshape(SEQS, PICKS).astype(jnp.int32)


def with_ends(values, own_key, low, largest):
    shape = values.shape
    index_at = [jax.random.randint(jax.random.fold_in(own_key, axis), (), 0, shape[axis]) for axis in range(len(shape))]
    values = values.at[tuple(index_at)].set(low)
    longest = shape.index(max(shape))
    index_at[longest] = (index_at[longest] + 1) % shape[longest]
    return values.at[tuple(index_at)].set(largest)


def block_levels(stream_key, extent, pieces, smallest, largest):
    def one(axis_at, blocks):
        heights = jax.random.uniform(jax.random.fold_in(jax.random.fold_in(stream_key, 6), axis_at), (blocks,), jnp.float32, smallest / len(pieces), largest / len(pieces))
        return jnp.repeat(jnp.exp(heights), extent[axis_at] // blocks).reshape((-1,) + (1,) * (len(extent) - axis_at - 1))

    factor_of = one(*pieces[0])
    for cut in pieces[1:]:
        factor_of = factor_of * one(*cut)
    return factor_of


def normal_values(key, extent, width, bound, pieces=(), kind=jnp.bfloat16):
    array = width * jax.random.normal(key, extent, jnp.float32)
    if pieces:
        array = array * block_levels(key, extent, pieces, -0.22, 0.18)
    return jnp.clip(array, -bound, bound).astype(kind)


def setup_inputs(seed: int = 0) -> dict:
    seeds = jax.random.split(jax.random.key(seed), 25)
    tokens = with_ends(jax.random.randint(seeds[0], (SEQS, L), 5, VREAL), jax.random.fold_in(seeds[0], 1), 5, VREAL - 1).astype(jnp.int32)
    picks = draw_picks(jax.random.fold_in(seeds[24], 71), 0)
    species = with_ends(jax.random.randint(seeds[2], (SEQS,), 0, NSPEC), jax.random.fold_in(seeds[2], 1), 0, NSPEC - 1).astype(jnp.int32)
    table = draw_table(jax.random.fold_in(seeds[24], 71), 0)
    table_m = normal_values(seeds[4], (VOCAB, D), (0.01 * NPARAM ** -0.5), 1.9073486328125e-05, ((0, 4), (1, 8)), jnp.float32)
    table_v = jnp.clip(jnp.exp(math.log(3.6933296698737905e-11) - 1.3862944 * jax.random.uniform(seeds[5], (VOCAB, D), jnp.float32) ** block_levels(seeds[5], (VOCAB, D), ((0, 4), (1, 8)), -0.2, 0.2)), 9.233324174684476e-12, 3.6933296698737905e-11)
    qkv_w = normal_values(seeds[6], (D, 3 * D), D ** -0.5, 0.21875, ((0, 32),), jnp.float32)
    qkv_m = normal_values(seeds[7], (D, 3 * D), (0.01 * NPARAM ** -0.5), 1.9073486328125e-05, ((0, 32),), jnp.float32)
    qkv_v = jnp.clip(jnp.exp(math.log(3.6933296698737905e-11) - 1.3862944 * jax.random.uniform(seeds[8], (D, 3 * D), jnp.float32) ** block_levels(seeds[8], (D, 3 * D), ((0, 32),), -0.2, 0.2)), 9.233324174684476e-12, 3.6933296698737905e-11)
    out_w = normal_values(seeds[9], (D, D), (D * 8 // L) ** -0.5, 1.75, ((0, 32),), jnp.float32)
    out_m = normal_values(seeds[10], (D, D), (0.01 * NPARAM ** -0.5), 1.9073486328125e-05, ((0, 32),), jnp.float32)
    out_v = jnp.clip(jnp.exp(math.log(3.6933296698737905e-11) - 1.3862944 * jax.random.uniform(seeds[11], (D, D), jnp.float32) ** block_levels(seeds[11], (D, D), ((0, 32),), -0.2, 0.2)), 9.233324174684476e-12, 3.6933296698737905e-11)
    up_w = normal_values(seeds[12], (D, FF), D ** -0.5, 0.21875, ((0, 32),), jnp.float32)
    up_m = normal_values(seeds[13], (D, FF), (0.01 * NPARAM ** -0.5), 1.9073486328125e-05, ((0, 32),), jnp.float32)
    up_v = jnp.clip(jnp.exp(math.log(3.6933296698737905e-11) - 1.3862944 * jax.random.uniform(seeds[14], (D, FF), jnp.float32) ** block_levels(seeds[14], (D, FF), ((0, 32),), -0.2, 0.2)), 9.233324174684476e-12, 3.6933296698737905e-11)
    down_w = normal_values(seeds[15], (FF, D), FF ** -0.5, 0.109375, ((0, 32),), jnp.float32)
    down_m = normal_values(seeds[16], (FF, D), (0.01 * NPARAM ** -0.5), 1.9073486328125e-05, ((0, 32),), jnp.float32)
    down_v = jnp.clip(jnp.exp(math.log(3.6933296698737905e-11) - 1.3862944 * jax.random.uniform(seeds[17], (FF, D), jnp.float32) ** block_levels(seeds[17], (FF, D), ((0, 32),), -0.2, 0.2)), 9.233324174684476e-12, 3.6933296698737905e-11)
    trans_w = normal_values(seeds[18], (D, D), D ** -0.5, 0.21875, ((0, 32),), jnp.float32)
    trans_m = normal_values(seeds[19], (D, D), (0.01 * NPARAM ** -0.5), 1.9073486328125e-05, ((0, 32),), jnp.float32)
    trans_v = jnp.clip(jnp.exp(math.log(3.6933296698737905e-11) - 1.3862944 * jax.random.uniform(seeds[20], (D, D), jnp.float32) ** block_levels(seeds[20], (D, D), ((0, 32),), -0.2, 0.2)), 9.233324174684476e-12, 3.6933296698737905e-11)
    vectors = draw_vectors(jax.random.fold_in(seeds[24], 71), 0)
    vectors_m = normal_values(seeds[22], (D, NVEC), (0.04 * NPARAM ** -0.5), 7.62939453125e-05, ((0, 32),), jnp.float32)
    vectors_v = jnp.clip(jnp.exp(math.log(5.909327471798065e-10) - 1.3862944 * jax.random.uniform(seeds[23], (D, NVEC), jnp.float32) ** block_levels(seeds[23], (D, NVEC), ((0, 32),), -0.2, 0.2)), 1.4773318679495162e-10, 5.909327471798065e-10)
    return dict(tokens=tokens, picks=picks, species=species, table=table, table_m=table_m, table_v=table_v, qkv_w=qkv_w, qkv_m=qkv_m, qkv_v=qkv_v, out_w=out_w, out_m=out_m, out_v=out_v, up_w=up_w, up_m=up_m, up_v=up_v, down_w=down_w, down_m=down_m, down_v=down_v, trans_w=trans_w, trans_m=trans_m, trans_v=trans_v, vectors=vectors, vectors_m=vectors_m, vectors_v=vectors_v)


@jax.custom_vjp
def low(v):
    return lax.optimization_barrier(v.astype(jnp.bfloat16)).astype(jnp.float32)

@jax.custom_vjp
def low_back(v):
    return v

def low_keep(v):
    return (low(v), None)

def low_pass(kept, grad):
    return (grad,)

def back_keep(v):
    return (v, None)

def back_low(kept, grad):
    return (low(grad),)
low.defvjp(low_keep, low_pass)
low_back.defvjp(back_keep, back_low)
HIGH = lax.Precision.HIGHEST
norm_eps = 1e-05
clip_limit = 0.01
matrix_rate = 0.06
vector_rate = 0.5
decay_rate = 0.01
adam_eps = 1e-08

def product(left, right):
    return jnp.dot(left, right, precision=HIGH, preferred_element_type=jnp.float32)

def layer_norm(value, norm_gain, norm_shift):
    row_mean = lax.optimization_barrier(jnp.mean(value, axis=-1, keepdims=True))
    centered_input = value - row_mean
    var = lax.optimization_barrier(jnp.mean(centered_input * centered_input, axis=-1, keepdims=True))
    return centered_input * lax.rsqrt(var + norm_eps) * norm_gain + norm_shift

def gelu(value):
    return jax.nn.gelu(value, approximate=False)

def attend(qkv):
    query = qkv[:, :D].reshape(L, HEADS, HD)
    keys = qkv[:, D:2 * D].reshape(L, HEADS, HD)
    values = qkv[:, 2 * D:].reshape(L, HEADS, HD)
    scores = low_back(jnp.einsum('qhd,khd->hqk', query, keys, precision=HIGH) * HD ** (-0.5))
    probs = low(jax.nn.softmax(scores, axis=-1))
    result = jnp.einsum('hqk,khd->qhd', probs, values, precision=HIGH).reshape(L, D)
    return low_back(low(result))

def block_loss(lowered, ids, masked, spot, target, weight, onehot):
    table, qkv_w, out_w, up_w, down_w, trans_w, vector_params = lowered
    count = ids.shape[0]
    emb = low_back(jnp.where(masked[:, :, None], vector_params[:, 13], table[ids]))
    stream_zero = layer_norm(emb, vector_params[:, 0], vector_params[:, 1])
    bias = jnp.concatenate([vector_params[:, 8], jnp.zeros((D,), vector_params.dtype), vector_params[:, 9]])
    qkv = low_back(low(product(low(stream_zero), qkv_w) + bias))
    att = jax.vmap(attend)(qkv)
    output_projection = low_back(product(att, out_w) + vector_params[:, 10])
    stream_one = layer_norm(stream_zero + output_projection, vector_params[:, 2], vector_params[:, 3])
    hidden = low_back(product(low(stream_one), up_w))
    feedforward_block = low_back(product(low(gelu(hidden)), down_w) + vector_params[:, 11])
    stream_two = layer_norm(stream_one + feedforward_block, vector_params[:, 4], vector_params[:, 5])
    rows = stream_two[jnp.arange(count)[:, None], spot].reshape(-1, D)
    trans = low_back(product(low(rows), trans_w) + vector_params[:, 12])
    latent_state = layer_norm(gelu(trans), vector_params[:, 6], vector_params[:, 7])
    logits = low_back(product(low(latent_state), table.T))
    logits = jnp.where(jnp.arange(VOCAB)[None, :] < VREAL, logits, -1e+30)
    lse = jax.nn.logsumexp(logits, axis=-1)
    chosen = jnp.take_along_axis(logits, target.reshape(-1, 1), axis=1)[:, 0]
    loss_rows = lse - chosen
    return (jnp.sum(weight.reshape(-1) * loss_rows), lax.optimization_barrier(jnp.sum(onehot.reshape(-1, NSPEC) * loss_rows[:, None], axis=0)))

def adamw(weight, first, second, gradient, rate):
    first = 0.5 * first + 0.5 * gradient
    second = 0.5 * second + 0.5 * gradient * gradient
    fix = 1.0 - 0.5 ** STEP
    step = first / fix / (jnp.sqrt(second / fix) + adam_eps)
    return (first, second, weight - rate * (step + decay_rate * weight))

def reference(tokens, picks, species, table, table_m, table_v, qkv_w, qkv_m, qkv_v, out_w, out_m, out_v, up_w, up_m, up_v, down_w, down_m, down_v, trans_w, trans_m, trans_v, vectors, vectors_m, vectors_v):
    positions = jnp.arange(L, dtype=jnp.int32)
    masked = jnp.any(picks[:, :, None] == positions[None, None, :], axis=1)
    inputs = tokens.astype(jnp.int32)
    live = picks < L
    spot = jnp.minimum(picks, L - 1).astype(jnp.int32)
    target = jnp.take_along_axis(tokens, spot, axis=1).astype(jnp.int32)
    onehot = ((species[:, None, None] == jnp.arange(NSPEC)[None, None, :]) & live[:, :, None]).astype(jnp.float32)
    counts = lax.optimization_barrier(jnp.sum(onehot, axis=(0, 1)))
    present_mask = counts > 0
    present = jnp.sum(present_mask.astype(jnp.float32))
    inverse = jnp.where(present_mask, 1.0 / jnp.maximum(counts, 1.0), 0.0) / present
    weight = lax.optimization_barrier(jnp.sum(onehot * inverse, axis=-1))
    block_seqs = math.gcd(SEQS, max(1, 4096 // L))
    blocks = SEQS // block_seqs

    def split(value):
        return value.reshape((blocks, block_seqs) + value.shape[1:])
    data = (split(inputs), split(masked), split(spot), split(target), split(weight), split(onehot))

    def total_loss(params):
        lowered = tuple((low(p) for p in params))

        def advance(carry, item):
            part_loss, part_species = jax.checkpoint(block_loss)(lowered, *item)
            return ((carry[0] + part_loss, carry[1] + part_species), None)
        start = (jnp.zeros((), jnp.float32), jnp.zeros((NSPEC,), jnp.float32))
        (loss, by_species), _ = lax.scan(advance, start, data)
        return (loss, by_species)
    params = (table, qkv_w, out_w, up_w, down_w, trans_w, vectors)
    loss, grad_fn, by_species = jax.vjp(total_loss, params, has_aux=True)
    grads, = grad_fn(jnp.ones((), jnp.float32))
    square = sum((jnp.sum(g * g) for g in grads))
    grad_norm = jnp.sqrt(square)
    factor = jnp.minimum(1.0, clip_limit / (grad_norm + 1e-06))
    firsts = (table_m, qkv_m, out_m, up_m, down_m, trans_m, vectors_m)
    seconds = (table_v, qkv_v, out_v, up_v, down_v, trans_v, vectors_v)
    results = []
    for index in range(7):
        rate = vector_rate if index == 6 else matrix_rate
        results.append(adamw(params[index], firsts[index], seconds[index], grads[index] * factor, rate))
    loss_sum = jnp.sum(jnp.where(present_mask, by_species / jnp.maximum(counts, 1.0), 0.0))
    outs = []
    for index in range(6):
        first, second, new = results[index]
        outs.extend([first, second, new, new.astype(jnp.bfloat16)])
    outs.extend(list(results[6]))
    return (outs[0], outs[1], outs[2], outs[3], outs[4], outs[5], outs[6], outs[7], outs[8], outs[9], outs[10], outs[11], outs[12], outs[13], outs[14], outs[15], outs[16], outs[17], outs[18], outs[19], outs[20], outs[21], outs[22], outs[23], outs[24], outs[25], outs[26], loss_sum, present, grad_norm)
```

```python
import functools

import jax
import jax.numpy as jnp
from jax import lax
from jax.experimental import pallas as pl
from jax.experimental.pallas import tpu as pltpu
from jax.sharding import PartitionSpec as P

D = 768
HEADS = 12
HD = 64
FF = 3072
NSPEC = 8
NVEC = 14
STEP = 10
VREAL = 4101
MESH = pl.DeviceIdType.MESH
BF = jnp.bfloat16
F32 = jnp.float32

norm_eps = 1e-05
clip_limit = 0.01
matrix_rate = 0.06
vector_rate = 0.5
decay_rate = 0.01
adam_eps = 1e-08
floor_value = -1e30

VEC_AT = 3 * D
OUT_AT = VEC_AT + 256
UP_AT = OUT_AT + D
TRANS_AT = UP_AT + FF
JOIN = TRANS_AT + D
JOIN_PARTS = (
    (0, 1280, True),
    (1280, 1280, False),
    (OUT_AT, 768, True),
    (UP_AT, 1536, False),
    (UP_AT + 1536, 1536, True),
    (TRANS_AT, 768, False),
)
VMEM_LIMIT = 62 * 2**20


def padded(rows):
    return -(-rows // 128) * 128


def pack_parts(value):
    pieces = []
    for first, width, _ in JOIN_PARTS:
        half = width // 2
        pieces.append(
            jnp.concatenate([value[:, first : first + half], value[:, first + half : first + width]], axis=0)
        )
    return jnp.concatenate(pieces, axis=1)


def unpack_parts(value):
    rows = value.shape[0] // 2
    pieces = []
    for first, width, _ in JOIN_PARTS:
        at = first // 2
        piece = value[:, at : at + width // 2]
        pieces += [piece[:rows], piece[rows:]]
    return jnp.concatenate(pieces, axis=1)


class Place:
    def __init__(self, n_vocab):
        dp = lax.axis_index("dp")
        z = lax.axis_index("vocab")
        core = lax.rem(dp, 2)
        bit_x = lax.rem(lax.div(dp, 2), 2)
        bit_y = lax.div(dp, 4)
        self.dp, self.z, self.core, self.n_vocab = dp, z, core, n_vocab
        self.step_core = 1 - 2 * core
        self.step_x = 2 - 4 * bit_x
        self.step_y = 4 - 8 * bit_y

    def across(self, which):
        return self.dp + {"core": self.step_core, "x": self.step_x, "y": self.step_y}[which]

    def device(self, which):
        return (self.across(which), self.z)

    def along(self, k):
        return lax.rem(self.z + k, self.n_vocab)

    def greet(self):
        barrier = pltpu.get_barrier_semaphore()
        for which in ("core", "x", "y"):
            pl.semaphore_signal(barrier, inc=1, device_id=self.device(which), device_id_type=MESH)
        for k in range(1, self.n_vocab):
            pl.semaphore_signal(barrier, inc=1, device_id=(self.dp, self.along(k)), device_id_type=MESH)
        pl.semaphore_wait(barrier, 3 + self.n_vocab - 1)


def remote(src, dst, send, recv, device):
    return pltpu.make_async_remote_copy(
        src_ref=src, dst_ref=dst, send_sem=send, recv_sem=recv, device_id=device, device_id_type=MESH
    )


def block_view(ref, stride, offset, rows, first, width):
    def view(index):
        return ref.at[pl.ds(pl.multiple_of(index * stride + offset, 16), rows), pl.ds(first, width)]

    return view


def tile_sum(place, tile_ref, land, ring, send, recv):
    for i, which in enumerate(("core", "x", "y")):
        copy = remote(tile_ref, land.at[i], send.at[i], recv.at[i], place.device(which))
        copy.start()
        copy.wait()
        tile_ref[...] = tile_ref[...] + land[i]
    ring[place.z] = tile_ref[...]
    copies = []
    for k in range(1, place.n_vocab):
        copy = remote(
            tile_ref, ring.at[place.z], send.at[2 + k], recv.at[2 + k], (place.dp, place.along(k))
        )
        copy.start()
        copies.append(copy)
    for copy in copies:
        copy.wait()
    total = ring[0]
    for k in range(1, place.n_vocab):
        total = total + ring[k]
    return total


def gather_kernel(
    n_vocab, packed_ref, table_ref, down_ref, tile_in,
    join_out, down_out, table_out, tile_out,
    join, down, table, stage, tile, land, ring,
    z_send, z_recv, d_send, d_recv, out_sem, t_send, t_recv,
):
    place = Place(n_vocab)
    place.greet()
    dp, z = place.dp, place.z
    t_rows, t_cols = table_ref.shape
    rows = packed_ref.shape[0] // 2
    d_rows = down_ref.shape[0]
    started = []

    def go(copy):
        copy.start()
        started.append(copy)

    chunks = []
    z_slot = 0

    def along_z(slot, src, dst):
        for k in range(1, n_vocab):
            go(remote(src, dst, z_send.at[slot, k - 1], z_recv.at[slot, k - 1], (dp, place.along(k))))

    def wait_z(slot, src, dst):
        for k in range(1, n_vocab):
            remote(src, dst, z_send.at[slot, k - 1], z_recv.at[slot, k - 1], (dp, place.along(k))).wait_recv()

    def nothing():
        pass

    sub = t_rows // 3
    for j in range(3):
        src = table_ref.at[pl.ds(sub * j, sub), :]
        dst = table.at[
            pl.ds(pl.multiple_of(dp * t_rows + sub * j, 16), sub), pl.ds(pl.multiple_of(z * t_cols, 128), t_cols)
        ]
        along_z(z_slot, src, dst)
        half = n_vocab * t_cols // 2
        ready = functools.partial(wait_z, z_slot, src, dst)
        chunks.append((block_view(table, t_rows, sub * j, sub, 0, half), True, ready))
        chunks.append((block_view(table, t_rows, sub * j, sub, half, half), False, nothing))
        z_slot += 1
    table[
        pl.ds(pl.multiple_of(dp * t_rows, 16), t_rows), pl.ds(pl.multiple_of(z * t_cols, 128), t_cols)
    ] = table_ref[...]

    def assemble(first, width):
        half = width // 2
        at = first // 2
        lefts, rights = [], []
        for k in range(n_vocab):
            piece = stage[k, :, at : at + half].astype(F32)
            lefts.append(piece[:rows])
            rights.append(piece[rows:])
        where = pl.ds(pl.multiple_of(dp * rows * n_vocab, 16), rows * n_vocab)
        join[where, first : first + half] = jnp.concatenate(lefts, axis=0).astype(BF)
        join[where, first + half : first + width] = jnp.concatenate(rights, axis=0).astype(BF)

    def join_ready(slot, src, dst, first, width):
        wait_z(slot, src, dst)
        assemble(first, width)

    stage[z] = packed_ref[...]
    for first, width, x_first in JOIN_PARTS:
        src = packed_ref.at[:, pl.ds(first // 2, width // 2)]
        dst = stage.at[z, :, pl.ds(first // 2, width // 2)]
        along_z(z_slot, src, dst)
        ready = functools.partial(join_ready, z_slot, src, dst, first, width)
        chunks.append((block_view(join, rows * n_vocab, 0, rows * n_vocab, first, width), x_first, ready))
        z_slot += 1
    down[pl.ds(pl.multiple_of((dp * n_vocab + z) * d_rows, 16), d_rows), :] = down_ref[...]
    for j in range(2):
        half = D // 2
        src = down_ref.at[:, pl.ds(half * j, half)]
        dst = down.at[pl.ds(pl.multiple_of((dp * n_vocab + z) * d_rows, 16), d_rows), pl.ds(half * j, half)]
        along_z(z_slot, src, dst)
        ready = functools.partial(wait_z, z_slot, src, dst)
        chunks.append((block_view(down, d_rows * n_vocab, 0, d_rows * n_vocab, half * j, half), j == 0, ready))
        z_slot += 1

    tile[...] = tile_in[...]
    tile_out[...] = tile_sum(place, tile, land, ring, t_send, t_recv)

    def moves(i):
        view, x_first, _ = chunks[i]
        one, two = ("x", "y") if x_first else ("y", "x")
        own = dp
        a = place.across(one)
        b = place.across(two)
        ab = a + b - own

        def move(k, block, which):
            return remote(view(block), view(block), d_send.at[i, k], d_recv.at[i, k], place.device(which))

        flip = place.step_core
        sends = (
            move(0, own, one), move(1, own, two), move(2, a, two), move(3, own, "core"),
            move(4, a, "core"), move(5, b, "core"), move(6, ab, "core"),
        )
        arrivals = (
            move(0, a, one), move(1, b, two), move(2, ab, two), move(3, own + flip, "core"),
            move(4, a + flip, "core"), move(5, b + flip, "core"), move(6, ab + flip, "core"),
        )
        return sends, arrivals

    every = [moves(i) for i in range(len(chunks))]
    n = len(chunks)
    for turn in range(n + 3):
        i = turn
        if i < n:
            chunks[i][2]()
            sends, _ = every[i]
            go(sends[0])
            go(sends[1])
            go(sends[3])
        i = turn - 1
        if 0 <= i < n:
            sends, arrivals = every[i]
            arrivals[0].wait_recv()
            go(sends[2])
            go(sends[4])
        i = turn - 2
        if 0 <= i < n:
            sends, arrivals = every[i]
            arrivals[1].wait_recv()
            go(sends[5])
            arrivals[2].wait_recv()
            go(sends[6])
        i = turn - 3
        if 0 <= i < n:
            _, arrivals = every[i]
            for k in range(3, 7):
                arrivals[k].wait_recv()
    outs = [
        pltpu.make_async_copy(join, join_out, out_sem.at[0]),
        pltpu.make_async_copy(down, down_out, out_sem.at[1]),
        pltpu.make_async_copy(table, table_out, out_sem.at[2]),
    ]
    for copy in outs:
        copy.start()
    for copy in started:
        copy.wait_send()
    for copy in outs:
        copy.wait()


def gather_all(packed, table_t, down, tile, n_dp, n_vocab):
    rows = packed.shape[0] // 2 * n_vocab * n_dp
    t_rows, t_cols = table_t.shape
    join_shape = (rows, JOIN)
    down_shape = (down.shape[0] * n_vocab * n_dp, D)
    table_shape = (t_rows * n_dp, t_cols * n_vocab)
    n_chunks = 6 + len(JOIN_PARTS) + 2
    slots = 3 + len(JOIN_PARTS) + 2
    vmem = pl.BlockSpec(memory_space=pltpu.VMEM)
    anywhere = pl.BlockSpec(memory_space=pl.ANY)
    return pl.pallas_call(
        functools.partial(gather_kernel, n_vocab),
        out_shape=(
            jax.ShapeDtypeStruct(join_shape, BF),
            jax.ShapeDtypeStruct(down_shape, BF),
            jax.ShapeDtypeStruct(table_shape, BF),
            jax.ShapeDtypeStruct(tile.shape, F32),
        ),
        in_specs=[vmem] * 4,
        out_specs=(anywhere, anywhere, anywhere, vmem),
        scratch_shapes=[
            pltpu.VMEM(join_shape, BF),
            pltpu.VMEM(down_shape, BF),
            pltpu.VMEM(table_shape, BF),
            pltpu.VMEM((n_vocab,) + packed.shape, BF),
            pltpu.VMEM(tile.shape, F32),
            pltpu.VMEM((3,) + tile.shape, F32),
            pltpu.VMEM((n_vocab,) + tile.shape, F32),
            pltpu.SemaphoreType.DMA((slots, n_vocab - 1)),
            pltpu.SemaphoreType.DMA((slots, n_vocab - 1)),
            pltpu.SemaphoreType.DMA((n_chunks, 7)),
            pltpu.SemaphoreType.DMA((n_chunks, 7)),
            pltpu.SemaphoreType.DMA((3,)),
            pltpu.SemaphoreType.DMA((2 + n_vocab,)),
            pltpu.SemaphoreType.DMA((2 + n_vocab,)),
        ],
        compiler_params=pltpu.CompilerParams(
            collective_id=0, has_side_effects=True, vmem_limit_bytes=VMEM_LIMIT
        ),
    )(packed, table_t, down, tile)


def reduce_kernel(
    n_vocab, join_in, down_in, table_in, tile_in,
    join_out, down_out, table_out, tile_out,
    join, down, table, *rest,
):
    n_join = len(JOIN_PARTS)
    n_chunks = 6 + n_join + 2
    from_core = rest[:n_chunks]
    from_two = rest[n_chunks : 2 * n_chunks]
    from_one = rest[2 * n_chunks : 3 * n_chunks]
    (packed, z_join, z_down, z_table, tile, land, ring,
     in_sem, z_send, z_recv, d_send, d_recv, t_send, t_recv) = rest[3 * n_chunks :]
    place = Place(n_vocab)
    loads = [
        pltpu.make_async_copy(join_in, join, in_sem.at[0]),
        pltpu.make_async_copy(down_in, down, in_sem.at[1]),
        pltpu.make_async_copy(table_in, table, in_sem.at[2]),
    ]
    for copy in loads:
        copy.start()
    place.greet()
    dp, z = place.dp, place.z
    t_rows, t_cols = table_out.shape
    rows = join_out.shape[0] // 2
    d_rows = down_out.shape[0]
    sub = t_rows // 3
    started = []

    def go(copy):
        copy.start()
        started.append(copy)

    chunks = []
    for first, width, x_first in JOIN_PARTS:
        chunks.append((block_view(join, rows * n_vocab, 0, rows * n_vocab, first, width), x_first, 0))
    for j in range(2):
        half = D // 2
        chunks.append((block_view(down, d_rows * n_vocab, 0, d_rows * n_vocab, half * j, half), j == 0, 1))
    for j in range(3):
        half = n_vocab * t_cols // 2
        chunks.append((block_view(table, t_rows, sub * j, sub, 0, half), True, 2))
        chunks.append((block_view(table, t_rows, sub * j, sub, half, half), False, 2))

    def add_into(target, source):
        size = target.shape[0]

        def step(i, carry):
            at = pl.ds(pl.multiple_of(i * 16, 16), 16)
            target[at, :] = target[at, :] + source[at, :]
            return carry

        lax.fori_loop(0, size // 16, step, 0)

    def names(i):
        one, two = ("x", "y") if chunks[i][1] else ("y", "x")
        own = dp
        a = place.across(one)
        b = place.across(two)
        return one, two, (own, a, b, a + b - own)

    def to_core(i):
        view = chunks[i][0]
        _, _, blocks = names(i)
        return [
            remote(
                view(block + place.step_core), from_core[i].at[k], d_send.at[i, k], d_recv.at[i, k],
                place.device("core"),
            )
            for k, block in enumerate(blocks)
        ]

    def to_two(i):
        view = chunks[i][0]
        _, two, (own, a, b, ab) = names(i)
        return [
            remote(view(block), from_two[i].at[k], d_send.at[i, 4 + k], d_recv.at[i, 4 + k], place.device(two))
            for k, block in enumerate((b, ab))
        ]

    def to_one(i):
        view = chunks[i][0]
        one, _, (own, a, b, ab) = names(i)
        return [remote(view(a), from_one[i], d_send.at[i, 6], d_recv.at[i, 6], place.device(one))]

    def z_copies(slot, src_of, dst_of):
        return [
            remote(
                src_of(place.along(k)), dst_of(k - 1), z_send.at[slot, k - 1], z_recv.at[slot, k - 1],
                (dp, place.along(k)),
            )
            for k in range(1, n_vocab)
        ]

    def join_pack(first, width):
        half = width // 2
        at = first // 2
        block = join[
            pl.ds(pl.multiple_of(dp * rows * n_vocab, 16), rows * n_vocab), first : first + width
        ].astype(F32)
        for k in range(n_vocab):
            piece = block[k * rows : (k + 1) * rows]
            packed[k, :, at : at + half] = jnp.concatenate([piece[:, :half], piece[:, half:]], axis=0).astype(BF)

    z_jobs = []

    def finish(i):
        if i < n_join:
            first, width, _ = JOIN_PARTS[i]
            join_pack(first, width)
            cols = pl.ds(first // 2, width // 2)
            copies = z_copies(i, lambda to: packed.at[to, :, cols], lambda k: z_join.at[k, :, cols])
        elif i < n_join + 2:
            cols = pl.ds((i - n_join) * (D // 2), D // 2)
            copies = z_copies(
                i,
                lambda to: down.at[pl.ds(pl.multiple_of((dp * n_vocab + to) * d_rows, 16), d_rows), cols],
                lambda k: z_down.at[k, :, cols],
            )
        else:
            j = i - n_join - 2
            if j % 2 == 0:
                return
            j = j // 2
            copies = z_copies(
                n_join + 2 + j,
                lambda to: table.at[
                    pl.ds(pl.multiple_of(dp * t_rows + sub * j, 16), sub),
                    pl.ds(pl.multiple_of(to * t_cols, 128), t_cols),
                ],
                lambda k: z_table.at[k, pl.ds(sub * j, sub), :],
            )
        for copy in copies:
            go(copy)
        z_jobs.append(copies)

    n = n_chunks
    for turn in range(n + 3):
        i = turn
        if i < n:
            if i == 0:
                loads[0].wait()
            if i == n_join:
                loads[1].wait()
            if i == n_join + 2:
                loads[2].wait()
            for copy in to_core(i):
                go(copy)
        i = turn - 1
        if 0 <= i < n:
            view = chunks[i][0]
            _, _, (own, a, b, ab) = names(i)
            arrivals = to_core(i)
            for k, block in ((2, b), (3, ab)):
                arrivals[k].wait_recv()
                add_into(view(block), from_core[i].at[k])
            for copy in to_two(i):
                go(copy)
            for k, block in ((0, own), (1, a)):
                arrivals[k].wait_recv()
                add_into(view(block), from_core[i].at[k])
        i = turn - 2
        if 0 <= i < n:
            view = chunks[i][0]
            _, _, (own, a, b, ab) = names(i)
            arrivals = to_two(i)
            arrivals[1].wait_recv()
            add_into(view(a), from_two[i].at[1])
            for copy in to_one(i):
                go(copy)
            arrivals[0].wait_recv()
            add_into(view(own), from_two[i].at[0])
        i = turn - 3
        if 0 <= i < n:
            view = chunks[i][0]
            to_one(i)[0].wait_recv()
            add_into(view(dp), from_one[i])
            finish(i)
    for copies in z_jobs:
        for copy in copies:
            copy.wait_recv()
    square = jnp.zeros((), F32)
    whole = packed[z].astype(F32)
    for k in range(n_vocab - 1):
        whole = whole + z_join[k].astype(F32)
    join_out[...] = whole
    square = square + jnp.sum(whole * whole)
    whole = down[pl.ds(pl.multiple_of((dp * n_vocab + z) * d_rows, 16), d_rows), :].astype(F32)
    for k in range(n_vocab - 1):
        whole = whole + z_down[k].astype(F32)
    down_out[...] = whole
    square = square + jnp.sum(whole * whole)
    whole = table[
        pl.ds(pl.multiple_of(dp * t_rows, 16), t_rows), pl.ds(pl.multiple_of(z * t_cols, 128), t_cols)
    ].astype(F32)
    for k in range(n_vocab - 1):
        whole = whole + z_table[k].astype(F32)
    table_out[...] = whole
    square = square + jnp.sum(whole * whole)
    row = lax.broadcasted_iota(jnp.int32, tile.shape, 0)
    tile[...] = jnp.where(row == 0, square, tile_in[...])
    tile_out[...] = tile_sum(place, tile, land, ring, t_send, t_recv)
    for copy in started:
        copy.wait_send()


def reduce_all(g_join, g_down, g_table, tile, n_dp, n_vocab):
    rows = g_join.shape[0] // (n_dp * n_vocab)
    d_rows = g_down.shape[0] // (n_dp * n_vocab)
    t_rows = g_table.shape[0] // n_dp
    t_cols = g_table.shape[1] // n_vocab
    shapes = [(rows * n_vocab, width) for _, width, _ in JOIN_PARTS]
    shapes += [(d_rows * n_vocab, D // 2)] * 2
    shapes += [(t_rows // 3, n_vocab * t_cols // 2)] * 6
    slots = len(JOIN_PARTS) + 5
    vmem = pl.BlockSpec(memory_space=pltpu.VMEM)
    anywhere = pl.BlockSpec(memory_space=pl.ANY)
    dma = pltpu.SemaphoreType.DMA
    return pl.pallas_call(
        functools.partial(reduce_kernel, n_vocab),
        out_shape=(
            jax.ShapeDtypeStruct((2 * rows, JOIN // 2), F32),
            jax.ShapeDtypeStruct((d_rows, D), F32),
            jax.ShapeDtypeStruct((t_rows, t_cols), F32),
            jax.ShapeDtypeStruct(tile.shape, F32),
        ),
        in_specs=[anywhere, anywhere, anywhere, vmem],
        out_specs=(vmem,) * 4,
        scratch_shapes=[
            pltpu.VMEM(g_join.shape, BF),
            pltpu.VMEM(g_down.shape, BF),
            pltpu.VMEM(g_table.shape, BF),
        ]
        + [pltpu.VMEM((4,) + shape, BF) for shape in shapes]
        + [pltpu.VMEM((2,) + shape, BF) for shape in shapes]
        + [pltpu.VMEM(shape, BF) for shape in shapes]
        + [
            pltpu.VMEM((n_vocab, 2 * rows, JOIN // 2), BF),
            pltpu.VMEM((n_vocab - 1, 2 * rows, JOIN // 2), BF),
            pltpu.VMEM((n_vocab - 1, d_rows, D), BF),
            pltpu.VMEM((n_vocab - 1, t_rows, t_cols), BF),
            pltpu.VMEM(tile.shape, F32),
            pltpu.VMEM((3,) + tile.shape, F32),
            pltpu.VMEM((n_vocab,) + tile.shape, F32),
            dma((3,)),
            dma((slots, n_vocab - 1)),
            dma((slots, n_vocab - 1)),
            dma((len(shapes), 7)),
            dma((len(shapes), 7)),
            dma((2 + n_vocab,)),
            dma((2 + n_vocab,)),
        ],
        compiler_params=pltpu.CompilerParams(
            collective_id=1, has_side_effects=True, vmem_limit_bytes=VMEM_LIMIT
        ),
    )(g_join, g_down, g_table, tile)


def dot_low(left, right):
    return jnp.dot(left, right, preferred_element_type=F32)


def dot_left(left, right):
    return lax.dot_general(left, right, (((0,), (0,)), ((), ())), preferred_element_type=F32)


def dot_right(left, right):
    return lax.dot_general(left, right, (((1,), (1,)), ((), ())), preferred_element_type=F32)


def norm_forward(value, gain, shift):
    mean = jnp.mean(value, axis=-1, keepdims=True)
    centered = value - mean
    inverse = lax.rsqrt(jnp.mean(centered * centered, axis=-1, keepdims=True) + norm_eps)
    normal = centered * inverse
    return normal * gain + shift, normal, inverse


def norm_backward(gradient, normal, inverse, gain):
    gain_gradient = jnp.sum(gradient * normal, axis=0)
    shift_gradient = jnp.sum(gradient, axis=0)
    scaled = gradient * gain
    inner = jnp.mean(scaled, axis=-1, keepdims=True) + normal * jnp.mean(
        scaled * normal, axis=-1, keepdims=True
    )
    return inverse * (scaled - inner), gain_gradient, shift_gradient


def gelu(value):
    return 0.5 * value * (1.0 + lax.erf(value * 0.7071067811865476))


def gelu_slope(value):
    cdf = 0.5 * (1.0 + lax.erf(value * 0.7071067811865476))
    return cdf + value * jnp.exp(-0.5 * value * value) * 0.3989422804014327


def species_counts(picks, species, seq_len):
    live = (picks < seq_len).astype(F32)
    kinds = jnp.arange(NSPEC, dtype=jnp.int32)
    return jnp.sum((species[:, None] == kinds[None, :]).astype(F32) * jnp.sum(live, axis=1)[:, None], axis=0)


def local_step(tokens, picks, species, counts, join, down, table_t, block, wide):
    seqs, seq_len = tokens.shape
    slots = picks.shape[1]
    w_qkv = join[:, : 3 * D]
    vec = join[:, VEC_AT : VEC_AT + NVEC].astype(F32)
    w_out = join[:, OUT_AT : OUT_AT + D]
    w_up = join[:, UP_AT : UP_AT + FF]
    w_trans = join[:, TRANS_AT : TRANS_AT + D]

    masked = jnp.any(picks[:, :, None] == jnp.arange(seq_len, dtype=jnp.int32)[None, None, :], axis=1)
    masked_flat = masked.reshape(-1)
    live = (picks < seq_len).reshape(-1)
    spot = jnp.minimum(picks, seq_len - 1)
    row_index = (spot + jnp.arange(seqs, dtype=jnp.int32)[:, None] * seq_len).reshape(-1)
    target = jnp.take_along_axis(tokens, spot, axis=1).reshape(-1)
    row_species = jnp.broadcast_to(species[:, None], picks.shape).reshape(-1)

    cols = jnp.arange(table_t.shape[1], dtype=jnp.int32)
    col_real = cols % wide < block
    col_id = jnp.where(col_real, cols // wide * block + cols % wide, -1)
    inputs = jnp.where(masked, -2, tokens).reshape(-1)
    onehot = (inputs[:, None] == col_id[None, :]).astype(BF)
    embedded = jnp.where(masked_flat[:, None], vec[:, 13], dot_right(onehot, table_t))
    stream_zero, normal0, inverse0 = norm_forward(embedded, vec[:, 0], vec[:, 1])
    x0_low = stream_zero.astype(BF)
    keys = dot_low(x0_low, w_qkv[:, D : 2 * D]).astype(BF)
    values = (dot_low(x0_low, w_qkv[:, 2 * D :]) + vec[:, 9]).astype(BF)
    x0_rows = stream_zero[row_index]
    x0_rows_low = x0_rows.astype(BF)
    query = (dot_low(x0_rows_low, w_qkv[:, :D]) + vec[:, 8]).astype(BF)
    q4 = query.reshape(seqs, slots, HEADS, HD)
    k4 = keys.reshape(seqs, seq_len, HEADS, HD)
    v4 = values.reshape(seqs, seq_len, HEADS, HD)
    scores = jnp.einsum("sqhd,skhd->shqk", q4, k4, preferred_element_type=F32) * HD ** (-0.5)
    probs = jax.nn.softmax(scores, axis=-1)
    probs_low = probs.astype(BF)
    att = jnp.einsum("shqk,skhd->sqhd", probs_low, v4, preferred_element_type=F32)
    att_low = att.reshape(-1, D).astype(BF)
    stream_one, normal1, inverse1 = norm_forward(
        x0_rows + dot_low(att_low, w_out) + vec[:, 10], vec[:, 2], vec[:, 3]
    )
    x1_low = stream_one.astype(BF)
    hidden = dot_low(x1_low, w_up)
    hidden_low = gelu(hidden).astype(BF)
    stream_two, normal2, inverse2 = norm_forward(
        stream_one + dot_low(hidden_low, down) + vec[:, 11], vec[:, 4], vec[:, 5]
    )
    picked_low = stream_two.astype(BF)
    trans = dot_low(picked_low, w_trans) + vec[:, 12]
    latent, normal3, inverse3 = norm_forward(gelu(trans), vec[:, 6], vec[:, 7])
    latent_low = latent.astype(BF)
    logits = dot_low(latent_low, table_t)
    logits = jnp.where((col_real & (col_id < VREAL))[None, :], logits, floor_value)
    top = jnp.max(logits, axis=-1, keepdims=True)
    expo = jnp.exp(logits - top)
    total = jnp.sum(expo, axis=-1, keepdims=True)
    is_target = col_id[None, :] == target[:, None]
    hit = jnp.sum(jnp.where(is_target, logits, 0.0), axis=-1)
    loss_rows = (top + jnp.log(total))[:, 0] - hit
    kinds = jnp.arange(NSPEC, dtype=jnp.int32)
    own = ((row_species[:, None] == kinds[None, :]) & live[:, None]).astype(F32)
    species_loss = jnp.sum(own * loss_rows[:, None], axis=0)
    present_mask = counts > 0
    present = jnp.sum(present_mask.astype(F32))
    inverse = jnp.where(present_mask, 1.0 / jnp.maximum(counts, 1.0), 0.0) / present
    weight = jnp.sum(own * inverse[None, :], axis=-1)
    loss_part = jnp.sum(jnp.where(present_mask, species_loss / jnp.maximum(counts, 1.0), 0.0))
    d_logits = (weight[:, None] * (expo / total - is_target.astype(F32))).astype(BF)

    d_latent = dot_right(d_logits, table_t)
    d_act, d6, d7 = norm_backward(d_latent, normal3, inverse3, vec[:, 6])
    d_trans = (d_act * gelu_slope(trans)).astype(BF)
    g_trans = dot_left(picked_low, d_trans)
    d12 = jnp.sum(d_trans.astype(F32), axis=0)
    d_two, d4, d5 = norm_backward(dot_right(d_trans, w_trans), normal2, inverse2, vec[:, 4])
    d_ffn = d_two.astype(BF)
    d11 = jnp.sum(d_ffn.astype(F32), axis=0)
    g_down = dot_left(hidden_low, d_ffn)
    d_hidden = (dot_right(d_ffn, down) * gelu_slope(hidden)).astype(BF)
    g_up = dot_left(x1_low, d_hidden)
    d_one, d2, d3 = norm_backward(d_two + dot_right(d_hidden, w_up), normal1, inverse1, vec[:, 2])
    d_proj = d_one.astype(BF)
    d10 = jnp.sum(d_proj.astype(F32), axis=0)
    g_out = dot_left(att_low, d_proj)
    d_att = dot_right(d_proj, w_out).astype(BF).reshape(seqs, slots, HEADS, HD)
    d_probs = jnp.einsum("sqhd,skhd->shqk", d_att, v4, preferred_element_type=F32)
    delta = jnp.sum(d_probs * probs, axis=-1, keepdims=True)
    d_scores = (probs * (d_probs - delta)).astype(BF)
    d_q = jnp.einsum("shqk,skhd->sqhd", d_scores, k4, preferred_element_type=F32) * HD ** (-0.5)
    d_k = jnp.einsum("shqk,sqhd->skhd", d_scores, q4, preferred_element_type=F32) * HD ** (-0.5)
    d_v = jnp.einsum("shqk,sqhd->skhd", probs_low, d_att, preferred_element_type=F32)
    d_q = d_q.reshape(-1, D).astype(BF)
    d_k = d_k.reshape(-1, D).astype(BF)
    d_v = d_v.reshape(-1, D).astype(BF)
    d8 = jnp.sum(d_q.astype(F32), axis=0)
    d9 = jnp.sum(d_v.astype(F32), axis=0)
    g_q = dot_left(x0_rows_low, d_q)
    g_k = dot_left(x0_low, d_k)
    g_v = dot_left(x0_low, d_v)
    d_rows = d_one + dot_right(d_q, w_qkv[:, :D])
    d_zero = dot_right(d_k, w_qkv[:, D : 2 * D]) + dot_right(d_v, w_qkv[:, 2 * D :])
    d_zero = d_zero.at[row_index].add(jnp.where(live[:, None], d_rows, 0.0))
    d_emb, d0, d1 = norm_backward(d_zero, normal0, inverse0, vec[:, 0])
    d_emb_low = d_emb.astype(BF)
    d13 = jnp.sum(jnp.where(masked_flat[:, None], d_emb_low.astype(F32), 0.0), axis=0)
    g_table = dot_left(latent_low, d_logits) + dot_left(d_emb_low, onehot)
    g_vec = jnp.stack([d0, d1, d2, d3, d4, d5, d6, d7, d8, d9, d10, d11, d12, d13], axis=1)
    g_vec = jnp.pad(g_vec, ((0, 0), (0, OUT_AT - VEC_AT - NVEC)))
    g_join = jnp.concatenate([g_q, g_k, g_v, g_vec, g_out, g_up, g_trans], axis=1)
    return loss_part, present, g_join.astype(BF), g_down.astype(BF), g_table.astype(BF)


def adamw(weight, first, second, gradient, rate):
    first = 0.5 * first + 0.5 * gradient
    second = 0.5 * second + 0.5 * gradient * gradient
    fix = 1.0 - 0.5**STEP
    step = first / fix / (jnp.sqrt(second / fix) + adam_eps)
    return (first, second, weight - rate * (step + decay_rate * weight))


def body(
    n_dp, n_vocab, tokens, picks, species,
    table, table_m, table_v, qkv_w, qkv_m, qkv_v, out_w, out_m, out_v, up_w, up_m, up_v,
    down_w, down_m, down_v, trans_w, trans_m, trans_v, vectors, vectors_m, vectors_v,
):
    block, columns = table.shape
    wide = padded(block)
    rows = qkv_w.shape[0]
    own_kernels = n_dp == 8 and rows % 8 == 0 and columns % 48 == 0
    joined = jnp.concatenate(
        [qkv_w, jnp.pad(vectors, ((0, 0), (0, OUT_AT - VEC_AT - NVEC))), out_w, up_w, trans_w], axis=1
    ).astype(BF)
    down_low = down_w.astype(BF)
    table_t = jnp.pad(table.T.astype(BF), ((0, 0), (0, wide - block)))
    counts = species_counts(picks, species, tokens.shape[1])
    if own_kernels:
        tile = jnp.broadcast_to(jnp.pad(counts, (0, 128 - NSPEC))[None, :], (8, 128))
        join_all, down_all, table_all, tile = gather_all(
            pack_parts(joined), table_t, down_low, tile, n_dp, n_vocab
        )
        counts = tile[0, :NSPEC]
    else:
        both = ("dp", "vocab")
        join_all = lax.all_gather(joined, both, axis=0, tiled=True)
        down_all = lax.all_gather(down_low, both, axis=0, tiled=True)
        table_all = lax.all_gather(table_t, "vocab", axis=1, tiled=True)
        table_all = lax.all_gather(table_all, "dp", axis=0, tiled=True)
        counts = lax.psum(counts, both)
    loss, present, g_join, g_down, g_table = local_step(
        tokens, picks, species, counts, join_all, down_all, table_all, block, wide
    )
    if own_kernels:
        tile = jnp.full((8, 128), loss, F32)
        g_join, g_down, g_table, tile = reduce_all(g_join, g_down, g_table, tile, n_dp, n_vocab)
        g_join = unpack_parts(g_join)
        square, loss_sum = tile[0, 0], tile[1, 0]
    else:
        g_join = lax.psum_scatter(g_join.astype(F32), both, scatter_dimension=0, tiled=True)
        g_down = lax.psum_scatter(g_down.astype(F32), both, scatter_dimension=0, tiled=True)
        g_table = lax.psum_scatter(g_table, "dp", scatter_dimension=0, tiled=True)
        g_table = lax.psum_scatter(g_table, "vocab", scatter_dimension=1, tiled=True).astype(F32)
        square = jnp.sum(g_join * g_join) + jnp.sum(g_down * g_down) + jnp.sum(g_table * g_table)
        square, loss_sum = lax.psum((square, loss), both)
    grad_norm = jnp.sqrt(square)
    factor = jnp.minimum(1.0, clip_limit / (grad_norm + 1e-06))
    grads = (
        g_table[:, :block].T, g_join[:, : 3 * D], g_join[:, OUT_AT : OUT_AT + D], g_join[:, UP_AT : UP_AT + FF],
        g_down, g_join[:, TRANS_AT:], g_join[:, VEC_AT : VEC_AT + NVEC],
    )
    masters = (table, qkv_w, out_w, up_w, down_w, trans_w, vectors)
    firsts = (table_m, qkv_m, out_m, up_m, down_m, trans_m, vectors_m)
    seconds = (table_v, qkv_v, out_v, up_v, down_v, trans_v, vectors_v)
    outs = []
    for index in range(7):
        rate = vector_rate if index == 6 else matrix_rate
        first, second, new = adamw(masters[index], firsts[index], seconds[index], grads[index] * factor, rate)
        outs.extend([first, second, new])
        if index < 6:
            outs.append(new.astype(BF))
    return tuple(outs) + (loss_sum, present, grad_norm)


def solution(mesh):
    both = P(("dp", "vocab"), None)
    split = P("vocab", "dp")
    in_specs = (both, both, P(("dp", "vocab"))) + (split,) * 3 + (both,) * 18
    out_specs = (split,) * 4 + (both,) * 23 + (P(),) * 3
    step = functools.partial(body, mesh.shape["dp"], mesh.shape["vocab"])
    return jax.shard_map(step, mesh=mesh, in_specs=in_specs, out_specs=out_specs, check_vma=False)
```

```python
import functools

import jax
import jax.numpy as jnp
import numpy as np
from jax import lax
from jax.experimental import pallas as pl
from jax.experimental.pallas import tpu as pltpu
from jax.sharding import PartitionSpec as P

D = 768
HEADS = 12
HD = 64
FF = 3072
NSPEC = 8
NVEC = 14
STEP = 10
VREAL = 4101
MESH = pl.DeviceIdType.MESH
BF = jnp.bfloat16
F32 = jnp.float32

norm_eps = 1e-05
clip_limit = 0.01
matrix_rate = 0.06
vector_rate = 0.5
decay_rate = 0.01
adam_eps = 1e-08
floor_value = -1e30

VEC_AT = 3 * D
OUT_AT = VEC_AT + 256
UP_AT = OUT_AT + D
TRANS_AT = UP_AT + FF
JOIN = TRANS_AT + D
JOIN_PARTS = (
    (0, 1280, True),
    (1280, 1280, False),
    (OUT_AT, 768, True),
    (UP_AT, 1536, False),
    (UP_AT + 1536, 1536, True),
    (TRANS_AT, 768, False),
)
VMEM_LIMIT = 62 * 2**20


T_PARTS = 3
CORE, X, Y = range(3)


def padded(rows):
    return -(-rows // 128) * 128


def part_cols(wide):
    return wide // T_PARTS if wide % (128 * T_PARTS) == 0 else wide


def token_of(column, block, n_vocab, wide, xp):
    piece = part_cols(wide)
    inside = column % (piece * n_vocab)
    row = column // (piece * n_vocab) * piece + inside % piece
    return xp.where(row < block, inside // piece * block + row, -1)


class Place:
    def __init__(self, n_vocab):
        dp = lax.axis_index("dp")
        z = lax.axis_index("vocab")
        core = lax.rem(dp, 2)
        bit_x = lax.rem(lax.div(dp, 2), 2)
        bit_y = lax.div(dp, 4)
        self.dp, self.z, self.core, self.n_vocab = dp, z, core, n_vocab
        self.step_core = 1 - 2 * core
        self.step_x = 2 - 4 * bit_x
        self.step_y = 4 - 8 * bit_y

    def across(self, which):
        return self.dp + (self.step_core, self.step_x, self.step_y)[which]

    def device(self, which):
        return (self.across(which), self.z)

    def along(self, k):
        return lax.rem(self.z + k, self.n_vocab)

    def greet(self):
        barrier = pltpu.get_barrier_semaphore()
        for which in (CORE, X, Y):
            pl.semaphore_signal(barrier, inc=1, device_id=self.device(which), device_id_type=MESH)
        for k in range(1, self.n_vocab):
            pl.semaphore_signal(barrier, inc=1, device_id=(self.dp, self.along(k)), device_id_type=MESH)
        pl.semaphore_wait(barrier, 3 + self.n_vocab - 1)


def remote(src, dst, send, recv, device):
    return pltpu.make_async_remote_copy(
        src_ref=src, dst_ref=dst, send_sem=send, recv_sem=recv, device_id=device, device_id_type=MESH
    )


def block_view(ref, stride, offset, rows, first, width):
    def view(index):
        return ref.at[pl.ds(pl.multiple_of(index * stride + offset, 16), rows), pl.ds(first, width)]

    return view


class TileSum:
    def __init__(self, place, tiles, land, ring, send, recv):
        self.place, self.tiles, self.land, self.ring = place, tiles, land, ring
        self.send, self.recv = send, recv

    def z_copies(self):
        place = self.place
        return [
            remote(
                self.tiles.at[0], self.ring.at[place.z], self.send.at[2 + k], self.recv.at[2 + k],
                (place.dp, place.along(k)),
            )
            for k in range(1, place.n_vocab)
        ]

    def copy(self, i):
        return remote(
            self.tiles.at[1 + i], self.land.at[i], self.send.at[i], self.recv.at[i], self.place.device(i)
        )

    def begin(self, value):
        self.tiles[0] = value
        self.ring[self.place.z] = value
        for copy in self.z_copies():
            copy.start()

    def round(self, i):
        if i == 0:
            for copy in self.z_copies():
                copy.wait()
            value = self.ring[0]
            for k in range(1, self.place.n_vocab):
                value = value + self.ring[k]
        else:
            self.copy(i - 1).wait()
            value = self.tiles[i] + self.land[i - 1]
        if i < 3:
            self.tiles[1 + i] = value
            self.copy(i).start()
        return value


class Sender:
    def __init__(self):
        self.started = []

    def go(self, copy):
        copy.start()
        self.started.append(copy)

    def finish(self):
        for copy in self.started:
            copy.wait_send()


def dot_low(left, right):
    return jnp.dot(left, right, preferred_element_type=F32)


def dot_left(left, right):
    return lax.dot_general(left, right, (((0,), (0,)), ((), ())), preferred_element_type=F32)


def dot_right(left, right):
    return lax.dot_general(left, right, (((1,), (1,)), ((), ())), preferred_element_type=F32)


def norm_forward(value, gain, shift):
    mean = jnp.mean(value, axis=-1, keepdims=True)
    centered = value - mean
    inverse = lax.rsqrt(jnp.mean(centered * centered, axis=-1, keepdims=True) + norm_eps)
    normal = centered * inverse
    return normal * gain + shift, normal, inverse


def norm_backward(gradient, normal, inverse, gain):
    gain_gradient = jnp.sum(gradient * normal, axis=0)
    shift_gradient = jnp.sum(gradient, axis=0)
    scaled = gradient * gain
    inner = jnp.mean(scaled, axis=-1, keepdims=True) + normal * jnp.mean(
        scaled * normal, axis=-1, keepdims=True
    )
    return inverse * (scaled - inner), gain_gradient, shift_gradient


def gelu(value):
    return 0.5 * value * (1.0 + lax.erf(value * 0.7071067811865476))


def gelu_slope(value):
    cdf = 0.5 * (1.0 + lax.erf(value * 0.7071067811865476))
    return cdf + value * jnp.exp(-0.5 * value * value) * 0.3989422804014327


def rows_dot(left, right):
    return jnp.dot(left, right, preferred_element_type=F32)


def norm_rows(value):
    mean = jnp.mean(value, axis=-1, keepdims=True)
    centered = value - mean
    inverse = lax.rsqrt(jnp.mean(centered * centered, axis=-1, keepdims=True) + norm_eps)
    return centered * inverse, inverse


def norm_rows_backward(gradient, normal, inverse, gain):
    scaled = gradient * gain
    inner = jnp.mean(scaled, axis=-1, keepdims=True) + normal * jnp.mean(
        scaled * normal, axis=-1, keepdims=True
    )
    return inverse * (scaled - inner)


def column_sum(value):
    return jnp.sum(value, axis=0, keepdims=True)


def gelu_both(value):
    cdf = 0.5 * (1.0 + lax.erf(value * 0.7071067811865476))
    slope = cdf + value * jnp.exp(-0.5 * value * value) * 0.3989422804014327
    return value * cdf, slope


def aligned(start, size, to=128):
    return pl.ds(pl.multiple_of(start, to), size)


class Refs:
    def __init__(self, names, refs):
        for name, ref in zip(names, refs, strict=True):
            setattr(self, name, ref)


def join_pieces():
    spans = ((0, 3 * D), (VEC_AT, NVEC), (OUT_AT, D), (UP_AT, FF), (TRANS_AT, D))
    pieces = []
    for first, width, _ in JOIN_PARTS:
        for low in (first, first + width // 2):
            high = low + width // 2
            for matrix, (start, size) in enumerate(spans):
                a, b = max(low, start), min(high, start + size)
                if a < b:
                    pieces.append((matrix, a - start, a, b - a))
    return pieces


def packed_at(column):
    for first, width, _ in JOIN_PARTS:
        half = width // 2
        if first <= column < first + width:
            side, inside = divmod(column - first, half)
            return side, first // 2 + inside
    raise ValueError


class Gather:
    def __init__(self, place, r):
        self.place, self.r, self.sender = place, r, Sender()
        n_vocab = place.n_vocab
        self.t_rows, self.t_cols = r.table_t.shape
        self.rows = r.packed.shape[0] // 2
        self.d_rows = r.down_low.shape[0]
        piece = self.t_cols // T_PARTS
        rows = self.rows
        self.chunks = []
        self.z_moves = []
        for q in range(T_PARTS):
            first = piece * n_vocab * q
            where = (
                aligned(place.dp * self.t_rows, self.t_rows, 16),
                aligned(first + place.z * piece, piece),
            )
            half = n_vocab * piece // 2
            view = block_view(r.table, self.t_rows, 0, self.t_rows, first, half)
            self.chunks.append((view, True, len(self.z_moves), None))
            view = block_view(r.table, self.t_rows, 0, self.t_rows, first + half, half)
            self.chunks.append((view, False, None, None))
            self.z_moves.append((r.table_t.at[:, pl.ds(piece * q, piece)], r.table.at[where]))
        for part in JOIN_PARTS[:-1]:
            self.add_part(*part)
        half = D // 2
        d_rows = self.d_rows
        dst = r.down.at[aligned((place.dp * n_vocab + place.z) * d_rows, d_rows, 16), pl.ds(half, half)]
        view = block_view(r.down, d_rows * n_vocab, 0, d_rows * n_vocab, half, half)
        self.chunks.append((view, False, len(self.z_moves), None))
        self.z_moves.append((r.down_low.at[:, pl.ds(half, half)], dst))
        self.add_part(*JOIN_PARTS[-1])
        self.late = len(self.chunks)

    def add_part(self, first, width, x_first):
        place, r, rows = self.place, self.r, self.rows
        cols = pl.ds(first // 2, width // 2)
        view = block_view(r.join, rows * place.n_vocab, 0, rows * place.n_vocab, first, width)
        assemble = functools.partial(self.assemble, first, width)
        self.chunks.append((view, x_first, len(self.z_moves), assemble))
        self.z_moves.append((r.packed.at[:, cols], r.stage.at[place.z, :, cols]))

    def place_own(self):
        place, r = self.place, self.r
        for src, dst in self.z_moves[:T_PARTS]:
            dst[...] = src[...]
        r.stage[place.z] = r.packed[...]

    def place_down(self):
        place, r, d_rows = self.place, self.r, self.d_rows
        r.down[aligned((place.dp * place.n_vocab + place.z) * d_rows, d_rows, 16), :] = r.down_low[...]

    def z_copies(self, slot):
        place, r = self.place, self.r
        src, dst = self.z_moves[slot]
        return [
            remote(src, dst, r.z_send.at[slot, k - 1], r.z_recv.at[slot, k - 1], (place.dp, place.along(k)))
            for k in range(1, place.n_vocab)
        ]

    def along_z(self, *slots):
        for slot in slots:
            for copy in self.z_copies(slot):
                self.sender.go(copy)

    def assemble(self, first, width):
        place, r, rows = self.place, self.r, self.rows
        half = width // 2
        at = first // 2
        lefts, rights = [], []
        for k in range(place.n_vocab):
            piece = r.stage[k, :, at : at + half].astype(F32)
            lefts.append(piece[:rows])
            rights.append(piece[rows:])
        where = aligned(place.dp * rows * place.n_vocab, rows * place.n_vocab, 16)
        r.join[where, first : first + half] = jnp.concatenate(lefts, axis=0).astype(BF)
        r.join[where, first + half : first + width] = jnp.concatenate(rights, axis=0).astype(BF)

    def move(self, i, k, arriving):
        place, r = self.place, self.r
        if i == self.late:
            d_rows = self.d_rows
            if k < 3:
                view = block_view(
                    r.down, d_rows * place.n_vocab, place.z * d_rows, d_rows, 0, D // 2
                )
            else:
                view = block_view(r.down, d_rows * place.n_vocab, 0, d_rows * place.n_vocab, 0, D // 2)
            x_first = True
        else:
            view, x_first, _, _ = self.chunks[i]
        one, two = (X, Y) if x_first else (Y, X)
        own, a, b = place.dp, place.across(one), place.across(two)
        ab = a + b - own
        if k < 3:
            block = (a, b, ab)[k] if arriving else (own, own, a)[k]
            which = (one, two, two)[k]
        else:
            block = (own, a, b, ab)[k - 3] + (place.step_core if arriving else 0)
            which = CORE
        return remote(view(block), view(block), r.d_send.at[i, k], r.d_recv.at[i, k], place.device(which))

    def send(self, i, *which):
        for k in which:
            self.sender.go(self.move(i, k, False))

    def arrive(self, i, *which):
        for k in which:
            self.move(i, k, True).wait_recv()

    def late_copies(self, arriving):
        place, r, d_rows = self.place, self.r, self.d_rows
        a, b = place.across(X), place.across(Y)
        copies = []
        for j, block in enumerate((place.dp, a, b, a + b - place.dp)):
            for k in range(1, place.n_vocab):
                z = place.along(place.n_vocab - k) if arriving else place.z
                at = r.down.at[aligned((block * place.n_vocab + z) * d_rows, d_rows, 16), pl.ds(0, D // 2)]
                copies.append(
                    remote(at, at, r.l_send.at[j, k - 1], r.l_recv.at[j, k - 1], (place.dp, place.along(k)))
                )
        return copies

    def late_turn(self, t):
        i = self.late
        if t == 0:
            self.send(i, 0, 1)
        elif t == 1:
            self.arrive(i, 0)
            self.send(i, 2)
            self.arrive(i, 1, 2)
            for copy in self.late_copies(False):
                self.sender.go(copy)
        elif t == 2:
            for copy in self.late_copies(True):
                copy.wait_recv()
            self.send(i, 3, 4, 5, 6)
        else:
            self.arrive(i, 3, 4, 5, 6)

    def turn(self, t):
        n = len(self.chunks)
        if t < n:
            _, _, slot, then = self.chunks[t]
            if slot is not None:
                for copy in self.z_copies(slot):
                    copy.wait_recv()
            if then is not None:
                then()
            self.send(t, 0, 1, 3)
        if 0 <= t - 1 < n:
            self.arrive(t - 1, 0)
            self.send(t - 1, 2, 4)
        if 0 <= t - 2 < n:
            self.arrive(t - 2, 1)
            self.send(t - 2, 5)
            self.arrive(t - 2, 2)
            self.send(t - 2, 6)
        if 0 <= t - 3 < n:
            self.arrive(t - 3, 3, 4, 5, 6)


N_CHUNKS = 2 * T_PARTS + len(JOIN_PARTS) + 2
Z_SLOTS = T_PARTS + len(JOIN_PARTS) + 1


N_FORWARD_IN = 11


def saved_shapes(rows, d_rows, tokens, picked, t_cols_all):
    return dict(
        join=((rows, JOIN), BF),
        down=((d_rows, D), BF),
        normal0=((tokens, D), BF),
        inverse0=((tokens, 1), F32),
        x0_low=((tokens, D), BF),
        keys=((tokens, D), BF),
        values=((tokens, D), BF),
        query=((picked, D), BF),
        x0_rows=((picked, D), BF),
        att=((picked, D), BF),
        normal1=((picked, D), F32),
        inverse1=((picked, 1), F32),
        x1_low=((picked, D), BF),
        hidden=((picked, FF), BF),
        slope=((picked, FF), BF),
        x2_low=((picked, D), BF),
        d_trans=((picked, D), BF),
        d_two=((picked, D), F32),
        d_logits=((picked, t_cols_all), BF),
        latent=((picked, D), BF),
        g_vec=((16, D), F32),
        vec=((16, D), F32),
        col_ids=((tokens, 1), jnp.int32),
        spots=((picked, 1), jnp.int32),
    )


def tile_scratch(n_vocab):
    dma = pltpu.SemaphoreType.DMA
    return dict(
        tiles=pltpu.VMEM((4, 8, 128), F32),
        tile_land=pltpu.VMEM((3, 8, 128), F32),
        tile_ring=pltpu.VMEM((n_vocab, 8, 128), F32),
        tile_send=dma((2 + n_vocab,)),
        tile_recv=dma((2 + n_vocab,)),
    )


def whole_part(value, by):
    return jnp.floor((value + 0.5) * (1.0 / by))


def forward_kernel(n_vocab, names, out_names, *refs):
    r = Refs(names, refs[:N_FORWARD_IN] + refs[N_FORWARD_IN + len(out_names) + 2 :])
    out = Refs(out_names, refs[N_FORWARD_IN : N_FORWARD_IN + len(out_names)])
    counts_out, loss_out = refs[N_FORWARD_IN + len(out_names) : N_FORWARD_IN + len(out_names) + 2]
    seqs, seq_len = r.tokens.shape
    tokens = seqs * seq_len
    picked = r.spots.shape[0]
    slots = picked // seqs
    block = r.table_in.shape[1]
    place = Place(n_vocab)

    def prepare_table():
        full = block // 128 * 128
        r.table_t[:, :full] = r.table_in[:, :full].astype(BF)
        if full < r.table_t.shape[1]:
            r.table_rest[...] = jnp.zeros_like(r.table_rest)
            r.table_rest[:, : block - full] = r.table_in[:, full:]
            r.table_t[:, full:] = r.table_rest[...].astype(BF)

    def prepare_packed():
        r.vec_rest[...] = jnp.zeros_like(r.vec_rest)
        rows = r.packed.shape[0] // 2
        r.vec_rows[...] = jnp.zeros_like(r.vec_rows)
        r.vec_rows[:NVEC, :rows] = r.vectors[...]
        r.vec_rest[:, :16] = r.vec_rows[...].T[:rows, :]
        sources = (r.qkv_w, r.vec_rest, r.out_w, r.up_w, r.trans_w)
        spans = ((0, 3 * D), (VEC_AT, OUT_AT - VEC_AT), (OUT_AT, D), (UP_AT, FF), (TRANS_AT, D))

        def read(low, high):
            found = []
            for source, (start, size) in zip(sources, spans, strict=True):
                a, b = max(low, start), min(high, start + size)
                if a < b:
                    found.append(source[:, a - start : b - start])
            return found[0] if len(found) == 1 else jnp.concatenate(found, axis=1)

        for first, width, _ in JOIN_PARTS:
            half = width // 2
            both = jnp.concatenate([read(first, first + half), read(first + half, first + width)], axis=0)
            r.packed[:, first // 2 : first // 2 + half] = both.astype(BF)

    def prepare_ids():
        piece = r.table_t.shape[1] // T_PARTS
        token = r.tokens[...].astype(F32)
        owner = whole_part(token, block)
        row = token - owner * block
        part = whole_part(row, piece)
        column = part * (piece * n_vocab) + owner * piece + (row - part * piece)
        r.wide_rows[...] = jnp.full(r.wide_rows.shape, float(seq_len), F32)
        r.wide_rows[:seqs, : r.picks.shape[1]] = r.picks[...].astype(F32)
        spots = r.wide_rows[...].T
        lane = lax.broadcasted_iota(jnp.int32, (slots, 128), 1)
        masked_columns = []
        for s in range(seqs):
            rows = slice(s * slots, (s + 1) * slots)
            spot = spots[:slots, s : s + 1]
            position = lax.broadcasted_iota(jnp.int32, (slots, seq_len), 1).astype(F32)
            here = spot == position
            r.targets[rows, :] = jnp.sum(
                jnp.where(here, column[s : s + 1, :], 0.0), axis=-1, keepdims=True
            ).astype(jnp.int32)
            live = spot < float(seq_len)
            r.spots[rows, :] = jnp.where(live, spot, -1.0).astype(jnp.int32)
            kind = r.species[s] == lane
            r.own_kinds[rows, :] = jnp.where(kind & live, 1.0, 0.0)
            masked = jnp.max(jnp.where(here, 1.0, 0.0), axis=0, keepdims=True)
            masked_columns.append(jnp.where(masked > 0.0, -1.0, column[s : s + 1, :]))
        masked_columns.append(jnp.zeros((8 - seqs, seq_len), F32))
        turned = jnp.concatenate(masked_columns, axis=0).T
        for s in range(seqs):
            r.col_ids[s * seq_len : (s + 1) * seq_len, :] = turned[:, s : s + 1].astype(jnp.int32)

    saves = []

    def save(src, dst, *cols):
        if cols:
            src, dst = src.at[:, pl.ds(*cols)], dst.at[:, pl.ds(*cols)]
        copy = pltpu.make_async_copy(src, dst, r.save_sem.at[len(saves)])
        copy.start()
        saves.append(copy)

    def embed(q):
        width = r.table.shape[1] // T_PARTS
        first = q * width

        def step(i, carry):
            at = aligned(i * 256, 256)
            ids = r.col_ids[at, :]
            onehot = (ids == lax.broadcasted_iota(jnp.int32, (256, width), 1) + first).astype(BF)
            part = dot_right(onehot, r.table[:, first : first + width])
            r.embedded[at, :] = part if q == 0 else part + r.embedded[at, :]
            return carry

        lax.fori_loop(0, tokens // 256, step, 0)

    def first_norm():
        columns = r.join[:, VEC_AT : VEC_AT + 128].astype(F32).T
        r.vec[...] = columns[:16]

        def step(i, carry):
            at = aligned(i * 128, 128)
            value = jnp.where(r.col_ids[at, :] < 0, r.vec[13:14, :], r.embedded[at, :])
            normal, inverse = norm_rows(value)
            stream = normal * r.vec[0:1, :] + r.vec[1:2, :]
            high = stream.astype(BF)
            r.normal0[at, :] = normal.astype(BF)
            r.inverse0[at, :] = inverse
            r.x0_low[at, :] = high
            r.x0_rest[at, :] = (stream - high.astype(F32)).astype(BF)
            return carry

        lax.fori_loop(0, tokens // 128, step, 0)

    def project():
        def step(i, carry):
            at = aligned(i * 256, 256)
            low = r.x0_low[at, :]
            r.keys[at, :] = rows_dot(low, r.join[:, D : 2 * D]).astype(BF)
            r.values[at, :] = (rows_dot(low, r.join[:, 2 * D : 3 * D]) + r.vec[9:10, :]).astype(BF)
            return carry

        lax.fori_loop(0, tokens // 256, step, 0)
        for s in range(seqs):
            rows = slice(s * slots, (s + 1) * slots)
            seq = slice(s * seq_len, (s + 1) * seq_len)
            pick = (r.spots[rows, :] == lax.broadcasted_iota(jnp.int32, (slots, seq_len), 1)).astype(BF)
            high = rows_dot(pick, r.x0_low[seq, :])
            r.stream[rows, :] = high + rows_dot(pick, r.x0_rest[seq, :])
            r.x0_rows[rows, :] = high.astype(BF)
        r.query[...] = (rows_dot(r.x0_rows[...], r.join[:, :D]) + r.vec[8:9, :]).astype(BF)

    def attend():
        lane = lax.broadcasted_iota(jnp.int32, (slots, 128), 1)

        def step(j, carry):
            lanes = aligned(j * 128, 128)
            for s in range(seqs):
                rows = slice(s * slots, (s + 1) * slots)
                seq = slice(s * seq_len, (s + 1) * seq_len)
                q2 = r.query[rows, lanes]
                k2 = r.keys[seq, lanes]
                v2 = r.values[seq, lanes]
                parts = []
                for a in range(2):
                    mine = (lane >= HD) if a else (lane < HD)
                    scores = dot_right(jnp.where(mine, q2, jnp.zeros_like(q2)), k2) * HD ** (-0.5)
                    top = jnp.max(scores, axis=-1, keepdims=True)
                    expo = jnp.exp(scores - top)
                    total = jnp.sum(expo, axis=-1, keepdims=True)
                    parts.append(rows_dot((expo * (1.0 / total)).astype(BF), v2))
                r.att[rows, lanes] = jnp.where(lane < HD, parts[0], parts[1]).astype(BF)
            return carry

        lax.fori_loop(0, HEADS // 2, step, 0)

    def after_attention():
        value = r.stream[...] + (rows_dot(r.att[...], r.join[:, OUT_AT : OUT_AT + D]) + r.vec[10:11, :])
        normal, inverse = norm_rows(value)
        r.normal1[...] = normal
        r.inverse1[...] = inverse
        stream = normal * r.vec[2:3, :] + r.vec[3:4, :]
        r.stream[...] = stream
        r.x1_low[...] = stream.astype(BF)

    def feed_up(first):
        def step(j, carry):
            cols = aligned(j * 512, 512)
            act, slope = gelu_both(rows_dot(r.x1_low[...], r.join[:, aligned(UP_AT + j * 512, 512)]))
            r.hidden[:, cols] = act.astype(BF)
            r.slope[:, cols] = slope.astype(BF)
            return carry

        lax.fori_loop(3 * first, 3 * first + 3, step, 0)

    def feed_down():
        value = r.stream[...] + (rows_dot(r.hidden[...], r.down[...]) + r.vec[11:12, :])
        normal, inverse = norm_rows(value)
        r.normal2[...] = normal
        r.inverse2[...] = inverse
        r.x2_low[...] = (normal * r.vec[4:5, :] + r.vec[5:6, :]).astype(BF)

    def head(counts):
        act, slope3 = gelu_both(
            rows_dot(r.x2_low[...], r.join[:, TRANS_AT : TRANS_AT + D]) + r.vec[12:13, :]
        )
        normal3, inverse3 = norm_rows(act)
        r.stream[...] = normal3
        latent = (normal3 * r.vec[6:7, :] + r.vec[7:8, :]).astype(BF)
        r.latent[...] = latent
        width = r.table.shape[1] // (2 * T_PARTS)
        steps = 2 * T_PARTS

        def scores(i, top):
            cols = aligned(i * width, width)
            logits = rows_dot(r.latent[...], r.table[:, cols])
            logits = jnp.where(r.col_floor[:, cols] == 0.0, logits, floor_value)
            r.logits[:, cols] = logits
            return jnp.maximum(top, jnp.max(logits, axis=-1, keepdims=True))

        top = lax.fori_loop(0, steps, scores, jnp.full((picked, 1), floor_value, F32))

        def spread(i, carry):
            total, hit = carry
            cols = aligned(i * width, width)
            logits = r.logits[:, cols]
            column = lax.broadcasted_iota(jnp.int32, (picked, width), 1) + i * width
            hit = hit + jnp.sum(jnp.where(column == r.targets[...], logits, 0.0), axis=-1, keepdims=True)
            expo = jnp.exp(logits - top)
            r.logits[:, cols] = expo
            return total + jnp.sum(expo, axis=-1, keepdims=True), hit

        zero = jnp.zeros((picked, 1), F32)
        total, hit = lax.fori_loop(0, steps, spread, (zero, zero))
        loss_rows = top + jnp.log(total) - hit
        here = counts > 0.0
        present = jnp.sum(here.astype(F32), axis=-1, keepdims=True)
        inverse = jnp.where(here, 1.0 / jnp.maximum(counts, 1.0), 0.0)
        weight = jnp.sum(r.own_kinds[...] * inverse, axis=-1, keepdims=True)
        loss_out[...] = jnp.broadcast_to(column_sum(weight * loss_rows), (8, 128))
        weight = weight / present
        scale = weight / total

        def slopes(i, d_latent):
            cols = aligned(i * width, width)
            column = lax.broadcasted_iota(jnp.int32, (picked, width), 1) + i * width
            d_logits = r.logits[:, cols] * scale - jnp.where(column == r.targets[...], weight, 0.0)
            d_logits = d_logits.astype(BF)
            r.d_logits[:, cols] = d_logits
            return d_latent + dot_right(d_logits, r.table[:, cols])

        d_latent = lax.fori_loop(0, steps, slopes, jnp.zeros((picked, D), F32))
        normal3 = r.stream[...]
        r.g_vec[6:7, :] = column_sum(d_latent * normal3)
        r.g_vec[7:8, :] = column_sum(d_latent)
        d_act = norm_rows_backward(d_latent, normal3, inverse3, r.vec[6:7, :])
        d_trans = (d_act * slope3).astype(BF)
        r.d_trans[...] = d_trans
        r.g_vec[12:13, :] = column_sum(d_trans.astype(F32))
        d_two = dot_right(d_trans, r.join[:, TRANS_AT : TRANS_AT + D])
        normal2 = r.normal2[...]
        r.g_vec[4:5, :] = column_sum(d_two * normal2)
        r.g_vec[5:6, :] = column_sum(d_two)
        r.d_two[...] = norm_rows_backward(d_two, normal2, r.inverse2[...], r.vec[4:5, :])

    gather = Gather(place, r)
    prepare_table()
    place.greet()
    gather.along_z(0)
    r.down_low[...] = r.down_w[...].astype(BF)
    gather.place_down()
    gather.late_turn(0)
    gather.along_z(*range(1, T_PARTS))
    prepare_packed()
    gather.place_own()
    gather.along_z(*range(T_PARTS, Z_SLOTS - 3))
    prepare_ids()
    r.g_vec[...] = jnp.zeros_like(r.g_vec)
    gather.turn(0)
    gather.turn(1)
    counting = TileSum(place, r.tiles, r.tile_land, r.tile_ring, r.tile_send, r.tile_recv)
    counting.begin(jnp.broadcast_to(column_sum(r.own_kinds[...]), (8, 128)))
    gather.turn(2)
    gather.late_turn(1)
    gather.along_z(*range(Z_SLOTS - 3, Z_SLOTS))
    gather.turn(3)
    gather.turn(4)
    embed(0)
    gather.turn(5)
    gather.turn(6)
    embed(1)
    gather.turn(7)
    gather.turn(8)
    embed(2)
    gather.turn(9)
    gather.turn(10)
    first_norm()
    save(r.vec, out.vec)
    save(r.col_ids, out.col_ids)
    save(r.spots, out.spots)
    save(r.normal0, out.normal0)
    save(r.inverse0, out.inverse0)
    save(r.x0_low, out.x0_low)
    save(r.join, out.join, 0, OUT_AT)
    gather.turn(11)
    project()
    save(r.keys, out.keys)
    save(r.values, out.values)
    save(r.query, out.query)
    save(r.x0_rows, out.x0_rows)
    counting.round(0)
    gather.turn(12)
    counting.round(1)
    attend()
    save(r.att, out.att)
    gather.turn(13)
    counting.round(2)
    after_attention()
    save(r.normal1, out.normal1)
    save(r.inverse1, out.inverse1)
    save(r.x1_low, out.x1_low)
    feed_up(0)
    feed_up(1)
    save(r.join, out.join, OUT_AT, TRANS_AT - OUT_AT)
    save(r.hidden, out.hidden)
    save(r.slope, out.slope)
    gather.late_turn(2)
    gather.turn(14)
    gather.late_turn(3)
    feed_down()
    save(r.down, out.down)
    save(r.x2_low, out.x2_low)
    counts = counting.round(3)
    counts_out[...] = counts
    gather.turn(15)
    save(r.join, out.join, TRANS_AT, D)
    head(counts[0:1, :])
    for src, dst in (
        (r.d_trans, out.d_trans), (r.d_two, out.d_two), (r.d_logits, out.d_logits), (r.latent, out.latent),
        (r.g_vec, out.g_vec),
    ):
        save(src, dst)
    gather.sender.finish()
    for copy in saves:
        copy.wait()


def forward(inputs, n_dp, n_vocab):
    rows = inputs["qkv_w"].shape[0]
    columns, block = inputs["table_in"].shape
    wide = padded(block)
    d_rows = inputs["down_w"].shape[0]
    seqs, seq_len = inputs["tokens"].shape
    tokens, picked = seqs * seq_len, seqs * 128
    table_shape = (D, wide * n_vocab)
    shapes = saved_shapes(rows * n_dp * n_vocab, d_rows * n_dp * n_vocab, tokens, picked, wide * n_vocab)
    dma = pltpu.SemaphoreType.DMA
    scratch = {name: pltpu.VMEM(*shape) for name, shape in shapes.items()}
    scratch.update(
        table=pltpu.VMEM(table_shape, BF),
        table_t=pltpu.VMEM((columns, wide), BF),
        table_rest=pltpu.VMEM((columns, 128), F32),
        vec_rows=pltpu.VMEM((16, 128), F32),
        packed=pltpu.VMEM((2 * rows, JOIN // 2), BF),
        vec_rest=pltpu.VMEM((rows, OUT_AT - VEC_AT), F32),
        down_low=pltpu.VMEM((d_rows, D), BF),
        wide_rows=pltpu.VMEM((8, 128), F32),
        targets=pltpu.VMEM((picked, 1), jnp.int32),
        own_kinds=pltpu.VMEM((picked, 128), F32),
        stage=pltpu.VMEM((n_vocab, 2 * rows, JOIN // 2), BF),
        embedded=pltpu.VMEM((tokens, D), F32),
        x0_rest=pltpu.VMEM((tokens, D), BF),
        stream=pltpu.VMEM((picked, D), F32),
        normal2=pltpu.VMEM((picked, D), F32),
        inverse2=pltpu.VMEM((picked, 1), F32),
        logits=pltpu.VMEM((picked, wide * n_vocab), F32),
        z_send=dma((Z_SLOTS, n_vocab - 1)),
        z_recv=dma((Z_SLOTS, n_vocab - 1)),
        l_send=dma((4, n_vocab - 1)),
        l_recv=dma((4, n_vocab - 1)),
        d_send=dma((N_CHUNKS, 7)),
        d_recv=dma((N_CHUNKS, 7)),
        save_sem=dma((len(shapes) + 2,)),
        **tile_scratch(n_vocab),
    )
    vmem = pl.BlockSpec(memory_space=pltpu.VMEM)
    anywhere = pl.BlockSpec(memory_space=pl.ANY)
    tile = jax.ShapeDtypeStruct((8, 128), F32)
    names = tuple(inputs) + tuple(scratch)
    smem = pl.BlockSpec(memory_space=pltpu.SMEM)
    outs = pl.pallas_call(
        functools.partial(forward_kernel, n_vocab, names, tuple(shapes)),
        out_shape=tuple(jax.ShapeDtypeStruct(*shape) for shape in shapes.values()) + (tile, tile),
        in_specs=[smem if name == "species" else vmem for name in inputs],
        out_specs=(anywhere,) * len(shapes) + (vmem, vmem),
        scratch_shapes=list(scratch.values()),
        compiler_params=pltpu.CompilerParams(
            collective_id=0, has_side_effects=True, vmem_limit_bytes=VMEM_LIMIT
        ),
    )(*inputs.values())
    return dict(zip(shapes, outs[:-2], strict=True)), outs[-2], outs[-1]


JOINED, DOWN, TABLE = range(3)
REDUCE_ORDER = (
    (JOINED, 5), (JOINED, 3), (JOINED, 4), (DOWN, 0), (DOWN, 1), (JOINED, 2), (JOINED, 0), (JOINED, 1),
) + tuple((TABLE, j) for j in range(2 * T_PARTS))


class Reduce:
    def __init__(self, place, r, t_cols, from_core, from_two, from_one):
        self.place, self.r, self.sender = place, r, Sender()
        self.from_core, self.from_two, self.from_one = from_core, from_two, from_one
        n_vocab = place.n_vocab
        rows = r.join_out.shape[0] // 2
        d_rows = r.down_out.shape[0]
        t_rows = r.table_out.shape[0]
        piece = t_cols // T_PARTS
        self.rows, self.d_rows, self.t_rows, self.piece = rows, d_rows, t_rows, piece
        self.chunks = []
        for kind, j in REDUCE_ORDER:
            if kind == JOINED:
                first, width, x_first = JOIN_PARTS[j]
                view = block_view(r.join, rows * n_vocab, 0, rows * n_vocab, first, width)
            elif kind == DOWN:
                half = D // 2
                view = block_view(r.down, d_rows * n_vocab, 0, d_rows * n_vocab, half * j, half)
                x_first = j == 0
            else:
                half = n_vocab * piece // 2
                view = block_view(r.table, t_rows, 0, t_rows, half * j, half)
                x_first = j % 2 == 0
            narrow = view
            if (kind, j) == (DOWN, 0):
                narrow = block_view(r.down, d_rows * n_vocab, place.z * d_rows, d_rows, 0, D // 2)
            self.chunks.append(((kind, j), view, narrow, x_first))
        self.jobs = {}

    def blocks(self, i):
        place = self.place
        one, two = (X, Y) if self.chunks[i][3] else (Y, X)
        own, a, b = place.dp, place.across(one), place.across(two)
        return one, two, (own, a, b, a + b - own)

    def add_into(self, target, *sources):
        def step(i, carry):
            at = aligned(i * 16, 16, 16)
            if len(sources) == 1:
                target[at, :] = target[at, :] + sources[0][at, :]
            else:
                total = target[at, :].astype(F32)
                for source in sources:
                    total = total + source[at, :].astype(F32)
                target[at, :] = total.astype(BF)
            return carry

        lax.fori_loop(0, target.shape[0] // 16, step, 0)

    def to_core(self, i, k):
        _, _, blocks = self.blocks(i)
        block = blocks[k] + self.place.step_core
        r, place = self.r, self.place
        return remote(
            self.chunks[i][1](block), self.from_core[i].at[k], r.d_send.at[i, k], r.d_recv.at[i, k],
            place.device(CORE),
        )

    def to_two(self, i, k):
        _, two, blocks = self.blocks(i)
        r, place = self.r, self.place
        return remote(
            self.chunks[i][2](blocks[2 + k]), self.from_two[i].at[k], r.d_send.at[i, 4 + k],
            r.d_recv.at[i, 4 + k], place.device(two),
        )

    def to_one(self, i):
        one, _, blocks = self.blocks(i)
        r, place = self.r, self.place
        return remote(
            self.chunks[i][2](blocks[1]), self.from_one[i], r.d_send.at[i, 6], r.d_recv.at[i, 6],
            place.device(one),
        )

    def late_copies(self, i):
        place, r, d_rows = self.place, self.r, self.d_rows
        _, _, blocks = self.blocks(i)
        copies = []
        for j, block in enumerate(blocks):
            for k in range(1, place.n_vocab):
                row = (block * place.n_vocab + place.along(k)) * d_rows
                copies.append(
                    remote(
                        r.down.at[aligned(row, d_rows, 16), pl.ds(0, D // 2)], r.z_late.at[j, k - 1],
                        r.l_send.at[j, k - 1], r.l_recv.at[j, k - 1], (place.dp, place.along(k)),
                    )
                )
        return copies

    def z_copies(self, slot, src_of, dst_of):
        place, r = self.place, self.r
        return [
            remote(
                src_of(place.along(k)), dst_of(k - 1), r.z_send.at[slot, k - 1], r.z_recv.at[slot, k - 1],
                (place.dp, place.along(k)),
            )
            for k in range(1, place.n_vocab)
        ]

    def pack(self, first, width):
        r, rows, n_vocab = self.r, self.rows, self.place.n_vocab
        half = width // 2
        at = first // 2
        where = aligned(self.place.dp * rows * n_vocab, rows * n_vocab, 16)
        block = r.join[where, first : first + width].astype(F32)
        for k in range(n_vocab):
            piece = block[k * rows : (k + 1) * rows]
            r.packed[k, :, at : at + half] = jnp.concatenate([piece[:, :half], piece[:, half:]], axis=0).astype(BF)

    def along_z(self, i):
        place, r = self.place, self.r
        kind, j = self.chunks[i][0]
        slot = len(self.jobs)
        if kind == JOINED:
            first, width, _ = JOIN_PARTS[j]
            self.pack(first, width)
            cols = pl.ds(first // 2, width // 2)
            copies = self.z_copies(slot, lambda to: r.packed.at[to, :, cols], lambda k: r.z_join.at[k, :, cols])
        elif kind == DOWN:
            cols = pl.ds(D // 2, D // 2)
            d_rows, n_vocab = self.d_rows, place.n_vocab
            copies = self.z_copies(
                slot,
                lambda to: r.down.at[aligned((place.dp * n_vocab + to) * d_rows, d_rows, 16), cols],
                lambda k: r.z_down.at[k],
            )
        else:
            piece, q = self.piece, j // 2
            copies = self.z_copies(
                slot,
                lambda to: r.table.at[
                    aligned(place.dp * self.t_rows, self.t_rows, 16),
                    aligned(q * piece * place.n_vocab + to * piece, piece),
                ],
                lambda k: r.z_table.at[k, :, pl.ds(q * piece, piece)],
            )
        for copy in copies:
            self.sender.go(copy)
        self.jobs[i] = copies

    def is_late(self, i):
        return self.chunks[i][0] == (DOWN, 0)

    def step(self, stage, *which):
        for i in which:
            (self.start, self.after_core, self.after_two, self.after_one, self.after_late)[stage](i)

    def start(self, i):
        for k in range(4):
            self.sender.go(self.to_core(i, k))

    def after_core(self, i):
        view = self.chunks[i][1]
        _, _, blocks = self.blocks(i)
        for k in (2, 3, 0, 1):
            self.to_core(i, k).wait_recv()
            self.add_into(view(blocks[k]), self.from_core[i].at[k])
            if k == 3 and not self.is_late(i):
                self.send_two(i)
        if self.is_late(i):
            for copy in self.late_copies(i):
                self.sender.go(copy)

    def after_late(self, i):
        narrow = self.chunks[i][2]
        _, _, blocks = self.blocks(i)
        for copy in self.late_copies(i):
            copy.wait_recv()
        for j in (2, 3, 0, 1):
            parts = [self.r.z_late.at[j, k] for k in range(self.place.n_vocab - 1)]
            self.add_into(narrow(blocks[j]), *parts)
            if j == 3:
                self.send_two(i)

    def send_two(self, i):
        for k in range(2):
            self.sender.go(self.to_two(i, k))

    def after_two(self, i):
        narrow = self.chunks[i][2]
        _, _, blocks = self.blocks(i)
        self.to_two(i, 1).wait_recv()
        self.add_into(narrow(blocks[1]), self.from_two[i].at[1])
        self.sender.go(self.to_one(i))
        self.to_two(i, 0).wait_recv()
        self.add_into(narrow(blocks[0]), self.from_two[i].at[0])

    def after_one(self, i):
        kind, j = self.chunks[i][0]
        self.to_one(i).wait_recv()
        self.add_into(self.chunks[i][2](self.place.dp), self.from_one[i])
        if not (self.is_late(i) or kind == TABLE and j % 2 == 0):
            self.along_z(i)

    def collect(self):
        place, r = self.place, self.r
        n_vocab = place.n_vocab

        def total(own, parts, out, cols):
            whole = own.astype(F32)
            for part in parts:
                whole = whole + part.astype(F32)
            out[:, cols] = whole
            return jnp.sum(column_sum(whole * whole), axis=-1, keepdims=True)

        square = jnp.zeros((1, 1), F32)
        half = D // 2
        rows = aligned((place.dp * n_vocab + place.z) * self.d_rows, self.d_rows, 16)
        square += total(r.down[rows, :half], (), r.down_out, slice(0, half))
        for i, ((kind, j), _, _, _) in enumerate(self.chunks):
            if self.is_late(i) or kind == TABLE and j % 2 == 0:
                continue
            for copy in self.jobs[i]:
                copy.wait_recv()
            if kind == JOINED:
                first, width, _ = JOIN_PARTS[j]
                cols = slice(first // 2, first // 2 + width // 2)
                own = r.packed[place.z, :, cols]
                parts = [r.z_join[k, :, cols] for k in range(n_vocab - 1)]
                square += total(own, parts, r.join_out, cols)
            elif kind == DOWN:
                parts = [r.z_down[k] for k in range(n_vocab - 1)]
                square += total(r.down[rows, half:], parts, r.down_out, slice(half, D))
            else:
                q = j // 2
                cols = slice(q * self.piece, (q + 1) * self.piece)
                t_rows = aligned(place.dp * self.t_rows, self.t_rows, 16)
                own = r.table[t_rows, aligned(q * self.piece * n_vocab + place.z * self.piece, self.piece)]
                parts = [r.z_table[k, :, cols] for k in range(n_vocab - 1)]
                square += total(own, parts, r.table_out, cols)
        return square


def backward_kernel(n_vocab, in_names, names, *refs):
    given = Refs(in_names, refs[: len(in_names)])
    scratch = refs[len(in_names) :]
    n_chunks = len(REDUCE_ORDER)
    lands, scratch = scratch[-3 * n_chunks :], scratch[: -3 * n_chunks]
    r = Refs(names, scratch)
    tokens = given.col_ids.shape[0]
    picked = given.spots.shape[0]
    seqs = 2
    seq_len, slots = tokens // seqs, picked // seqs
    wide = r.table.shape[1]

    def keys_at(s):
        return r.table.at[pl.ds(0, seq_len), pl.ds(s * D, D)]

    def values_at(s):
        return r.table.at[pl.ds(0, seq_len), pl.ds((2 + s) * D, D)]

    hidden = r.table.at[pl.ds(seq_len, picked), pl.ds(0, FF)]
    query = r.table.at[pl.ds(seq_len, picked), pl.ds(FF, D)]
    x0_rows = r.table.at[pl.ds(seq_len, picked), pl.ds(FF + D, D)]
    half = FF // 2
    slopes = [r.table.at[pl.ds(s * picked, picked), pl.ds(4 * D, half)] for s in range(2)]
    count = [0]

    def load(*pairs):
        copies = []
        for src, dst in pairs:
            copies.append(pltpu.make_async_copy(src, dst, r.load_sem.at[count[0]]))
            copies[-1].start()
            count[0] += 1
        return copies

    def seq_pairs(src, dst):
        return [(src.at[pl.ds(s * seq_len, seq_len), :], dst(s)) for s in range(seqs)]

    def need(*groups):
        for copies in groups:
            for copy in copies:
                copy.wait()

    up_cols, low_cols = pl.ds(UP_AT, FF), pl.ds(0, UP_AT)
    got_trans = load((given.x2_low, r.x2_low), (given.d_trans, r.d_trans))
    got_feed = load(
        (given.d_two, r.stream), (given.x1_low, r.x1_low),
        *[(given.slope.at[:, pl.ds(s * half, half)], slopes[s]) for s in range(2)],
        (given.join.at[:, up_cols], r.join.at[:, up_cols]), (given.down, r.down),
    )
    got_hidden = load((given.hidden, hidden))
    got_out = load(
        (given.normal1, r.normal1), (given.att, r.att), (given.join.at[:, low_cols], r.join.at[:, low_cols])
    )
    got_att = load(
        *seq_pairs(given.values, values_at), *seq_pairs(given.keys, keys_at), (given.query, query)
    )
    got_first = load((given.x0_rows, x0_rows), (given.x0_low, r.x0_low), (given.normal0, r.normal0))
    got_head = load((given.latent, r.latent), (given.d_logits, r.d_logits))

    place = Place(n_vocab)
    place.greet()
    reduce = Reduce(
        place, r, wide // n_vocab, lands[:n_chunks], lands[n_chunks : 2 * n_chunks], lands[2 * n_chunks :]
    )
    r.g_vec[...] = given.g_vec[...]

    def gain(i):
        return given.vec[i : i + 1, :]

    def put(first, width, value):
        r.join[:, first : first + width] = value.astype(BF)

    need(got_trans)
    put(TRANS_AT, D, dot_left(r.x2_low[...], r.d_trans[...]))
    reduce.step(0, 0)

    need(got_feed)
    d_ffn = r.stream[...].astype(BF)
    r.d_rows_low[...] = d_ffn
    r.g_vec[11:12, :] = column_sum(d_ffn.astype(F32))

    def feed(part):
        def step(j, carry):
            cols = aligned(j * D, D)
            up_at = aligned(UP_AT + part * half + j * D, D)
            d_act = dot_right(r.d_rows_low[...], r.down[aligned(part * half + j * D, D), :])
            d_hidden = (d_act * slopes[part][:, cols].astype(F32)).astype(BF)
            r.stream[...] += dot_right(d_hidden, r.join[:, up_at])
            r.join[:, up_at] = dot_left(r.x1_low[...], d_hidden).astype(BF)
            return carry

        lax.fori_loop(0, half // D, step, 0)

    feed(0)
    reduce.step(0, 1)
    reduce.step(1, 0)
    feed(1)
    reduce.step(0, 2)
    reduce.step(1, 1)
    need(got_hidden)

    def feed_down(part):
        def step(j, carry):
            rows = aligned(j * D, D)
            cols = slice(part * (D // 2), (part + 1) * (D // 2))
            r.down[rows, cols] = dot_left(hidden[:, rows], r.d_rows_low[:, cols]).astype(BF)
            return carry

        lax.fori_loop(0, FF // D, step, 0)

    feed_down(0)
    reduce.step(0, 3)
    reduce.step(1, 2)
    feed_down(1)
    reduce.step(0, 4)
    reduce.step(1, 3)
    reduce.step(2, 0)

    need(got_out)
    d_one = r.stream[...]
    normal1 = r.normal1[...]
    r.g_vec[2:3, :] = column_sum(d_one * normal1)
    r.g_vec[3:4, :] = column_sum(d_one)
    d_one = norm_rows_backward(d_one, normal1, given.inverse1[...], gain(2))
    r.stream[...] = d_one
    d_proj = d_one.astype(BF)
    r.g_vec[10:11, :] = column_sum(d_proj.astype(F32))
    r.x2_low[...] = dot_right(d_proj, r.join[:, OUT_AT : OUT_AT + D]).astype(BF)
    put(OUT_AT, D, dot_left(r.att[...], d_proj))
    reduce.step(0, 5)
    reduce.step(1, 4)

    need(got_att)
    lane = lax.broadcasted_iota(jnp.int32, (slots, 128), 1)

    def attend(j, carry):
        lanes = aligned(j * 128, 128)
        for s in range(seqs):
            rows = slice(s * slots, (s + 1) * slots)
            q2 = query[rows, lanes]
            g2 = r.x2_low[rows, lanes]
            k2 = keys_at(s)[:, lanes]
            v2 = values_at(s)[:, lanes]
            d_q, d_k, d_v = [], None, None
            for a in range(2):
                mine = (lane >= HD) if a else (lane < HD)
                q1 = jnp.where(mine, q2, jnp.zeros_like(q2))
                g1 = jnp.where(mine, g2, jnp.zeros_like(g2))
                scores = dot_right(q1, k2) * HD ** (-0.5)
                expo = jnp.exp(scores - jnp.max(scores, axis=-1, keepdims=True))
                probs = expo * (1.0 / jnp.sum(expo, axis=-1, keepdims=True))
                d_probs = dot_right(g1, v2)
                delta = jnp.sum(d_probs * probs, axis=-1, keepdims=True)
                d_scores = (probs * (d_probs - delta)).astype(BF)
                d_q.append(rows_dot(d_scores, k2))
                more_k = dot_left(d_scores, q1)
                more_v = dot_left(probs.astype(BF), g1)
                d_k = more_k if d_k is None else d_k + more_k
                d_v = more_v if d_v is None else d_v + more_v
            r.d_trans[rows, lanes] = (jnp.where(lane < HD, d_q[0], d_q[1]) * HD ** (-0.5)).astype(BF)
            keys_at(s)[:, lanes] = (d_k * HD ** (-0.5)).astype(BF)
            values_at(s)[:, lanes] = d_v.astype(BF)
        return carry

    lax.fori_loop(0, 2, attend, 0)
    reduce.step(1, 5)
    lax.fori_loop(2, 4, attend, 0)
    reduce.step(2, 2)
    reduce.step(2, 1)
    lax.fori_loop(4, 6, attend, 0)
    reduce.step(3, 0)

    need(got_first)
    d_query = r.d_trans[...]
    r.g_vec[8:9, :] = column_sum(d_query.astype(F32))
    d_rows = r.stream[...] + dot_right(d_query, r.join[:, :D])
    high = d_rows.astype(BF)
    r.d_rows_low[...] = high
    r.x1_low[...] = (d_rows - high.astype(F32)).astype(BF)
    put(0, D, dot_left(x0_rows[...], d_query))
    for i in (0, 1, 9, 13):
        r.g_vec[i : i + 1, :] = jnp.zeros((1, D), F32)
    reduce.step(2, 5)

    for s in range(seqs):

        def step(i, carry, s=s):
            inside = aligned(i * 256, 256)
            at = aligned(s * seq_len + i * 256, 256)
            d_v = values_at(s)[inside, :]
            r.g_vec[9:10, :] += column_sum(d_v.astype(F32))
            d_zero = dot_right(keys_at(s)[inside, :], r.join[:, D : 2 * D])
            d_zero = d_zero + dot_right(d_v, r.join[:, 2 * D : 3 * D])
            column = lax.broadcasted_iota(jnp.int32, (slots, 256), 1) + i * 256
            rows = slice(s * slots, (s + 1) * slots)
            pick = (given.spots[rows, :] == column).astype(BF)
            d_zero = d_zero + (dot_left(pick, r.d_rows_low[rows, :]) + dot_left(pick, r.x1_low[rows, :]))
            normal = r.normal0[at, :].astype(F32)
            r.g_vec[0:1, :] += column_sum(d_zero * normal)
            r.g_vec[1:2, :] += column_sum(d_zero)
            d_emb = norm_rows_backward(d_zero, normal, given.inverse0[at, :], gain(0)).astype(BF)
            r.g_vec[13:14, :] += column_sum(jnp.where(given.col_ids[at, :] < 0, d_emb.astype(F32), 0.0))
            r.normal0[at, :] = d_emb
            return carry

        lax.fori_loop(0, seq_len // 256, step, 0)
        if s == 0:
            reduce.step(3, 2)
            reduce.step(2, 4)
        else:
            reduce.step(3, 1)

    def weigh(i, carry):
        cols = aligned(i * 256, 256)
        for part, source in ((1, keys_at), (2, values_at)):
            value = sum(
                dot_left(r.x0_low[s * seq_len : (s + 1) * seq_len, :], source(s)[:, cols]) for s in range(seqs)
            )
            r.join[:, aligned(part * D + i * 256, 256)] = value.astype(BF)
        return carry

    lax.fori_loop(0, D // 256, weigh, 0)
    columns = jnp.concatenate([r.g_vec[...], jnp.zeros((112, D), F32)], axis=0).T
    put(VEC_AT, 128, columns)
    put(VEC_AT + 128, 128, jnp.zeros((D, 128), F32))
    reduce.step(0, 6, 7)
    reduce.step(4, 3)
    reduce.step(3, 5)

    need(got_head)
    r.flipped[:, :tokens] = r.normal0[...].T
    r.flipped[:, tokens:] = r.latent[...].T
    reduce.step(1, 6, 7)
    reduce.step(3, 4)
    width = wide // (2 * T_PARTS)
    for j in range(2 * T_PARTS):
        cols = slice(j * width, (j + 1) * width)
        column = lax.broadcasted_iota(jnp.int32, (tokens, width), 1) + j * width
        onehot = (given.col_ids[...] == column).astype(BF)
        value = rows_dot(r.flipped[:, :tokens], onehot) + rows_dot(r.flipped[:, tokens:], r.d_logits[:, cols])
        r.table[:, cols] = value.astype(BF)
        reduce.step(0, 8 + j)
        if j >= 1:
            reduce.step(1, 7 + j)
    reduce.step(2, 3, 6)
    reduce.step(1, 13)
    reduce.step(2, 7)
    reduce.step(3, 3)
    reduce.step(2, 8)
    reduce.step(3, 6)
    reduce.step(2, 9)
    reduce.step(3, 7)
    for j in range(10, 14):
        reduce.step(2, j)
        reduce.step(3, j - 2)
    reduce.step(3, 12, 13)
    square = reduce.collect()
    row = lax.broadcasted_iota(jnp.int32, (8, 128), 0)
    summing = TileSum(place, r.tiles, r.tile_land, r.tile_ring, r.tile_send, r.tile_recv)
    summing.begin(jnp.where(row == 0, square, given.loss[...]))
    for i in range(3):
        summing.round(i)
    r.tile_out[...] = summing.round(3)
    reduce.sender.finish()


def backward(saved, loss, n_dp, n_vocab):
    rows = saved["join"].shape[0] // (n_dp * n_vocab)
    d_rows = saved["down"].shape[0] // (n_dp * n_vocab)
    t_rows = D // n_dp
    t_cols = saved["d_logits"].shape[1] // n_vocab
    tokens, picked = saved["col_ids"].shape[0], saved["spots"].shape[0]
    core_shapes, far_shapes = [], []
    for kind, j in REDUCE_ORDER:
        if kind == JOINED:
            shape = (rows * n_vocab, JOIN_PARTS[j][1])
        elif kind == DOWN:
            shape = (d_rows * n_vocab, D // 2)
        else:
            shape = (t_rows, t_cols * n_vocab // (2 * T_PARTS))
        core_shapes.append((4,) + shape)
        far_shapes.append((d_rows, D // 2) if (kind, j) == (DOWN, 0) else shape)
    inputs = dict(saved, loss=loss)
    inputs.pop("x0_rest", None)
    outs = dict(
        join_out=(2 * rows, JOIN // 2), down_out=(d_rows, D), table_out=(t_rows, t_cols), tile_out=(8, 128)
    )
    dma = pltpu.SemaphoreType.DMA
    rows_low = pltpu.VMEM((picked, D), BF)
    tokens_low = pltpu.VMEM((tokens, D), BF)
    scratch = dict(
        join=pltpu.VMEM(saved["join"].shape, BF),
        down=pltpu.VMEM(saved["down"].shape, BF),
        table=pltpu.VMEM((D, t_cols * n_vocab), BF),
        normal0=tokens_low,
        x0_low=tokens_low,
        att=rows_low,
        x1_low=rows_low,
        x2_low=rows_low,
        d_trans=rows_low,
        latent=rows_low,
        d_rows_low=rows_low,
        normal1=pltpu.VMEM((picked, D), F32),
        stream=pltpu.VMEM((picked, D), F32),
        d_logits=pltpu.VMEM(saved["d_logits"].shape, BF),
        g_vec=pltpu.VMEM((16, D), F32),
        flipped=pltpu.VMEM((D, tokens + picked), BF),
        packed=pltpu.VMEM((n_vocab, 2 * rows, JOIN // 2), BF),
        z_join=pltpu.VMEM((n_vocab - 1, 2 * rows, JOIN // 2), BF),
        z_down=pltpu.VMEM((n_vocab - 1, d_rows, D // 2), BF),
        z_late=pltpu.VMEM((4, n_vocab - 1, d_rows, D // 2), BF),
        z_table=pltpu.VMEM((n_vocab - 1, t_rows, t_cols), BF),
        load_sem=dma((len(saved) + 4,)),
        z_send=dma((Z_SLOTS, n_vocab - 1)),
        z_recv=dma((Z_SLOTS, n_vocab - 1)),
        l_send=dma((4, n_vocab - 1)),
        l_recv=dma((4, n_vocab - 1)),
        d_send=dma((N_CHUNKS, 7)),
        d_recv=dma((N_CHUNKS, 7)),
        **tile_scratch(n_vocab),
    )
    lands = [pltpu.VMEM(shape, BF) for shape in core_shapes]
    lands += [pltpu.VMEM((2,) + shape, BF) for shape in far_shapes]
    lands += [pltpu.VMEM(shape, BF) for shape in far_shapes]
    vmem = pl.BlockSpec(memory_space=pltpu.VMEM)
    anywhere = pl.BlockSpec(memory_space=pl.ANY)
    near = set(dict(vec=0, g_vec=0, inverse0=0, inverse1=0, col_ids=0, spots=0, loss=0))
    return pl.pallas_call(
        functools.partial(backward_kernel, n_vocab, tuple(inputs), tuple(outs) + tuple(scratch)),
        out_shape=tuple(jax.ShapeDtypeStruct(shape, F32) for shape in outs.values()),
        in_specs=[vmem if name in near else anywhere for name in inputs],
        out_specs=(vmem,) * len(outs),
        scratch_shapes=list(scratch.values()) + lands,
        compiler_params=pltpu.CompilerParams(
            collective_id=1, has_side_effects=True, vmem_limit_bytes=VMEM_LIMIT
        ),
    )(*inputs.values())


def update_kernel(n_state, *refs):
    tile, counts, g_join, g_down, g_table = refs[:5]
    states = refs[5 : 5 + 3 * n_state]
    outs = refs[5 + 3 * n_state : 5 + 7 * n_state]
    loss_out, present_out, norm_out = refs[5 + 7 * n_state :]
    norm = jnp.sqrt(tile[0:1, 0:1])
    factor = jnp.minimum(1.0, clip_limit / (norm + 1e-06))
    norm_out[0] = jnp.max(norm)
    loss_out[0] = jnp.max(tile[1:2, 0:1])
    present_out[0] = jnp.sum((counts[0:1, :] > 0.0).astype(F32))

    def advance(index, cols, gradient, rate):
        weight, first, second = (ref[:, cols] for ref in states[3 * index : 3 * index + 3])
        first, second, new = adamw(weight, first, second, gradient * factor, rate)
        targets = outs[4 * index : 4 * index + 4]
        targets[0][:, cols] = first
        targets[1][:, cols] = second
        targets[2][:, cols] = new
        targets[3][:, cols] = new.astype(targets[3].dtype)

    every = slice(None)
    block = states[0].shape[1]
    full = block // 128 * 128
    advance(0, slice(0, full), g_table[:, :full], matrix_rate)
    if full < block:
        advance(0, slice(full, block), g_table[:, full:block], matrix_rate)
    rows = g_join.shape[0] // 2
    for matrix, first, column, width in join_pieces():
        side, at = packed_at(column)
        if matrix == 1:
            square = jnp.concatenate([g_join[side * rows : (side + 1) * rows, at : at + 128], jnp.zeros((128 - rows, 128), F32)], axis=0)
            advance(2, every, square.T[:width, :rows], vector_rate)
        else:
            gradient = g_join[side * rows : (side + 1) * rows, at : at + width]
            advance(1 + matrix, slice(first, first + width), gradient, matrix_rate)
    advance(6, every, g_down[...], matrix_rate)


def update(tile, counts, g_join, g_down, g_table, states):
    vmem = pl.BlockSpec(memory_space=pltpu.VMEM)
    smem = pl.BlockSpec(memory_space=pltpu.SMEM)
    shapes = []
    for index, (weight, _, _) in enumerate(states):
        shapes += [jax.ShapeDtypeStruct(weight.shape, F32)] * 3
        shapes.append(jax.ShapeDtypeStruct(weight.shape, F32 if index == 2 else BF))
    flat = [array for state in states for array in state]
    scalars = [jax.ShapeDtypeStruct((1,), F32)] * 3
    return pl.pallas_call(
        functools.partial(update_kernel, len(states)),
        out_shape=tuple(shapes + scalars),
        in_specs=[vmem] * (5 + len(flat)),
        out_specs=(vmem,) * len(shapes) + (smem,) * 3,
        compiler_params=pltpu.CompilerParams(vmem_limit_bytes=VMEM_LIMIT),
    )(tile, counts, g_join, g_down, g_table, *flat)


def species_counts(picks, species, seq_len):
    live = (picks < seq_len).astype(F32)
    kinds = jnp.arange(NSPEC, dtype=jnp.int32)
    return jnp.sum((species[:, None] == kinds[None, :]).astype(F32) * jnp.sum(live, axis=1)[:, None], axis=0)


def local_step(tokens, picks, species, counts, join, down, table_t, col_id):
    seqs, seq_len = tokens.shape
    slots = picks.shape[1]
    w_qkv = join[:, : 3 * D]
    vec = join[:, VEC_AT : VEC_AT + NVEC].astype(F32)
    w_out = join[:, OUT_AT : OUT_AT + D]
    w_up = join[:, UP_AT : UP_AT + FF]
    w_trans = join[:, TRANS_AT : TRANS_AT + D]

    masked = jnp.any(picks[:, :, None] == jnp.arange(seq_len, dtype=jnp.int32)[None, None, :], axis=1)
    masked_flat = masked.reshape(-1)
    live = (picks < seq_len).reshape(-1)
    spot = jnp.minimum(picks, seq_len - 1)
    row_index = (spot + jnp.arange(seqs, dtype=jnp.int32)[:, None] * seq_len).reshape(-1)
    target = jnp.take_along_axis(tokens, spot, axis=1).reshape(-1)
    row_species = jnp.broadcast_to(species[:, None], picks.shape).reshape(-1)

    inputs = jnp.where(masked, -2, tokens).reshape(-1)
    onehot = (inputs[:, None] == col_id[None, :]).astype(BF)
    embedded = jnp.where(masked_flat[:, None], vec[:, 13], dot_right(onehot, table_t))
    stream_zero, normal0, inverse0 = norm_forward(embedded, vec[:, 0], vec[:, 1])
    x0_low = stream_zero.astype(BF)
    keys = dot_low(x0_low, w_qkv[:, D : 2 * D]).astype(BF)
    values = (dot_low(x0_low, w_qkv[:, 2 * D :]) + vec[:, 9]).astype(BF)
    x0_rows = stream_zero[row_index]
    x0_rows_low = x0_rows.astype(BF)
    query = (dot_low(x0_rows_low, w_qkv[:, :D]) + vec[:, 8]).astype(BF)
    q4 = query.reshape(seqs, slots, HEADS, HD)
    k4 = keys.reshape(seqs, seq_len, HEADS, HD)
    v4 = values.reshape(seqs, seq_len, HEADS, HD)
    scores = jnp.einsum("sqhd,skhd->shqk", q4, k4, preferred_element_type=F32) * HD ** (-0.5)
    probs = jax.nn.softmax(scores, axis=-1)
    probs_low = probs.astype(BF)
    att = jnp.einsum("shqk,skhd->sqhd", probs_low, v4, preferred_element_type=F32)
    att_low = att.reshape(-1, D).astype(BF)
    stream_one, normal1, inverse1 = norm_forward(
        x0_rows + dot_low(att_low, w_out) + vec[:, 10], vec[:, 2], vec[:, 3]
    )
    x1_low = stream_one.astype(BF)
    hidden = dot_low(x1_low, w_up)
    hidden_low = gelu(hidden).astype(BF)
    stream_two, normal2, inverse2 = norm_forward(
        stream_one + dot_low(hidden_low, down) + vec[:, 11], vec[:, 4], vec[:, 5]
    )
    picked_low = stream_two.astype(BF)
    trans = dot_low(picked_low, w_trans) + vec[:, 12]
    latent, normal3, inverse3 = norm_forward(gelu(trans), vec[:, 6], vec[:, 7])
    latent_low = latent.astype(BF)
    logits = dot_low(latent_low, table_t)
    logits = jnp.where(((col_id >= 0) & (col_id < VREAL))[None, :], logits, floor_value)
    top = jnp.max(logits, axis=-1, keepdims=True)
    expo = jnp.exp(logits - top)
    total = jnp.sum(expo, axis=-1, keepdims=True)
    is_target = col_id[None, :] == target[:, None]
    hit = jnp.sum(jnp.where(is_target, logits, 0.0), axis=-1)
    loss_rows = (top + jnp.log(total))[:, 0] - hit
    kinds = jnp.arange(NSPEC, dtype=jnp.int32)
    own = ((row_species[:, None] == kinds[None, :]) & live[:, None]).astype(F32)
    species_loss = jnp.sum(own * loss_rows[:, None], axis=0)
    present_mask = counts > 0
    present = jnp.sum(present_mask.astype(F32))
    inverse = jnp.where(present_mask, 1.0 / jnp.maximum(counts, 1.0), 0.0) / present
    weight = jnp.sum(own * inverse[None, :], axis=-1)
    loss_part = jnp.sum(jnp.where(present_mask, species_loss / jnp.maximum(counts, 1.0), 0.0))
    d_logits = (weight[:, None] * (expo / total - is_target.astype(F32))).astype(BF)

    d_latent = dot_right(d_logits, table_t)
    d_act, d6, d7 = norm_backward(d_latent, normal3, inverse3, vec[:, 6])
    d_trans = (d_act * gelu_slope(trans)).astype(BF)
    g_trans = dot_left(picked_low, d_trans)
    d12 = jnp.sum(d_trans.astype(F32), axis=0)
    d_two, d4, d5 = norm_backward(dot_right(d_trans, w_trans), normal2, inverse2, vec[:, 4])
    d_ffn = d_two.astype(BF)
    d11 = jnp.sum(d_ffn.astype(F32), axis=0)
    g_down = dot_left(hidden_low, d_ffn)
    d_hidden = (dot_right(d_ffn, down) * gelu_slope(hidden)).astype(BF)
    g_up = dot_left(x1_low, d_hidden)
    d_one, d2, d3 = norm_backward(d_two + dot_right(d_hidden, w_up), normal1, inverse1, vec[:, 2])
    d_proj = d_one.astype(BF)
    d10 = jnp.sum(d_proj.astype(F32), axis=0)
    g_out = dot_left(att_low, d_proj)
    d_att = dot_right(d_proj, w_out).astype(BF).reshape(seqs, slots, HEADS, HD)
    d_probs = jnp.einsum("sqhd,skhd->shqk", d_att, v4, preferred_element_type=F32)
    delta = jnp.sum(d_probs * probs, axis=-1, keepdims=True)
    d_scores = (probs * (d_probs - delta)).astype(BF)
    d_q = jnp.einsum("shqk,skhd->sqhd", d_scores, k4, preferred_element_type=F32) * HD ** (-0.5)
    d_k = jnp.einsum("shqk,sqhd->skhd", d_scores, q4, preferred_element_type=F32) * HD ** (-0.5)
    d_v = jnp.einsum("shqk,sqhd->skhd", probs_low, d_att, preferred_element_type=F32)
    d_q = d_q.reshape(-1, D).astype(BF)
    d_k = d_k.reshape(-1, D).astype(BF)
    d_v = d_v.reshape(-1, D).astype(BF)
    d8 = jnp.sum(d_q.astype(F32), axis=0)
    d9 = jnp.sum(d_v.astype(F32), axis=0)
    g_q = dot_left(x0_rows_low, d_q)
    g_k = dot_left(x0_low, d_k)
    g_v = dot_left(x0_low, d_v)
    d_rows = d_one + dot_right(d_q, w_qkv[:, :D])
    d_zero = dot_right(d_k, w_qkv[:, D : 2 * D]) + dot_right(d_v, w_qkv[:, 2 * D :])
    d_zero = d_zero.at[row_index].add(jnp.where(live[:, None], d_rows, 0.0))
    d_emb, d0, d1 = norm_backward(d_zero, normal0, inverse0, vec[:, 0])
    d_emb_low = d_emb.astype(BF)
    d13 = jnp.sum(jnp.where(masked_flat[:, None], d_emb_low.astype(F32), 0.0), axis=0)
    g_table = dot_left(latent_low, d_logits) + dot_left(d_emb_low, onehot)
    g_vec = jnp.stack([d0, d1, d2, d3, d4, d5, d6, d7, d8, d9, d10, d11, d12, d13], axis=1)
    g_vec = jnp.pad(g_vec, ((0, 0), (0, OUT_AT - VEC_AT - NVEC)))
    g_join = jnp.concatenate([g_q, g_k, g_v, g_vec, g_out, g_up, g_trans], axis=1)
    return loss_part, present, g_join.astype(BF), g_down.astype(BF), g_table.astype(BF)


def adamw(weight, first, second, gradient, rate):
    first = 0.5 * first + 0.5 * gradient
    second = 0.5 * second + 0.5 * gradient * gradient
    fix = 1.0 - 0.5**STEP
    step = first / fix / (jnp.sqrt(second / fix) + adam_eps)
    return (first, second, weight - rate * (step + decay_rate * weight))


def body(
    n_dp, n_vocab, tokens, picks, species,
    table, table_m, table_v, qkv_w, qkv_m, qkv_v, out_w, out_m, out_v, up_w, up_m, up_v,
    down_w, down_m, down_v, trans_w, trans_m, trans_v, vectors, vectors_m, vectors_v,
):
    block, columns = table.shape
    wide = padded(block)
    rows = qkv_w.shape[0]
    seqs, seq_len = tokens.shape
    both = ("dp", "vocab")
    own_kernels = n_dp == 8 and n_vocab * rows % 16 == 0 and rows % 8 == 0 and columns % 16 == 0 and seqs == 2
    own_kernels = own_kernels and part_cols(wide) * T_PARTS == wide
    if own_kernels:
        column = np.arange(wide * n_vocab)
        token = np.array(token_of(column, block, n_vocab, wide, np))
        col_floor = np.where((token >= 0) & (token < VREAL), 0.0, floor_value).astype(np.float32)[None, :]
        inputs = dict(
            table_in=table.T, down_w=down_w, qkv_w=qkv_w, vectors=vectors.T, out_w=out_w, up_w=up_w, trans_w=trans_w,
            tokens=tokens, picks=picks, species=species, col_floor=jnp.asarray(col_floor),
        )
        saved, counts, loss = forward(inputs, n_dp, n_vocab)
        g_join, g_down, g_table, tile = backward(saved, loss, n_dp, n_vocab)
        states = (
            (table.T, table_m.T, table_v.T), (qkv_w, qkv_m, qkv_v), (vectors.T, vectors_m.T, vectors_v.T),
            (out_w, out_m, out_v), (up_w, up_m, up_v), (trans_w, trans_m, trans_v), (down_w, down_m, down_v),
        )
        new = list(update(tile, counts, g_join, g_down, g_table, states))
        for index in (0, 2):
            new[4 * index : 4 * index + 4] = [array.T for array in new[4 * index : 4 * index + 4]]
        order = (0, 1, 3, 4, 6, 5)
        outs = [new[4 * index + part] for index in order for part in range(4)] + new[8:11]
        return tuple(outs) + tuple(array.reshape(()) for array in new[28:])
    col_token = token_of(jnp.arange(wide * n_vocab, dtype=jnp.int32), block, n_vocab, wide, jnp)
    joined = jnp.concatenate(
        [qkv_w, jnp.pad(vectors, ((0, 0), (0, OUT_AT - VEC_AT - NVEC))), out_w, up_w, trans_w], axis=1
    ).astype(BF)
    down_low = down_w.astype(BF)
    table_t = jnp.pad(table.T.astype(BF), ((0, 0), (0, wide - block)))
    counts = species_counts(picks, species, seq_len)
    piece = part_cols(wide)
    parts = wide // piece
    join_all = lax.all_gather(joined, both, axis=0, tiled=True)
    down_all = lax.all_gather(down_low, both, axis=0, tiled=True)
    table_all = lax.all_gather(table_t, "dp", axis=0, tiled=True).reshape(D, parts, 1, piece)
    table_all = lax.all_gather(table_all, "vocab", axis=2, tiled=True).reshape(D, wide * n_vocab)
    counts = lax.psum(counts, both)
    loss, present, g_join, g_down, g_table = local_step(
        tokens, picks, species, counts, join_all, down_all, table_all, col_token
    )
    g_join = lax.psum_scatter(g_join.astype(F32), both, scatter_dimension=0, tiled=True)
    g_down = lax.psum_scatter(g_down.astype(F32), both, scatter_dimension=0, tiled=True)
    g_table = lax.psum_scatter(g_table, "dp", scatter_dimension=0, tiled=True)
    g_table = g_table.reshape(columns, parts, n_vocab, piece)
    g_table = lax.psum_scatter(g_table, "vocab", scatter_dimension=2, tiled=True)
    g_table = g_table.reshape(columns, wide).astype(F32)
    square = jnp.sum(g_join * g_join) + jnp.sum(g_down * g_down) + jnp.sum(g_table * g_table)
    square, loss_sum = lax.psum((square, loss), both)
    grad_norm = jnp.sqrt(square)
    factor = jnp.minimum(1.0, clip_limit / (grad_norm + 1e-06))
    grads = (
        g_table[:, :block].T, g_join[:, : 3 * D], g_join[:, OUT_AT : OUT_AT + D], g_join[:, UP_AT : UP_AT + FF],
        g_down, g_join[:, TRANS_AT:], g_join[:, VEC_AT : VEC_AT + NVEC],
    )
    masters = (table, qkv_w, out_w, up_w, down_w, trans_w, vectors)
    firsts = (table_m, qkv_m, out_m, up_m, down_m, trans_m, vectors_m)
    seconds = (table_v, qkv_v, out_v, up_v, down_v, trans_v, vectors_v)
    outs = []
    for index in range(7):
        rate = vector_rate if index == 6 else matrix_rate
        first, second, new = adamw(masters[index], firsts[index], seconds[index], grads[index] * factor, rate)
        outs.extend([first, second, new])
        if index < 6:
            outs.append(new.astype(BF))
    return tuple(outs) + (loss_sum, present, grad_norm)


def solution(mesh):
    both = P(("dp", "vocab"), None)
    split = P("vocab", "dp")
    in_specs = (both, both, P(("dp", "vocab"))) + (split,) * 3 + (both,) * 18
    out_specs = (split,) * 4 + (both,) * 23 + (P(),) * 3
    step = functools.partial(body, mesh.shape["dp"], mesh.shape["vocab"])
    return jax.shard_map(step, mesh=mesh, in_specs=in_specs, out_specs=out_specs, check_vma=False)
```

```python
import functools

import jax
import jax.numpy as jnp
import numpy as np
from jax import lax
from jax.experimental import pallas as pl
from jax.experimental.pallas import tpu as pltpu
from jax.sharding import PartitionSpec as P

D = 768
HEADS = 12
HD = 64
FF = 3072
NSPEC = 8
NVEC = 14
STEP = 10
VREAL = 4101
MESH = pl.DeviceIdType.MESH
BF = jnp.bfloat16
F32 = jnp.float32

norm_eps = 1e-05
clip_limit = 0.01
matrix_rate = 0.06
vector_rate = 0.5
decay_rate = 0.01
adam_eps = 1e-08
floor_value = -1e30

VEC_AT = 3 * D
OUT_AT = VEC_AT + 256
UP_AT = OUT_AT + D
TRANS_AT = UP_AT + FF
JOIN = TRANS_AT + D
JOIN_PARTS = (
    (0, 1280),
    (1280, 1280),
    (OUT_AT, 768),
    (UP_AT, 1536),
    (UP_AT + 1536, 1536),
    (TRANS_AT, 768),
)
VMEM_LIMIT = 63 * 2**20


T_PARTS = 9
LATE = 128
DOWN_PARTS = ((LATE, 256), (LATE + 256, D - LATE - 256))
GATHER_X = "yxxyyxxxxyyxyxyxyy"
REDUCE_X = "xxyyyxxyxxyyxxyxxy"
CORE, X, Y = range(3)


def padded(rows):
    return -(-rows // 128) * 128


def part_cols(wide):
    return wide // T_PARTS if wide % (128 * T_PARTS) == 0 else wide


def token_of(column, block, n_vocab, wide, xp):
    piece = part_cols(wide)
    inside = column % (piece * n_vocab)
    row = column // (piece * n_vocab) * piece + inside % piece
    return xp.where(row < block, inside // piece * block + row, -1)


class Place:
    def __init__(self, n_vocab):
        dp = lax.axis_index("dp")
        z = lax.axis_index("vocab")
        core = lax.rem(dp, 2)
        bit_x = lax.rem(lax.div(dp, 2), 2)
        bit_y = lax.div(dp, 4)
        self.dp, self.z, self.core, self.n_vocab = dp, z, core, n_vocab
        self.step_core = 1 - 2 * core
        self.step_x = 2 - 4 * bit_x
        self.step_y = 4 - 8 * bit_y

    def across(self, which):
        return self.dp + (self.step_core, self.step_x, self.step_y)[which]

    def device(self, which):
        return (self.across(which), self.z)

    def along(self, k):
        return lax.rem(self.z + k, self.n_vocab)

    def greet(self, n_dp):
        barrier = pltpu.get_barrier_semaphore()
        for k in range(1, n_dp):
            other = lax.rem(self.dp + k, n_dp)
            pl.semaphore_signal(barrier, inc=1, device_id=(other, self.z), device_id_type=MESH)
        for k in range(1, self.n_vocab):
            pl.semaphore_signal(barrier, inc=1, device_id=(self.dp, self.along(k)), device_id_type=MESH)
        pl.semaphore_wait(barrier, n_dp + self.n_vocab - 2)


def remote(src, dst, send, recv, device):
    return pltpu.make_async_remote_copy(
        src_ref=src, dst_ref=dst, send_sem=send, recv_sem=recv, device_id=device, device_id_type=MESH
    )


def block_view(ref, stride, offset, rows, first, width):
    def view(index):
        return ref.at[pl.ds(pl.multiple_of(index * stride + offset, 16), rows), pl.ds(first, width)]

    return view


class TileSum:
    def __init__(self, place, n_dp, r):
        self.place, self.n_dp, self.r = place, n_dp, r

    def z_copies(self):
        place, r = self.place, self.r
        return [
            remote(
                r.tiles.at[0], r.tile_ring.at[place.z], r.tile_send.at[k - 1], r.tile_recv.at[k - 1],
                (place.dp, place.along(k)),
            )
            for k in range(1, place.n_vocab)
        ]

    def dp_copies(self):
        place, r, base = self.place, self.r, self.place.n_vocab - 1
        return [
            remote(
                r.tiles.at[1], r.tile_land.at[place.dp], r.tile_send.at[base + k - 1],
                r.tile_recv.at[base + k - 1], (lax.rem(place.dp + k, self.n_dp), place.z),
            )
            for k in range(1, self.n_dp)
        ]

    def begin(self, value):
        self.r.tiles[0] = value
        self.r.tile_ring[self.place.z] = value
        for copy in self.z_copies():
            copy.start()

    def go_on(self):
        for copy in self.z_copies():
            copy.wait()
        value = self.r.tile_ring[0]
        for k in range(1, self.place.n_vocab):
            value = value + self.r.tile_ring[k]
        self.r.tiles[1] = value
        self.r.tile_land[self.place.dp] = value
        for copy in self.dp_copies():
            copy.start()

    def total(self):
        for copy in self.dp_copies():
            copy.wait()
        value = self.r.tile_land[0]
        for k in range(1, self.n_dp):
            value = value + self.r.tile_land[k]
        return value


class Sender:
    def __init__(self):
        self.started = []

    def go(self, copy):
        copy.start()
        self.started.append(copy)

    def finish(self):
        for copy in self.started:
            copy.wait_send()


def dot_low(left, right):
    return jnp.dot(left, right, preferred_element_type=F32)


def dot_left(left, right):
    return lax.dot_general(left, right, (((0,), (0,)), ((), ())), preferred_element_type=F32)


def dot_right(left, right):
    return lax.dot_general(left, right, (((1,), (1,)), ((), ())), preferred_element_type=F32)


def norm_forward(value, gain, shift):
    mean = jnp.mean(value, axis=-1, keepdims=True)
    centered = value - mean
    inverse = lax.rsqrt(jnp.mean(centered * centered, axis=-1, keepdims=True) + norm_eps)
    normal = centered * inverse
    return normal * gain + shift, normal, inverse


def norm_backward(gradient, normal, inverse, gain):
    gain_gradient = jnp.sum(gradient * normal, axis=0)
    shift_gradient = jnp.sum(gradient, axis=0)
    scaled = gradient * gain
    inner = jnp.mean(scaled, axis=-1, keepdims=True) + normal * jnp.mean(
        scaled * normal, axis=-1, keepdims=True
    )
    return inverse * (scaled - inner), gain_gradient, shift_gradient


def gelu(value):
    return 0.5 * value * (1.0 + lax.erf(value * 0.7071067811865476))


def gelu_slope(value):
    cdf = 0.5 * (1.0 + lax.erf(value * 0.7071067811865476))
    return cdf + value * jnp.exp(-0.5 * value * value) * 0.3989422804014327


def rows_dot(left, right):
    return jnp.dot(left, right, preferred_element_type=F32)


def norm_rows(value):
    mean = jnp.mean(value, axis=-1, keepdims=True)
    centered = value - mean
    inverse = lax.rsqrt(jnp.mean(centered * centered, axis=-1, keepdims=True) + norm_eps)
    return centered * inverse, inverse


def norm_rows_backward(gradient, normal, inverse, gain):
    scaled = gradient * gain
    inner = jnp.mean(scaled, axis=-1, keepdims=True) + normal * jnp.mean(
        scaled * normal, axis=-1, keepdims=True
    )
    return inverse * (scaled - inner)


def column_sum(value):
    return jnp.sum(value, axis=0, keepdims=True)


def gelu_both(value):
    cdf = 0.5 * (1.0 + lax.erf(value * 0.7071067811865476))
    slope = cdf + value * jnp.exp(-0.5 * value * value) * 0.3989422804014327
    return value * cdf, slope


def aligned(start, size, to=128):
    return pl.ds(pl.multiple_of(start, to), size)


class Refs:
    def __init__(self, names, refs):
        for name, ref in zip(names, refs, strict=True):
            setattr(self, name, ref)


def join_pieces():
    spans = ((0, 3 * D), (VEC_AT, NVEC), (OUT_AT, D), (UP_AT, FF), (TRANS_AT, D))
    pieces = []
    for first, width in JOIN_PARTS:
        for low in (first, first + width // 2):
            high = low + width // 2
            for matrix, (start, size) in enumerate(spans):
                a, b = max(low, start), min(high, start + size)
                if a < b:
                    pieces.append((matrix, a - start, a, b - a))
    return pieces


def packed_at(column):
    for first, width in JOIN_PARTS:
        half = width // 2
        if first <= column < first + width:
            side, inside = divmod(column - first, half)
            return side, first // 2 + inside
    raise ValueError


class Gather:
    def __init__(self, place, r):
        self.place, self.r, self.sender = place, r, Sender()
        n_vocab = place.n_vocab
        self.t_rows, self.t_cols = r.table_t.shape
        self.rows = r.packed.shape[0] // 2
        self.d_rows = r.down_low.shape[0]
        piece = self.t_cols // T_PARTS
        rows = self.rows
        self.chunks = []
        self.z_moves = []
        for q in range(T_PARTS):
            first = piece * n_vocab * q
            where = (
                aligned(place.dp * self.t_rows, self.t_rows, 16),
                aligned(first + place.z * piece, piece),
            )
            view = block_view(r.table, self.t_rows, 0, self.t_rows, first, n_vocab * piece)
            self.chunks.append((view, None))
            self.z_moves.append((r.table_t.at[:, pl.ds(piece * q, piece)], r.table.at[where]))
        for part in JOIN_PARTS[:-1]:
            self.add_part(*part)
        d_rows = self.d_rows
        for first, width in DOWN_PARTS:
            dst = r.down.at[aligned((place.dp * n_vocab + place.z) * d_rows, d_rows, 16), pl.ds(first, width)]
            view = block_view(r.down, d_rows * n_vocab, 0, d_rows * n_vocab, first, width)
            self.chunks.append((view, None))
            self.z_moves.append((r.down_low.at[:, pl.ds(first, width)], dst))
        self.add_part(*JOIN_PARTS[-1])
        self.late = len(self.chunks)

    def add_part(self, first, width):
        place, r, rows = self.place, self.r, self.rows
        cols = pl.ds(first // 2, width // 2)
        view = block_view(r.join, rows * place.n_vocab, 0, rows * place.n_vocab, first, width)
        assemble = functools.partial(self.assemble, first, width)
        self.chunks.append((view, assemble))
        self.z_moves.append((r.packed.at[:, cols], r.stage.at[place.z, :, cols]))

    def place_own(self):
        for src, dst in self.z_moves[:T_PARTS]:
            dst[...] = src[...]

    def place_packed(self):
        self.r.stage[self.place.z] = self.r.packed[...]

    def place_down(self):
        place, r, d_rows = self.place, self.r, self.d_rows
        r.down[aligned((place.dp * place.n_vocab + place.z) * d_rows, d_rows, 16), :] = r.down_low[...]

    def z_copies(self, slot):
        place, r = self.place, self.r
        src, dst = self.z_moves[slot]
        return [
            remote(src, dst, r.z_send.at[slot, k - 1], r.z_recv.at[slot, k - 1], (place.dp, place.along(k)))
            for k in range(1, place.n_vocab)
        ]

    def along_z(self, *slots):
        for slot in slots:
            for copy in self.z_copies(slot):
                self.sender.go(copy)

    def assemble(self, first, width):
        place, r, rows = self.place, self.r, self.rows
        half = width // 2
        at = first // 2
        lefts, rights = [], []
        for k in range(place.n_vocab):
            piece = r.stage[k, :, at : at + half].astype(F32)
            lefts.append(piece[:rows])
            rights.append(piece[rows:])
        where = aligned(place.dp * rows * place.n_vocab, rows * place.n_vocab, 16)
        r.join[where, first : first + half] = jnp.concatenate(lefts, axis=0).astype(BF)
        r.join[where, first + half : first + width] = jnp.concatenate(rights, axis=0).astype(BF)

    def move(self, i, k, arriving):
        place, r = self.place, self.r
        if i == self.late:
            d_rows = self.d_rows
            if k < 3:
                view = block_view(
                    r.down, d_rows * place.n_vocab, place.z * d_rows, d_rows, 0, LATE
                )
            else:
                view = block_view(r.down, d_rows * place.n_vocab, 0, d_rows * place.n_vocab, 0, LATE)
        else:
            view = self.chunks[i][0]
        one, two = self.directions(i)
        own, a, b = place.dp, place.across(one), place.across(two)
        ab = a + b - own
        if k < 3:
            block = (a, b, ab)[k] if arriving else (own, own, a)[k]
            which = (one, two, two)[k]
        else:
            block = (own, a, b, ab)[k - 3] + (place.step_core if arriving else 0)
            which = CORE
        return remote(view(block), view(block), r.d_send.at[i, k], r.d_recv.at[i, k], place.device(which))

    def directions(self, i):
        return (X, Y) if GATHER_X[i] == "x" else (Y, X)

    def send(self, i, *which):
        for k in which:
            self.sender.go(self.move(i, k, False))

    def arrive(self, i, *which):
        for k in which:
            self.move(i, k, True).wait_recv()

    def late_copies(self, arriving):
        place, r, d_rows = self.place, self.r, self.d_rows
        one, two = self.directions(self.late)
        a, b = place.across(one), place.across(two)
        copies = []
        for j, block in enumerate((place.dp, a, b, a + b - place.dp)):
            for k in range(1, place.n_vocab):
                z = place.along(place.n_vocab - k) if arriving else place.z
                at = r.down.at[aligned((block * place.n_vocab + z) * d_rows, d_rows, 16), pl.ds(0, LATE)]
                copies.append(
                    remote(at, at, r.l_send.at[j, k - 1], r.l_recv.at[j, k - 1], (place.dp, place.along(k)))
                )
        return copies

    def after_z(self, i):
        for copy in self.z_copies(i):
            copy.wait_recv()
        if self.chunks[i][1] is not None:
            self.chunks[i][1]()
        self.send(i, 0, 1, 3)

    def after_one(self, i):
        self.arrive(i, 0)
        self.send(i, 2)
        if i != self.late:
            self.send(i, 4)

    def after_two(self, i):
        self.arrive(i, 1)
        if i != self.late:
            self.send(i, 5)

    def after_both(self, i):
        self.arrive(i, 2)
        if i != self.late:
            self.send(i, 6)
        else:
            for copy in self.late_copies(False):
                self.sender.go(copy)
            self.along_z(*range(Z_TAIL, Z_SLOTS))

    def after_late(self, i):
        for copy in self.late_copies(True):
            copy.wait_recv()
        self.send(i, 3, 4, 5, 6)

    def go_on(self, steps):
        for kind, i in steps:
            (self.after_z, self.after_one, self.after_two, self.after_both, self.after_late)[kind](i)

    def need(self, *which):
        for i in which:
            self.arrive(i, 3, 4, 5, 6)


N_CHUNKS = T_PARTS + len(JOIN_PARTS) + len(DOWN_PARTS) + 1
Z_SLOTS = N_CHUNKS - 1
GATHER_PLAN = (
    (
        (1, 17), (0, 0), (2, 17), (0, 1), (3, 17), (0, 2), (1, 0), (2, 0), (0, 3), (2, 1), (1, 1), (0, 4),
        (2, 2), (1, 2), (0, 5), (1, 3), (3, 0), (0, 6), (3, 1), (2, 3), (0, 7), (1, 4), (2, 4), (0, 8), (3, 2),
        (1, 5),
    ),
    (
        (2, 5), (3, 3), (2, 6), (1, 6), (0, 9), (2, 7), (1, 7), (2, 8), (3, 4), (0, 10), (3, 5), (1, 8),
        (3, 6), (0, 11),
    ),
    (
        (2, 9), (1, 9), (3, 7), (2, 10), (4, 17), (1, 11), (1, 10), (3, 8), (0, 12),
    ),
    (
        (2, 11), (3, 9), (3, 11), (0, 13), (3, 10),
    ),
    (
        (1, 12), (0, 14),
    ),
    (
        (0, 15), (2, 12),
    ),
    (
        (1, 13), (0, 16), (2, 13),
    ),
    (
        (1, 14),
    ),
    (
        (3, 12),
    ),
    (
        (2, 15), (2, 14),
    ),
    (
        (3, 13), (1, 15),
    ),
    (
        (1, 16), (2, 16), (3, 14), (3, 15), (3, 16),
    ),
    (),
    (),
)
Z_TAIL = T_PARTS + 3


N_FORWARD_IN = 11


def saved_shapes(rows, d_rows, tokens, picked, t_cols_all):
    return dict(
        join=((rows, JOIN), BF),
        down=((d_rows, D), BF),
        normal0=((tokens, D), BF),
        inverse0=((tokens, 1), F32),
        x0_low=((tokens, D), BF),
        keys=((tokens, D), BF),
        values=((tokens, D), BF),
        query=((picked, D), BF),
        x0_rows=((picked, D), BF),
        att=((picked, D), BF),
        normal1=((picked, D), F32),
        inverse1=((picked, 1), F32),
        x1_low=((picked, D), BF),
        hidden=((picked, FF), BF),
        slope=((picked, FF), BF),
        x2_low=((picked, D), BF),
        d_trans=((picked, D), BF),
        d_two=((picked, D), F32),
        d_logits=((picked, t_cols_all), BF),
        latent=((picked, D), BF),
        g_vec=((16, D), F32),
        vec=((16, D), F32),
        col_ids=((tokens, 1), jnp.int32),
        spots=((picked, 1), jnp.int32),
    )


def tile_scratch(n_dp, n_vocab):
    dma = pltpu.SemaphoreType.DMA
    return dict(
        tiles=pltpu.VMEM((2, 8, 128), F32),
        tile_land=pltpu.VMEM((n_dp, 8, 128), F32),
        tile_ring=pltpu.VMEM((n_vocab, 8, 128), F32),
        tile_send=dma((n_dp + n_vocab - 2,)),
        tile_recv=dma((n_dp + n_vocab - 2,)),
    )


def whole_part(value, by):
    return jnp.floor((value + 0.5) * (1.0 / by))


def forward_kernel(n_dp, n_vocab, names, out_names, *refs):
    r = Refs(names, refs[:N_FORWARD_IN] + refs[N_FORWARD_IN + len(out_names) + 2 :])
    out = Refs(out_names, refs[N_FORWARD_IN : N_FORWARD_IN + len(out_names)])
    counts_out, loss_out = refs[N_FORWARD_IN + len(out_names) : N_FORWARD_IN + len(out_names) + 2]
    seqs, seq_len = r.tokens.shape
    tokens = seqs * seq_len
    picked = r.spots.shape[0]
    slots = picked // seqs
    block = r.table_in.shape[1]
    place = Place(n_vocab)

    def prepare_table():
        full = block // 128 * 128
        r.table_t[:, :full] = r.table_in[:, :full].astype(BF)
        if full < r.table_t.shape[1]:
            r.table_rest[...] = jnp.zeros_like(r.table_rest)
            r.table_rest[:, : block - full] = r.table_in[:, full:]
            r.table_t[:, full:] = r.table_rest[...].astype(BF)

    def prepare_packed():
        r.vec_rest[...] = jnp.zeros_like(r.vec_rest)
        rows = r.packed.shape[0] // 2
        r.vec_rows[...] = jnp.zeros_like(r.vec_rows)
        r.vec_rows[:NVEC, :rows] = r.vectors[...]
        r.vec_rest[:, :16] = r.vec_rows[...].T[:rows, :]
        sources = (r.qkv_w, r.vec_rest, r.out_w, r.up_w, r.trans_w)
        spans = ((0, 3 * D), (VEC_AT, OUT_AT - VEC_AT), (OUT_AT, D), (UP_AT, FF), (TRANS_AT, D))

        def read(low, high):
            found = []
            for source, (start, size) in zip(sources, spans, strict=True):
                a, b = max(low, start), min(high, start + size)
                if a < b:
                    found.append(source[:, a - start : b - start])
            return found[0] if len(found) == 1 else jnp.concatenate(found, axis=1)

        for first, width in JOIN_PARTS:
            half = width // 2
            both = jnp.concatenate([read(first, first + half), read(first + half, first + width)], axis=0)
            r.packed[:, first // 2 : first // 2 + half] = both.astype(BF)

    def prepare_ids():
        piece = part_cols(r.table_t.shape[1])
        token = r.tokens[...].astype(F32)
        owner = whole_part(token, block)
        row = token - owner * block
        part = whole_part(row, piece)
        column = part * (piece * n_vocab) + owner * piece + (row - part * piece)
        r.wide_rows[...] = jnp.full(r.wide_rows.shape, float(seq_len), F32)
        r.wide_rows[:seqs, : r.picks.shape[1]] = r.picks[...].astype(F32)
        spots = r.wide_rows[...].T
        lane = lax.broadcasted_iota(jnp.int32, (slots, 128), 1)
        masked_columns = []
        for s in range(seqs):
            rows = slice(s * slots, (s + 1) * slots)
            spot = spots[:slots, s : s + 1]
            position = lax.broadcasted_iota(jnp.int32, (slots, seq_len), 1).astype(F32)
            here = spot == position
            r.targets[rows, :] = jnp.sum(
                jnp.where(here, column[s : s + 1, :], 0.0), axis=-1, keepdims=True
            ).astype(jnp.int32)
            live = spot < float(seq_len)
            r.spots[rows, :] = jnp.where(live, spot, -1.0).astype(jnp.int32)
            kind = r.species[s] == lane
            r.own_kinds[rows, :] = jnp.where(kind & live, 1.0, 0.0)
            masked = jnp.max(jnp.where(here, 1.0, 0.0), axis=0, keepdims=True)
            masked_columns.append(jnp.where(masked > 0.0, -1.0, column[s : s + 1, :]))
        masked_columns.append(jnp.zeros((8 - seqs, seq_len), F32))
        turned = jnp.concatenate(masked_columns, axis=0).T
        for s in range(seqs):
            r.col_ids[s * seq_len : (s + 1) * seq_len, :] = turned[:, s : s + 1].astype(jnp.int32)

    saves = []

    def save(src, dst, *cols):
        if cols:
            src, dst = src.at[:, pl.ds(*cols)], dst.at[:, pl.ds(*cols)]
        copy = pltpu.make_async_copy(src, dst, r.save_sem.at[len(saves)])
        copy.start()
        saves.append(copy)

    def embed(q):
        width = r.table.shape[1] // 3
        first = q * width

        def step(i, carry):
            at = aligned(i * 256, 256)
            ids = r.col_ids[at, :]
            onehot = (ids == lax.broadcasted_iota(jnp.int32, (256, width), 1) + first).astype(BF)
            part = dot_right(onehot, r.table[:, first : first + width])
            r.embedded[at, :] = part if q == 0 else part + r.embedded[at, :]
            return carry

        lax.fori_loop(0, tokens // 256, step, 0)

    def first_norm():
        columns = r.join[:, VEC_AT : VEC_AT + 128].astype(F32).T
        r.vec[...] = columns[:16]

        def step(i, carry):
            at = aligned(i * 128, 128)
            value = jnp.where(r.col_ids[at, :] < 0, r.vec[13:14, :], r.embedded[at, :])
            normal, inverse = norm_rows(value)
            stream = normal * r.vec[0:1, :] + r.vec[1:2, :]
            high = stream.astype(BF)
            r.normal0[at, :] = normal.astype(BF)
            r.inverse0[at, :] = inverse
            r.x0_low[at, :] = high
            r.x0_rest[at, :] = (stream - high.astype(F32)).astype(BF)
            return carry

        lax.fori_loop(0, tokens // 128, step, 0)

    def project():
        def step(i, carry):
            at = aligned(i * 256, 256)
            low = r.x0_low[at, :]
            r.keys[at, :] = rows_dot(low, r.join[:, D : 2 * D]).astype(BF)
            r.values[at, :] = (rows_dot(low, r.join[:, 2 * D : 3 * D]) + r.vec[9:10, :]).astype(BF)
            return carry

        lax.fori_loop(0, tokens // 256, step, 0)
        for s in range(seqs):
            rows = slice(s * slots, (s + 1) * slots)
            seq = slice(s * seq_len, (s + 1) * seq_len)
            pick = (r.spots[rows, :] == lax.broadcasted_iota(jnp.int32, (slots, seq_len), 1)).astype(BF)
            high = rows_dot(pick, r.x0_low[seq, :])
            r.stream[rows, :] = high + rows_dot(pick, r.x0_rest[seq, :])
            r.x0_rows[rows, :] = high.astype(BF)
        r.query[...] = (rows_dot(r.x0_rows[...], r.join[:, :D]) + r.vec[8:9, :]).astype(BF)

    def attend(low, high):
        lane = lax.broadcasted_iota(jnp.int32, (slots, 128), 1)

        def step(j, carry):
            lanes = aligned(j * 128, 128)
            for s in range(seqs):
                rows = slice(s * slots, (s + 1) * slots)
                seq = slice(s * seq_len, (s + 1) * seq_len)
                q2 = r.query[rows, lanes]
                k2 = r.keys[seq, lanes]
                v2 = r.values[seq, lanes]
                parts = []
                for a in range(2):
                    mine = (lane >= HD) if a else (lane < HD)
                    scores = dot_right(jnp.where(mine, q2, jnp.zeros_like(q2)), k2) * HD ** (-0.5)
                    top = jnp.max(scores, axis=-1, keepdims=True)
                    expo = jnp.exp(scores - top)
                    total = jnp.sum(expo, axis=-1, keepdims=True)
                    parts.append(rows_dot((expo * (1.0 / total)).astype(BF), v2))
                r.att[rows, lanes] = jnp.where(lane < HD, parts[0], parts[1]).astype(BF)
            return carry

        lax.fori_loop(low, high, step, 0)

    def after_attention():
        value = r.stream[...] + (rows_dot(r.att[...], r.join[:, OUT_AT : OUT_AT + D]) + r.vec[10:11, :])
        normal, inverse = norm_rows(value)
        r.normal1[...] = normal
        r.inverse1[...] = inverse
        stream = normal * r.vec[2:3, :] + r.vec[3:4, :]
        r.stream[...] = stream
        r.x1_low[...] = stream.astype(BF)

    def feed_up(first):
        def step(j, carry):
            cols = aligned(j * 512, 512)
            act, slope = gelu_both(rows_dot(r.x1_low[...], r.join[:, aligned(UP_AT + j * 512, 512)]))
            r.hidden[:, cols] = act.astype(BF)
            r.slope[:, cols] = slope.astype(BF)
            return carry

        lax.fori_loop(3 * first, 3 * first + 3, step, 0)

    def feed_down():
        value = r.stream[...] + (rows_dot(r.hidden[...], r.down[...]) + r.vec[11:12, :])
        normal, inverse = norm_rows(value)
        r.normal2[...] = normal
        r.inverse2[...] = inverse
        r.x2_low[...] = (normal * r.vec[4:5, :] + r.vec[5:6, :]).astype(BF)

    def head(counts):
        act, slope3 = gelu_both(
            rows_dot(r.x2_low[...], r.join[:, TRANS_AT : TRANS_AT + D]) + r.vec[12:13, :]
        )
        normal3, inverse3 = norm_rows(act)
        r.stream[...] = normal3
        latent = (normal3 * r.vec[6:7, :] + r.vec[7:8, :]).astype(BF)
        r.latent[...] = latent
        steps = 6
        width = r.table.shape[1] // steps

        def scores(i, top):
            cols = aligned(i * width, width)
            logits = rows_dot(r.latent[...], r.table[:, cols])
            logits = jnp.where(r.col_floor[:, cols] == 0.0, logits, floor_value)
            r.logits[:, cols] = logits
            return jnp.maximum(top, jnp.max(logits, axis=-1, keepdims=True))

        top = lax.fori_loop(0, steps, scores, jnp.full((picked, 1), floor_value, F32))

        def spread(i, carry):
            total, hit = carry
            cols = aligned(i * width, width)
            logits = r.logits[:, cols]
            column = lax.broadcasted_iota(jnp.int32, (picked, width), 1) + i * width
            hit = hit + jnp.sum(jnp.where(column == r.targets[...], logits, 0.0), axis=-1, keepdims=True)
            expo = jnp.exp(logits - top)
            r.logits[:, cols] = expo
            return total + jnp.sum(expo, axis=-1, keepdims=True), hit

        zero = jnp.zeros((picked, 1), F32)
        total, hit = lax.fori_loop(0, steps, spread, (zero, zero))
        loss_rows = top + jnp.log(total) - hit
        here = counts > 0.0
        present = jnp.sum(here.astype(F32), axis=-1, keepdims=True)
        inverse = jnp.where(here, 1.0 / jnp.maximum(counts, 1.0), 0.0)
        weight = jnp.sum(r.own_kinds[...] * inverse, axis=-1, keepdims=True)
        loss_out[...] = jnp.broadcast_to(column_sum(weight * loss_rows), (8, 128))
        weight = weight / present
        scale = weight / total

        def slopes(i, d_latent):
            cols = aligned(i * width, width)
            column = lax.broadcasted_iota(jnp.int32, (picked, width), 1) + i * width
            d_logits = r.logits[:, cols] * scale - jnp.where(column == r.targets[...], weight, 0.0)
            d_logits = d_logits.astype(BF)
            r.d_logits[:, cols] = d_logits
            return d_latent + dot_right(d_logits, r.table[:, cols])

        d_latent = lax.fori_loop(0, steps, slopes, jnp.zeros((picked, D), F32))
        normal3 = r.stream[...]
        r.g_vec[6:7, :] = column_sum(d_latent * normal3)
        r.g_vec[7:8, :] = column_sum(d_latent)
        d_act = norm_rows_backward(d_latent, normal3, inverse3, r.vec[6:7, :])
        d_trans = (d_act * slope3).astype(BF)
        r.d_trans[...] = d_trans
        r.g_vec[12:13, :] = column_sum(d_trans.astype(F32))
        d_two = dot_right(d_trans, r.join[:, TRANS_AT : TRANS_AT + D])
        normal2 = r.normal2[...]
        r.g_vec[4:5, :] = column_sum(d_two * normal2)
        r.g_vec[5:6, :] = column_sum(d_two)
        r.d_two[...] = norm_rows_backward(d_two, normal2, r.inverse2[...], r.vec[4:5, :])

    gather = Gather(place, r)
    prepare_table()
    place.greet(n_dp)
    gather.along_z(0, 1)
    r.down_low[...] = r.down_w[...].astype(BF)
    gather.place_down()
    gather.send(gather.late, 0, 1)
    gather.along_z(*range(2, T_PARTS))
    gather.place_own()
    prepare_packed()
    gather.place_packed()
    gather.along_z(*range(T_PARTS, Z_TAIL))
    plan = iter(GATHER_PLAN)
    first = next(plan)
    gather.go_on(first[:8])
    prepare_ids()
    r.g_vec[...] = jnp.zeros_like(r.g_vec)
    counting = TileSum(place, n_dp, r)
    counting.begin(jnp.broadcast_to(column_sum(r.own_kinds[...]), (8, 128)))
    gather.go_on(first[8:])
    thirds = T_PARTS // 3
    for q in range(3):
        gather.need(*range(thirds * q, thirds * q + thirds))
        embed(q)
        gather.go_on(next(plan))
    at = T_PARTS
    gather.need(at, at + 1)
    first_norm()
    save(r.vec, out.vec)
    save(r.col_ids, out.col_ids)
    save(r.spots, out.spots)
    save(r.normal0, out.normal0)
    save(r.inverse0, out.inverse0)
    save(r.x0_low, out.x0_low)
    save(r.join, out.join, 0, OUT_AT)
    gather.go_on(next(plan))
    project()
    save(r.keys, out.keys)
    save(r.values, out.values)
    save(r.query, out.query)
    save(r.x0_rows, out.x0_rows)
    counting.go_on()
    gather.go_on(next(plan))
    for pair in range(0, HEADS // 2, 2):
        attend(pair, pair + 2)
        gather.go_on(next(plan))
    save(r.att, out.att)
    gather.need(at + 2)
    after_attention()
    save(r.normal1, out.normal1)
    save(r.inverse1, out.inverse1)
    save(r.x1_low, out.x1_low)
    gather.go_on(next(plan))
    for part in range(2):
        gather.need(at + 3 + part)
        feed_up(part)
        gather.go_on(next(plan))
    save(r.join, out.join, OUT_AT, TRANS_AT - OUT_AT)
    save(r.hidden, out.hidden)
    save(r.slope, out.slope)
    counts = counting.total()
    counts_out[...] = counts
    gather.need(at + 5, at + 6, gather.late)
    feed_down()
    save(r.down, out.down)
    save(r.x2_low, out.x2_low)
    gather.go_on(next(plan))
    gather.need(at + 7)
    save(r.join, out.join, TRANS_AT, D)
    head(counts[0:1, :])
    gather.go_on(next(plan))
    for src, dst in (
        (r.d_trans, out.d_trans), (r.d_two, out.d_two), (r.d_logits, out.d_logits), (r.latent, out.latent),
        (r.g_vec, out.g_vec),
    ):
        save(src, dst)
    gather.sender.finish()
    for copy in saves:
        copy.wait()


def forward(inputs, n_dp, n_vocab):
    rows = inputs["qkv_w"].shape[0]
    columns, block = inputs["table_in"].shape
    wide = padded(block)
    d_rows = inputs["down_w"].shape[0]
    seqs, seq_len = inputs["tokens"].shape
    tokens, picked = seqs * seq_len, seqs * 128
    table_shape = (D, wide * n_vocab)
    shapes = saved_shapes(rows * n_dp * n_vocab, d_rows * n_dp * n_vocab, tokens, picked, wide * n_vocab)
    dma = pltpu.SemaphoreType.DMA
    scratch = {name: pltpu.VMEM(*shape) for name, shape in shapes.items()}
    scratch.update(
        table=pltpu.VMEM(table_shape, BF),
        table_t=pltpu.VMEM((columns, wide), BF),
        table_rest=pltpu.VMEM((columns, 128), F32),
        vec_rows=pltpu.VMEM((16, 128), F32),
        packed=pltpu.VMEM((2 * rows, JOIN // 2), BF),
        vec_rest=pltpu.VMEM((rows, OUT_AT - VEC_AT), F32),
        down_low=pltpu.VMEM((d_rows, D), BF),
        wide_rows=pltpu.VMEM((8, 128), F32),
        targets=pltpu.VMEM((picked, 1), jnp.int32),
        own_kinds=pltpu.VMEM((picked, 128), F32),
        stage=pltpu.VMEM((n_vocab, 2 * rows, JOIN // 2), BF),
        embedded=pltpu.VMEM((tokens, D), F32),
        x0_rest=pltpu.VMEM((tokens, D), BF),
        stream=pltpu.VMEM((picked, D), F32),
        normal2=pltpu.VMEM((picked, D), F32),
        inverse2=pltpu.VMEM((picked, 1), F32),
        logits=pltpu.VMEM((picked, wide * n_vocab), F32),
        z_send=dma((Z_SLOTS, n_vocab - 1)),
        z_recv=dma((Z_SLOTS, n_vocab - 1)),
        l_send=dma((4, n_vocab - 1)),
        l_recv=dma((4, n_vocab - 1)),
        d_send=dma((N_CHUNKS, 7)),
        d_recv=dma((N_CHUNKS, 7)),
        save_sem=dma((len(shapes) + 2,)),
        **tile_scratch(n_dp, n_vocab),
    )
    vmem = pl.BlockSpec(memory_space=pltpu.VMEM)
    anywhere = pl.BlockSpec(memory_space=pl.ANY)
    tile = jax.ShapeDtypeStruct((8, 128), F32)
    names = tuple(inputs) + tuple(scratch)
    smem = pl.BlockSpec(memory_space=pltpu.SMEM)
    outs = pl.pallas_call(
        functools.partial(forward_kernel, n_dp, n_vocab, names, tuple(shapes)),
        out_shape=tuple(jax.ShapeDtypeStruct(*shape) for shape in shapes.values()) + (tile, tile),
        in_specs=[smem if name == "species" else vmem for name in inputs],
        out_specs=(anywhere,) * len(shapes) + (vmem, vmem),
        scratch_shapes=list(scratch.values()),
        compiler_params=pltpu.CompilerParams(
            collective_id=0, has_side_effects=True, vmem_limit_bytes=VMEM_LIMIT
        ),
    )(*inputs.values())
    return dict(zip(shapes, outs[:-2], strict=True)), outs[-2], outs[-1]


JOINED, DOWN, TABLE = range(3)
REDUCE_ORDER = (
    (JOINED, 5), (JOINED, 3), (JOINED, 4), (DOWN, -1), (DOWN, 0), (DOWN, 1), (JOINED, 2), (JOINED, 0), (JOINED, 1),
) + tuple((TABLE, j) for j in range(T_PARTS))


REDUCE_PLAN = (
    (
        (0, 0),
    ),
    (
        (0, 1), (1, 0),
    ),
    (
        (0, 2),
    ),
    (
        (0, 3), (0, 4), (1, 1),
    ),
    (
        (0, 5),
    ),
    (
        (0, 6), (2, 0), (1, 2),
    ),
    (),
    (
        (3, 0),
    ),
    (
        (1, 5),
    ),
    (),
    (
        (2, 1),
    ),
    (),
    (),
    (
        (2, 2),
    ),
    (
        (1, 3), (1, 4),
    ),
    (),
    (
        (3, 1), (2, 5),
    ),
    (
        (1, 6),
    ),
    (),
    (
        (0, 7), (0, 8),
    ),
    (
        (3, 2), (4, 3),
    ),
    (
        (0, 9), (2, 4),
    ),
    (
        (0, 10),
    ),
    (
        (0, 11), (1, 7),
    ),
    (
        (0, 12), (1, 8), (2, 6),
    ),
    (
        (0, 13), (3, 5),
    ),
    (
        (0, 14), (2, 3),
    ),
    (
        (0, 15), (3, 4),
    ),
    (
        (0, 16),
    ),
    (
        (0, 17),
    ),
    (
        (2, 7), (1, 10), (2, 8), (3, 3), (1, 9), (3, 6), (3, 7), (2, 10), (1, 11), (1, 12), (2, 9), (3, 8),
        (1, 13), (3, 10), (1, 14), (2, 11), (2, 12), (3, 9), (1, 15), (1, 17), (2, 13), (2, 14), (3, 11),
        (3, 12), (1, 16), (2, 15), (2, 17), (3, 14), (3, 13), (3, 15), (2, 16), (3, 17), (3, 16),
    ),
)


class Reduce:
    def __init__(self, place, r, t_cols, from_core, from_two, from_one):
        self.place, self.r, self.sender = place, r, Sender()
        self.from_core, self.from_two, self.from_one = from_core, from_two, from_one
        n_vocab = place.n_vocab
        rows = r.join_out.shape[0] // 2
        d_rows = r.down_out.shape[0]
        t_rows = r.table_out.shape[0]
        piece = t_cols // T_PARTS
        self.rows, self.d_rows, self.t_rows, self.piece = rows, d_rows, t_rows, piece
        self.chunks = []
        for kind, j in REDUCE_ORDER:
            if kind == JOINED:
                first, width = JOIN_PARTS[j]
                view = block_view(r.join, rows * n_vocab, 0, rows * n_vocab, first, width)
            elif kind == DOWN:
                first, width = DOWN_PARTS[j] if j >= 0 else (0, LATE)
                view = block_view(r.down, d_rows * n_vocab, 0, d_rows * n_vocab, first, width)
            else:
                view = block_view(r.table, t_rows, 0, t_rows, n_vocab * piece * j, n_vocab * piece)
            narrow = view
            if (kind, j) == (DOWN, -1):
                narrow = block_view(r.down, d_rows * n_vocab, place.z * d_rows, d_rows, 0, LATE)
            self.chunks.append(((kind, j), view, narrow))
        self.jobs = {}

    def blocks(self, i):
        place = self.place
        one, two = (X, Y) if REDUCE_X[i] == "x" else (Y, X)
        own, a, b = place.dp, place.across(one), place.across(two)
        return one, two, (own, a, b, a + b - own)

    def add_into(self, target, *sources):
        def step(i, carry):
            at = aligned(i * 16, 16, 16)
            if len(sources) == 1:
                target[at, :] = target[at, :] + sources[0][at, :]
            else:
                total = target[at, :].astype(F32)
                for source in sources:
                    total = total + source[at, :].astype(F32)
                target[at, :] = total.astype(BF)
            return carry

        lax.fori_loop(0, target.shape[0] // 16, step, 0)

    def to_core(self, i, k):
        _, _, blocks = self.blocks(i)
        block = blocks[k] + self.place.step_core
        r, place = self.r, self.place
        return remote(
            self.chunks[i][1](block), self.from_core[i].at[k], r.d_send.at[i, k], r.d_recv.at[i, k],
            place.device(CORE),
        )

    def to_two(self, i, k):
        _, two, blocks = self.blocks(i)
        r, place = self.r, self.place
        return remote(
            self.chunks[i][2](blocks[2 + k]), self.from_two[i].at[k], r.d_send.at[i, 4 + k],
            r.d_recv.at[i, 4 + k], place.device(two),
        )

    def to_one(self, i):
        one, _, blocks = self.blocks(i)
        r, place = self.r, self.place
        return remote(
            self.chunks[i][2](blocks[1]), self.from_one[i], r.d_send.at[i, 6], r.d_recv.at[i, 6],
            place.device(one),
        )

    def late_copies(self, i):
        place, r, d_rows = self.place, self.r, self.d_rows
        _, _, blocks = self.blocks(i)
        copies = []
        for j, block in enumerate(blocks):
            for k in range(1, place.n_vocab):
                row = (block * place.n_vocab + place.along(k)) * d_rows
                copies.append(
                    remote(
                        r.down.at[aligned(row, d_rows, 16), pl.ds(0, LATE)], r.z_late.at[j, k - 1],
                        r.l_send.at[j, k - 1], r.l_recv.at[j, k - 1], (place.dp, place.along(k)),
                    )
                )
        return copies

    def z_copies(self, slot, src_of, dst_of):
        place, r = self.place, self.r
        return [
            remote(
                src_of(place.along(k)), dst_of(k - 1), r.z_send.at[slot, k - 1], r.z_recv.at[slot, k - 1],
                (place.dp, place.along(k)),
            )
            for k in range(1, place.n_vocab)
        ]

    def pack(self, first, width):
        r, rows, n_vocab = self.r, self.rows, self.place.n_vocab
        half = width // 2
        at = first // 2
        where = aligned(self.place.dp * rows * n_vocab, rows * n_vocab, 16)
        block = r.join[where, first : first + width].astype(F32)
        for k in range(n_vocab):
            piece = block[k * rows : (k + 1) * rows]
            r.packed[k, :, at : at + half] = jnp.concatenate([piece[:, :half], piece[:, half:]], axis=0).astype(BF)

    def along_z(self, i):
        place, r = self.place, self.r
        kind, j = self.chunks[i][0]
        slot = len(self.jobs)
        if kind == JOINED:
            first, width = JOIN_PARTS[j]
            self.pack(first, width)
            cols = pl.ds(first // 2, width // 2)
            copies = self.z_copies(slot, lambda to: r.packed.at[to, :, cols], lambda k: r.z_join.at[k, :, cols])
        elif kind == DOWN:
            first, width = DOWN_PARTS[j]
            cols = pl.ds(first, width)
            d_rows, n_vocab = self.d_rows, place.n_vocab
            copies = self.z_copies(
                slot,
                lambda to: r.down.at[aligned((place.dp * n_vocab + to) * d_rows, d_rows, 16), cols],
                lambda k: r.z_down.at[k, :, pl.ds(first - LATE, width)],
            )
        else:
            piece, q = self.piece, j
            copies = self.z_copies(
                slot,
                lambda to: r.table.at[
                    aligned(place.dp * self.t_rows, self.t_rows, 16),
                    aligned(q * piece * place.n_vocab + to * piece, piece),
                ],
                lambda k: r.z_table.at[k, :, pl.ds(q * piece, piece)],
            )
        for copy in copies:
            self.sender.go(copy)
        self.jobs[i] = copies

    def is_late(self, i):
        return self.chunks[i][0] == (DOWN, -1)

    def go_on(self, steps):
        for stage, i in steps:
            (self.start, self.after_core, self.after_two, self.after_one, self.after_late)[stage](i)

    def start(self, i):
        for k in range(4):
            self.sender.go(self.to_core(i, k))

    def after_core(self, i):
        view = self.chunks[i][1]
        _, _, blocks = self.blocks(i)
        for k in (2, 3, 0, 1):
            self.to_core(i, k).wait_recv()
            self.add_into(view(blocks[k]), self.from_core[i].at[k])
            if k == 3 and not self.is_late(i):
                self.send_two(i)
        if self.is_late(i):
            for copy in self.late_copies(i):
                self.sender.go(copy)

    def after_late(self, i):
        narrow = self.chunks[i][2]
        _, _, blocks = self.blocks(i)
        for copy in self.late_copies(i):
            copy.wait_recv()
        for j in (2, 3, 0, 1):
            parts = [self.r.z_late.at[j, k] for k in range(self.place.n_vocab - 1)]
            self.add_into(narrow(blocks[j]), *parts)
            if j == 3:
                self.send_two(i)

    def send_two(self, i):
        for k in range(2):
            self.sender.go(self.to_two(i, k))

    def after_two(self, i):
        narrow = self.chunks[i][2]
        _, _, blocks = self.blocks(i)
        self.to_two(i, 1).wait_recv()
        self.add_into(narrow(blocks[1]), self.from_two[i].at[1])
        self.sender.go(self.to_one(i))
        self.to_two(i, 0).wait_recv()
        self.add_into(narrow(blocks[0]), self.from_two[i].at[0])

    def after_one(self, i):
        self.to_one(i).wait_recv()
        self.add_into(self.chunks[i][2](self.place.dp), self.from_one[i])
        if not self.is_late(i):
            self.along_z(i)

    def collect(self):
        place, r = self.place, self.r
        n_vocab = place.n_vocab

        def total(own, parts, out, cols):
            whole = own.astype(F32)
            for part in parts:
                whole = whole + part.astype(F32)
            out[:, cols] = whole
            return jnp.sum(column_sum(whole * whole), axis=-1, keepdims=True)

        square = jnp.zeros((1, 1), F32)
        rows = aligned((place.dp * n_vocab + place.z) * self.d_rows, self.d_rows, 16)
        square += total(r.down[rows, :LATE], (), r.down_out, slice(0, LATE))
        for i, ((kind, j), _, _) in enumerate(self.chunks):
            if self.is_late(i):
                continue
            for copy in self.jobs[i]:
                copy.wait_recv()
            if kind == JOINED:
                first, width = JOIN_PARTS[j]
                cols = slice(first // 2, first // 2 + width // 2)
                own = r.packed[place.z, :, cols]
                parts = [r.z_join[k, :, cols] for k in range(n_vocab - 1)]
                square += total(own, parts, r.join_out, cols)
            elif kind == DOWN:
                first, width = DOWN_PARTS[j]
                low = first - LATE
                parts = [r.z_down[k, :, low : low + width] for k in range(n_vocab - 1)]
                own = r.down[rows, first : first + width]
                square += total(own, parts, r.down_out, slice(first, first + width))
            else:
                q = j
                cols = slice(q * self.piece, (q + 1) * self.piece)
                t_rows = aligned(place.dp * self.t_rows, self.t_rows, 16)
                own = r.table[t_rows, aligned(q * self.piece * n_vocab + place.z * self.piece, self.piece)]
                parts = [r.z_table[k, :, cols] for k in range(n_vocab - 1)]
                square += total(own, parts, r.table_out, cols)
        return square


def backward_kernel(n_dp, n_vocab, in_names, names, *refs):
    given = Refs(in_names, refs[: len(in_names)])
    scratch = refs[len(in_names) :]
    n_chunks = len(REDUCE_ORDER)
    lands, scratch = scratch[-3 * n_chunks :], scratch[: -3 * n_chunks]
    r = Refs(names, scratch)
    tokens = given.col_ids.shape[0]
    picked = given.spots.shape[0]
    seqs = 2
    seq_len, slots = tokens // seqs, picked // seqs
    wide = r.table.shape[1]

    def keys_at(s):
        return r.table.at[pl.ds(0, seq_len), pl.ds(s * D, D)]

    def values_at(s):
        return r.table.at[pl.ds(0, seq_len), pl.ds((2 + s) * D, D)]

    hidden = r.table.at[pl.ds(seq_len, picked), pl.ds(0, FF)]
    query = r.table.at[pl.ds(seq_len, picked), pl.ds(FF, D)]
    x0_rows = r.table.at[pl.ds(seq_len, picked), pl.ds(FF + D, D)]
    half = FF // 2
    slopes = [r.table.at[pl.ds(s * picked, picked), pl.ds(4 * D, half)] for s in range(2)]
    count = [0]

    def load(*pairs):
        copies = []
        for src, dst in pairs:
            copies.append(pltpu.make_async_copy(src, dst, r.load_sem.at[count[0]]))
            copies[-1].start()
            count[0] += 1
        return copies

    def seq_pairs(src, dst):
        return [(src.at[pl.ds(s * seq_len, seq_len), :], dst(s)) for s in range(seqs)]

    def need(*groups):
        for copies in groups:
            for copy in copies:
                copy.wait()

    up_cols, low_cols = pl.ds(UP_AT, FF), pl.ds(0, UP_AT)
    got_trans = load((given.x2_low, r.x2_low), (given.d_trans, r.d_trans))
    got_feed = load(
        (given.d_two, r.stream), (given.x1_low, r.x1_low),
        *[(given.slope.at[:, pl.ds(s * half, half)], slopes[s]) for s in range(2)],
        (given.join.at[:, up_cols], r.join.at[:, up_cols]), (given.down, r.down),
    )
    got_hidden = load((given.hidden, hidden))
    got_out = load(
        (given.normal1, r.normal1), (given.att, r.att), (given.join.at[:, low_cols], r.join.at[:, low_cols])
    )
    got_att = load(
        *seq_pairs(given.values, values_at), *seq_pairs(given.keys, keys_at), (given.query, query)
    )
    got_first = load((given.x0_rows, x0_rows), (given.x0_low, r.x0_low), (given.normal0, r.normal0))
    got_head = load((given.d_logits, r.d_logits))

    place = Place(n_vocab)
    place.greet(n_dp)
    reduce = Reduce(
        place, r, wide // n_vocab, lands[:n_chunks], lands[n_chunks : 2 * n_chunks], lands[2 * n_chunks :]
    )
    r.g_vec[...] = given.g_vec[...]

    def gain(i):
        return given.vec[i : i + 1, :]

    def put(first, width, value):
        r.join[:, first : first + width] = value.astype(BF)

    need(got_trans)
    put(TRANS_AT, D, dot_left(r.x2_low[...], r.d_trans[...]))
    plan = iter(REDUCE_PLAN)
    reduce.go_on(next(plan))

    need(got_feed)
    d_ffn = r.stream[...].astype(BF)
    r.d_rows_low[...] = d_ffn
    r.g_vec[11:12, :] = column_sum(d_ffn.astype(F32))

    def feed(part):
        def step(j, carry):
            cols = aligned(j * D, D)
            up_at = aligned(UP_AT + part * half + j * D, D)
            d_act = dot_right(r.d_rows_low[...], r.down[aligned(part * half + j * D, D), :])
            d_hidden = (d_act * slopes[part][:, cols].astype(F32)).astype(BF)
            r.stream[...] += dot_right(d_hidden, r.join[:, up_at])
            r.join[:, up_at] = dot_left(r.x1_low[...], d_hidden).astype(BF)
            return carry

        lax.fori_loop(0, half // D, step, 0)

    feed(0)
    reduce.go_on(next(plan))
    feed(1)
    reduce.go_on(next(plan))
    need(got_hidden)

    def feed_down(first, width):
        def step(j, carry):
            rows = aligned(j * D, D)
            cols = slice(first, first + width)
            r.down[rows, cols] = dot_left(hidden[:, rows], r.d_rows_low[:, cols]).astype(BF)
            return carry

        lax.fori_loop(0, FF // D, step, 0)

    first = LATE + DOWN_PARTS[0][1]
    feed_down(0, first)
    reduce.go_on(next(plan))
    feed_down(first, D - first)
    reduce.go_on(next(plan))

    need(got_out)
    d_one = r.stream[...]
    normal1 = r.normal1[...]
    r.g_vec[2:3, :] = column_sum(d_one * normal1)
    r.g_vec[3:4, :] = column_sum(d_one)
    d_one = norm_rows_backward(d_one, normal1, given.inverse1[...], gain(2))
    r.stream[...] = d_one
    d_proj = d_one.astype(BF)
    r.g_vec[10:11, :] = column_sum(d_proj.astype(F32))
    r.x2_low[...] = dot_right(d_proj, r.join[:, OUT_AT : OUT_AT + D]).astype(BF)
    put(OUT_AT, D, dot_left(r.att[...], d_proj))
    got_latent = load((given.latent, r.att))
    reduce.go_on(next(plan))

    need(got_att)
    lane = lax.broadcasted_iota(jnp.int32, (slots, 128), 1)

    def attend(j, carry):
        lanes = aligned(j * 128, 128)
        for s in range(seqs):
            rows = slice(s * slots, (s + 1) * slots)
            q2 = query[rows, lanes]
            g2 = r.x2_low[rows, lanes]
            k2 = keys_at(s)[:, lanes]
            v2 = values_at(s)[:, lanes]
            d_q, d_k, d_v = [], None, None
            for a in range(2):
                mine = (lane >= HD) if a else (lane < HD)
                q1 = jnp.where(mine, q2, jnp.zeros_like(q2))
                g1 = jnp.where(mine, g2, jnp.zeros_like(g2))
                scores = dot_right(q1, k2) * HD ** (-0.5)
                expo = jnp.exp(scores - jnp.max(scores, axis=-1, keepdims=True))
                probs = expo * (1.0 / jnp.sum(expo, axis=-1, keepdims=True))
                d_probs = dot_right(g1, v2)
                delta = jnp.sum(d_probs * probs, axis=-1, keepdims=True)
                d_scores = (probs * (d_probs - delta)).astype(BF)
                d_q.append(rows_dot(d_scores, k2))
                more_k = dot_left(d_scores, q1)
                more_v = dot_left(probs.astype(BF), g1)
                d_k = more_k if d_k is None else d_k + more_k
                d_v = more_v if d_v is None else d_v + more_v
            r.d_trans[rows, lanes] = (jnp.where(lane < HD, d_q[0], d_q[1]) * HD ** (-0.5)).astype(BF)
            keys_at(s)[:, lanes] = (d_k * HD ** (-0.5)).astype(BF)
            values_at(s)[:, lanes] = d_v.astype(BF)
        return carry

    for pair in range(HEADS // 2):
        lax.fori_loop(pair, pair + 1, attend, 0)
        reduce.go_on(next(plan))

    need(got_first)
    d_query = r.d_trans[...]
    r.g_vec[8:9, :] = column_sum(d_query.astype(F32))
    d_rows = r.stream[...] + dot_right(d_query, r.join[:, :D])
    high = d_rows.astype(BF)
    r.d_rows_low[...] = high
    r.x1_low[...] = (d_rows - high.astype(F32)).astype(BF)
    put(0, D, dot_left(x0_rows[...], d_query))
    for i in (0, 1, 9, 13):
        r.g_vec[i : i + 1, :] = jnp.zeros((1, D), F32)

    reduce.go_on(next(plan))

    for s in range(seqs):

        def step(i, carry, s=s):
            inside = aligned(i * 256, 256)
            at = aligned(s * seq_len + i * 256, 256)
            d_v = values_at(s)[inside, :]
            r.g_vec[9:10, :] += column_sum(d_v.astype(F32))
            d_zero = dot_right(keys_at(s)[inside, :], r.join[:, D : 2 * D])
            d_zero = d_zero + dot_right(d_v, r.join[:, 2 * D : 3 * D])
            column = lax.broadcasted_iota(jnp.int32, (slots, 256), 1) + i * 256
            rows = slice(s * slots, (s + 1) * slots)
            pick = (given.spots[rows, :] == column).astype(BF)
            d_zero = d_zero + (dot_left(pick, r.d_rows_low[rows, :]) + dot_left(pick, r.x1_low[rows, :]))
            normal = r.normal0[at, :].astype(F32)
            r.g_vec[0:1, :] += column_sum(d_zero * normal)
            r.g_vec[1:2, :] += column_sum(d_zero)
            d_emb = norm_rows_backward(d_zero, normal, given.inverse0[at, :], gain(0)).astype(BF)
            r.g_vec[13:14, :] += column_sum(jnp.where(given.col_ids[at, :] < 0, d_emb.astype(F32), 0.0))
            r.normal0[at, :] = d_emb
            return carry

        for i in range(seq_len // 256):
            lax.fori_loop(i, i + 1, step, 0)
            reduce.go_on(next(plan))

    def weigh(i, carry):
        cols = aligned(i * 256, 256)
        for part, source in ((1, keys_at), (2, values_at)):
            value = sum(
                dot_left(r.x0_low[s * seq_len : (s + 1) * seq_len, :], source(s)[:, cols]) for s in range(seqs)
            )
            r.join[:, aligned(part * D + i * 256, 256)] = value.astype(BF)
        return carry

    lax.fori_loop(0, 2, weigh, 0)
    reduce.go_on(next(plan))
    lax.fori_loop(2, D // 256, weigh, 0)
    reduce.go_on(next(plan))
    columns = jnp.concatenate([r.g_vec[...], jnp.zeros((112, D), F32)], axis=0).T
    put(VEC_AT, 128, columns)
    put(VEC_AT + 128, 128, jnp.zeros((D, 128), F32))
    reduce.go_on(next(plan))

    need(got_head, got_latent)
    r.flipped[:, :tokens] = r.normal0[...].T
    r.flipped[:, tokens:] = r.att[...].T
    reduce.go_on(next(plan))
    width = wide // T_PARTS
    for j in range(T_PARTS):
        cols = slice(j * width, (j + 1) * width)
        column = lax.broadcasted_iota(jnp.int32, (tokens, width), 1) + j * width
        onehot = (given.col_ids[...] == column).astype(BF)
        value = rows_dot(r.flipped[:, :tokens], onehot) + rows_dot(r.flipped[:, tokens:], r.d_logits[:, cols])
        r.table[:, cols] = value.astype(BF)
        reduce.go_on(next(plan))
    reduce.go_on(next(plan))
    square = reduce.collect()
    row = lax.broadcasted_iota(jnp.int32, (8, 128), 0)
    summing = TileSum(place, n_dp, r)
    summing.begin(jnp.where(row == 0, square, given.loss[...]))
    summing.go_on()
    r.tile_out[...] = summing.total()
    reduce.sender.finish()


def backward(saved, loss, n_dp, n_vocab):
    rows = saved["join"].shape[0] // (n_dp * n_vocab)
    d_rows = saved["down"].shape[0] // (n_dp * n_vocab)
    t_rows = D // n_dp
    t_cols = saved["d_logits"].shape[1] // n_vocab
    tokens, picked = saved["col_ids"].shape[0], saved["spots"].shape[0]
    core_shapes, far_shapes = [], []
    for kind, j in REDUCE_ORDER:
        if kind == JOINED:
            shape = (rows * n_vocab, JOIN_PARTS[j][1])
        elif kind == DOWN:
            shape = (d_rows * n_vocab, DOWN_PARTS[j][1] if j >= 0 else LATE)
        else:
            shape = (t_rows, t_cols * n_vocab // T_PARTS)
        core_shapes.append((4,) + shape)
        far_shapes.append((d_rows, LATE) if (kind, j) == (DOWN, -1) else shape)
    inputs = dict(saved, loss=loss)
    inputs.pop("x0_rest", None)
    outs = dict(
        join_out=(2 * rows, JOIN // 2), down_out=(d_rows, D), table_out=(t_rows, t_cols), tile_out=(8, 128)
    )
    dma = pltpu.SemaphoreType.DMA
    rows_low = pltpu.VMEM((picked, D), BF)
    tokens_low = pltpu.VMEM((tokens, D), BF)
    scratch = dict(
        join=pltpu.VMEM(saved["join"].shape, BF),
        down=pltpu.VMEM(saved["down"].shape, BF),
        table=pltpu.VMEM((D, t_cols * n_vocab), BF),
        normal0=tokens_low,
        x0_low=tokens_low,
        att=rows_low,
        x1_low=rows_low,
        x2_low=rows_low,
        d_trans=rows_low,
        d_rows_low=rows_low,
        normal1=pltpu.VMEM((picked, D), F32),
        stream=pltpu.VMEM((picked, D), F32),
        d_logits=pltpu.VMEM(saved["d_logits"].shape, BF),
        g_vec=pltpu.VMEM((16, D), F32),
        flipped=pltpu.VMEM((D, tokens + picked), BF),
        packed=pltpu.VMEM((n_vocab, 2 * rows, JOIN // 2), BF),
        z_join=pltpu.VMEM((n_vocab - 1, 2 * rows, JOIN // 2), BF),
        z_down=pltpu.VMEM((n_vocab - 1, d_rows, D - LATE), BF),
        z_late=pltpu.VMEM((4, n_vocab - 1, d_rows, LATE), BF),
        z_table=pltpu.VMEM((n_vocab - 1, t_rows, t_cols), BF),
        load_sem=dma((len(saved) + 4,)),
        z_send=dma((Z_SLOTS, n_vocab - 1)),
        z_recv=dma((Z_SLOTS, n_vocab - 1)),
        l_send=dma((4, n_vocab - 1)),
        l_recv=dma((4, n_vocab - 1)),
        d_send=dma((N_CHUNKS, 7)),
        d_recv=dma((N_CHUNKS, 7)),
        **tile_scratch(n_dp, n_vocab),
    )
    lands = [pltpu.VMEM(shape, BF) for shape in core_shapes]
    lands += [pltpu.VMEM((2,) + shape, BF) for shape in far_shapes]
    lands += [pltpu.VMEM(shape, BF) for shape in far_shapes]
    vmem = pl.BlockSpec(memory_space=pltpu.VMEM)
    anywhere = pl.BlockSpec(memory_space=pl.ANY)
    near = set(dict(vec=0, g_vec=0, inverse0=0, inverse1=0, col_ids=0, spots=0, loss=0))
    return pl.pallas_call(
        functools.partial(backward_kernel, n_dp, n_vocab, tuple(inputs), tuple(outs) + tuple(scratch)),
        out_shape=tuple(jax.ShapeDtypeStruct(shape, F32) for shape in outs.values()),
        in_specs=[vmem if name in near else anywhere for name in inputs],
        out_specs=(vmem,) * len(outs),
        scratch_shapes=list(scratch.values()) + lands,
        compiler_params=pltpu.CompilerParams(
            collective_id=1, has_side_effects=True, vmem_limit_bytes=VMEM_LIMIT
        ),
    )(*inputs.values())


def update_kernel(n_state, *refs):
    tile, counts, g_join, g_down, g_table = refs[:5]
    states = refs[5 : 5 + 3 * n_state]
    outs = refs[5 + 3 * n_state : 5 + 7 * n_state]
    loss_out, present_out, norm_out = refs[5 + 7 * n_state :]
    norm = jnp.sqrt(tile[0:1, 0:1])
    factor = jnp.minimum(1.0, clip_limit / (norm + 1e-06))
    norm_out[0] = jnp.max(norm)
    loss_out[0] = jnp.max(tile[1:2, 0:1])
    present_out[0] = jnp.sum((counts[0:1, :] > 0.0).astype(F32))

    def advance(index, cols, gradient, rate):
        weight, first, second = (ref[:, cols] for ref in states[3 * index : 3 * index + 3])
        first, second, new = adamw(weight, first, second, gradient * factor, rate)
        targets = outs[4 * index : 4 * index + 4]
        targets[0][:, cols] = first
        targets[1][:, cols] = second
        targets[2][:, cols] = new
        targets[3][:, cols] = new.astype(targets[3].dtype)

    every = slice(None)
    block = states[0].shape[1]
    full = block // 128 * 128
    advance(0, slice(0, full), g_table[:, :full], matrix_rate)
    if full < block:
        advance(0, slice(full, block), g_table[:, full:block], matrix_rate)
    rows = g_join.shape[0] // 2
    for matrix, first, column, width in join_pieces():
        side, at = packed_at(column)
        if matrix == 1:
            square = jnp.concatenate([g_join[side * rows : (side + 1) * rows, at : at + 128], jnp.zeros((128 - rows, 128), F32)], axis=0)
            advance(2, every, square.T[:width, :rows], vector_rate)
        else:
            gradient = g_join[side * rows : (side + 1) * rows, at : at + width]
            advance(1 + matrix, slice(first, first + width), gradient, matrix_rate)
    advance(6, every, g_down[...], matrix_rate)


def update(tile, counts, g_join, g_down, g_table, states):
    vmem = pl.BlockSpec(memory_space=pltpu.VMEM)
    smem = pl.BlockSpec(memory_space=pltpu.SMEM)
    shapes = []
    for index, (weight, _, _) in enumerate(states):
        shapes += [jax.ShapeDtypeStruct(weight.shape, F32)] * 3
        shapes.append(jax.ShapeDtypeStruct(weight.shape, F32 if index == 2 else BF))
    flat = [array for state in states for array in state]
    scalars = [jax.ShapeDtypeStruct((1,), F32)] * 3
    return pl.pallas_call(
        functools.partial(update_kernel, len(states)),
        out_shape=tuple(shapes + scalars),
        in_specs=[vmem] * (5 + len(flat)),
        out_specs=(vmem,) * len(shapes) + (smem,) * 3,
        compiler_params=pltpu.CompilerParams(vmem_limit_bytes=VMEM_LIMIT),
    )(tile, counts, g_join, g_down, g_table, *flat)


def species_counts(picks, species, seq_len):
    live = (picks < seq_len).astype(F32)
    kinds = jnp.arange(NSPEC, dtype=jnp.int32)
    return jnp.sum((species[:, None] == kinds[None, :]).astype(F32) * jnp.sum(live, axis=1)[:, None], axis=0)


def local_step(tokens, picks, species, counts, join, down, table_t, col_id):
    seqs, seq_len = tokens.shape
    slots = picks.shape[1]
    w_qkv = join[:, : 3 * D]
    vec = join[:, VEC_AT : VEC_AT + NVEC].astype(F32)
    w_out = join[:, OUT_AT : OUT_AT + D]
    w_up = join[:, UP_AT : UP_AT + FF]
    w_trans = join[:, TRANS_AT : TRANS_AT + D]

    masked = jnp.any(picks[:, :, None] == jnp.arange(seq_len, dtype=jnp.int32)[None, None, :], axis=1)
    masked_flat = masked.reshape(-1)
    live = (picks < seq_len).reshape(-1)
    spot = jnp.minimum(picks, seq_len - 1)
    row_index = (spot + jnp.arange(seqs, dtype=jnp.int32)[:, None] * seq_len).reshape(-1)
    target = jnp.take_along_axis(tokens, spot, axis=1).reshape(-1)
    row_species = jnp.broadcast_to(species[:, None], picks.shape).reshape(-1)

    inputs = jnp.where(masked, -2, tokens).reshape(-1)
    onehot = (inputs[:, None] == col_id[None, :]).astype(BF)
    embedded = jnp.where(masked_flat[:, None], vec[:, 13], dot_right(onehot, table_t))
    stream_zero, normal0, inverse0 = norm_forward(embedded, vec[:, 0], vec[:, 1])
    x0_low = stream_zero.astype(BF)
    keys = dot_low(x0_low, w_qkv[:, D : 2 * D]).astype(BF)
    values = (dot_low(x0_low, w_qkv[:, 2 * D :]) + vec[:, 9]).astype(BF)
    x0_rows = stream_zero[row_index]
    x0_rows_low = x0_rows.astype(BF)
    query = (dot_low(x0_rows_low, w_qkv[:, :D]) + vec[:, 8]).astype(BF)
    q4 = query.reshape(seqs, slots, HEADS, HD)
    k4 = keys.reshape(seqs, seq_len, HEADS, HD)
    v4 = values.reshape(seqs, seq_len, HEADS, HD)
    scores = jnp.einsum("sqhd,skhd->shqk", q4, k4, preferred_element_type=F32) * HD ** (-0.5)
    probs = jax.nn.softmax(scores, axis=-1)
    probs_low = probs.astype(BF)
    att = jnp.einsum("shqk,skhd->sqhd", probs_low, v4, preferred_element_type=F32)
    att_low = att.reshape(-1, D).astype(BF)
    stream_one, normal1, inverse1 = norm_forward(
        x0_rows + dot_low(att_low, w_out) + vec[:, 10], vec[:, 2], vec[:, 3]
    )
    x1_low = stream_one.astype(BF)
    hidden = dot_low(x1_low, w_up)
    hidden_low = gelu(hidden).astype(BF)
    stream_two, normal2, inverse2 = norm_forward(
        stream_one + dot_low(hidden_low, down) + vec[:, 11], vec[:, 4], vec[:, 5]
    )
    picked_low = stream_two.astype(BF)
    trans = dot_low(picked_low, w_trans) + vec[:, 12]
    latent, normal3, inverse3 = norm_forward(gelu(trans), vec[:, 6], vec[:, 7])
    latent_low = latent.astype(BF)
    logits = dot_low(latent_low, table_t)
    logits = jnp.where(((col_id >= 0) & (col_id < VREAL))[None, :], logits, floor_value)
    top = jnp.max(logits, axis=-1, keepdims=True)
    expo = jnp.exp(logits - top)
    total = jnp.sum(expo, axis=-1, keepdims=True)
    is_target = col_id[None, :] == target[:, None]
    hit = jnp.sum(jnp.where(is_target, logits, 0.0), axis=-1)
    loss_rows = (top + jnp.log(total))[:, 0] - hit
    kinds = jnp.arange(NSPEC, dtype=jnp.int32)
    own = ((row_species[:, None] == kinds[None, :]) & live[:, None]).astype(F32)
    species_loss = jnp.sum(own * loss_rows[:, None], axis=0)
    present_mask = counts > 0
    present = jnp.sum(present_mask.astype(F32))
    inverse = jnp.where(present_mask, 1.0 / jnp.maximum(counts, 1.0), 0.0) / present
    weight = jnp.sum(own * inverse[None, :], axis=-1)
    loss_part = jnp.sum(jnp.where(present_mask, species_loss / jnp.maximum(counts, 1.0), 0.0))
    d_logits = (weight[:, None] * (expo / total - is_target.astype(F32))).astype(BF)

    d_latent = dot_right(d_logits, table_t)
    d_act, d6, d7 = norm_backward(d_latent, normal3, inverse3, vec[:, 6])
    d_trans = (d_act * gelu_slope(trans)).astype(BF)
    g_trans = dot_left(picked_low, d_trans)
    d12 = jnp.sum(d_trans.astype(F32), axis=0)
    d_two, d4, d5 = norm_backward(dot_right(d_trans, w_trans), normal2, inverse2, vec[:, 4])
    d_ffn = d_two.astype(BF)
    d11 = jnp.sum(d_ffn.astype(F32), axis=0)
    g_down = dot_left(hidden_low, d_ffn)
    d_hidden = (dot_right(d_ffn, down) * gelu_slope(hidden)).astype(BF)
    g_up = dot_left(x1_low, d_hidden)
    d_one, d2, d3 = norm_backward(d_two + dot_right(d_hidden, w_up), normal1, inverse1, vec[:, 2])
    d_proj = d_one.astype(BF)
    d10 = jnp.sum(d_proj.astype(F32), axis=0)
    g_out = dot_left(att_low, d_proj)
    d_att = dot_right(d_proj, w_out).astype(BF).reshape(seqs, slots, HEADS, HD)
    d_probs = jnp.einsum("sqhd,skhd->shqk", d_att, v4, preferred_element_type=F32)
    delta = jnp.sum(d_probs * probs, axis=-1, keepdims=True)
    d_scores = (probs * (d_probs - delta)).astype(BF)
    d_q = jnp.einsum("shqk,skhd->sqhd", d_scores, k4, preferred_element_type=F32) * HD ** (-0.5)
    d_k = jnp.einsum("shqk,sqhd->skhd", d_scores, q4, preferred_element_type=F32) * HD ** (-0.5)
    d_v = jnp.einsum("shqk,sqhd->skhd", probs_low, d_att, preferred_element_type=F32)
    d_q = d_q.reshape(-1, D).astype(BF)
    d_k = d_k.reshape(-1, D).astype(BF)
    d_v = d_v.reshape(-1, D).astype(BF)
    d8 = jnp.sum(d_q.astype(F32), axis=0)
    d9 = jnp.sum(d_v.astype(F32), axis=0)
    g_q = dot_left(x0_rows_low, d_q)
    g_k = dot_left(x0_low, d_k)
    g_v = dot_left(x0_low, d_v)
    d_rows = d_one + dot_right(d_q, w_qkv[:, :D])
    d_zero = dot_right(d_k, w_qkv[:, D : 2 * D]) + dot_right(d_v, w_qkv[:, 2 * D :])
    d_zero = d_zero.at[row_index].add(jnp.where(live[:, None], d_rows, 0.0))
    d_emb, d0, d1 = norm_backward(d_zero, normal0, inverse0, vec[:, 0])
    d_emb_low = d_emb.astype(BF)
    d13 = jnp.sum(jnp.where(masked_flat[:, None], d_emb_low.astype(F32), 0.0), axis=0)
    g_table = dot_left(latent_low, d_logits) + dot_left(d_emb_low, onehot)
    g_vec = jnp.stack([d0, d1, d2, d3, d4, d5, d6, d7, d8, d9, d10, d11, d12, d13], axis=1)
    g_vec = jnp.pad(g_vec, ((0, 0), (0, OUT_AT - VEC_AT - NVEC)))
    g_join = jnp.concatenate([g_q, g_k, g_v, g_vec, g_out, g_up, g_trans], axis=1)
    return loss_part, present, g_join.astype(BF), g_down.astype(BF), g_table.astype(BF)


def adamw(weight, first, second, gradient, rate):
    first = 0.5 * first + 0.5 * gradient
    second = 0.5 * second + 0.5 * gradient * gradient
    fix = 1.0 - 0.5**STEP
    step = first / fix / (jnp.sqrt(second / fix) + adam_eps)
    return (first, second, weight - rate * (step + decay_rate * weight))


def body(
    n_dp, n_vocab, tokens, picks, species,
    table, table_m, table_v, qkv_w, qkv_m, qkv_v, out_w, out_m, out_v, up_w, up_m, up_v,
    down_w, down_m, down_v, trans_w, trans_m, trans_v, vectors, vectors_m, vectors_v,
):
    block, columns = table.shape
    wide = padded(block)
    rows = qkv_w.shape[0]
    seqs, seq_len = tokens.shape
    both = ("dp", "vocab")
    own_kernels = n_dp == 8 and n_vocab * rows % 16 == 0 and rows % 8 == 0 and columns % 16 == 0 and seqs == 2
    own_kernels = own_kernels and part_cols(wide) * T_PARTS == wide
    if own_kernels:
        column = np.arange(wide * n_vocab)
        token = np.array(token_of(column, block, n_vocab, wide, np))
        col_floor = np.where((token >= 0) & (token < VREAL), 0.0, floor_value).astype(np.float32)[None, :]
        inputs = dict(
            table_in=table.T, down_w=down_w, qkv_w=qkv_w, vectors=vectors.T, out_w=out_w, up_w=up_w, trans_w=trans_w,
            tokens=tokens, picks=picks, species=species, col_floor=jnp.asarray(col_floor),
        )
        saved, counts, loss = forward(inputs, n_dp, n_vocab)
        g_join, g_down, g_table, tile = backward(saved, loss, n_dp, n_vocab)
        states = (
            (table.T, table_m.T, table_v.T), (qkv_w, qkv_m, qkv_v), (vectors.T, vectors_m.T, vectors_v.T),
            (out_w, out_m, out_v), (up_w, up_m, up_v), (trans_w, trans_m, trans_v), (down_w, down_m, down_v),
        )
        new = list(update(tile, counts, g_join, g_down, g_table, states))
        for index in (0, 2):
            new[4 * index : 4 * index + 4] = [array.T for array in new[4 * index : 4 * index + 4]]
        order = (0, 1, 3, 4, 6, 5)
        outs = [new[4 * index + part] for index in order for part in range(4)] + new[8:11]
        return tuple(outs) + tuple(array.reshape(()) for array in new[28:])
    col_token = token_of(jnp.arange(wide * n_vocab, dtype=jnp.int32), block, n_vocab, wide, jnp)
    joined = jnp.concatenate(
        [qkv_w, jnp.pad(vectors, ((0, 0), (0, OUT_AT - VEC_AT - NVEC))), out_w, up_w, trans_w], axis=1
    ).astype(BF)
    down_low = down_w.astype(BF)
    table_t = jnp.pad(table.T.astype(BF), ((0, 0), (0, wide - block)))
    counts = species_counts(picks, species, seq_len)
    piece = part_cols(wide)
    parts = wide // piece
    join_all = lax.all_gather(joined, both, axis=0, tiled=True)
    down_all = lax.all_gather(down_low, both, axis=0, tiled=True)
    table_all = lax.all_gather(table_t, "dp", axis=0, tiled=True).reshape(D, parts, 1, piece)
    table_all = lax.all_gather(table_all, "vocab", axis=2, tiled=True).reshape(D, wide * n_vocab)
    counts = lax.psum(counts, both)
    loss, present, g_join, g_down, g_table = local_step(
        tokens, picks, species, counts, join_all, down_all, table_all, col_token
    )
    g_join = lax.psum_scatter(g_join.astype(F32), both, scatter_dimension=0, tiled=True)
    g_down = lax.psum_scatter(g_down.astype(F32), both, scatter_dimension=0, tiled=True)
    g_table = lax.psum_scatter(g_table, "dp", scatter_dimension=0, tiled=True)
    g_table = g_table.reshape(columns, parts, n_vocab, piece)
    g_table = lax.psum_scatter(g_table, "vocab", scatter_dimension=2, tiled=True)
    g_table = g_table.reshape(columns, wide).astype(F32)
    square = jnp.sum(g_join * g_join) + jnp.sum(g_down * g_down) + jnp.sum(g_table * g_table)
    square, loss_sum = lax.psum((square, loss), both)
    grad_norm = jnp.sqrt(square)
    factor = jnp.minimum(1.0, clip_limit / (grad_norm + 1e-06))
    grads = (
        g_table[:, :block].T, g_join[:, : 3 * D], g_join[:, OUT_AT : OUT_AT + D], g_join[:, UP_AT : UP_AT + FF],
        g_down, g_join[:, TRANS_AT:], g_join[:, VEC_AT : VEC_AT + NVEC],
    )
    masters = (table, qkv_w, out_w, up_w, down_w, trans_w, vectors)
    firsts = (table_m, qkv_m, out_m, up_m, down_m, trans_m, vectors_m)
    seconds = (table_v, qkv_v, out_v, up_v, down_v, trans_v, vectors_v)
    outs = []
    for index in range(7):
        rate = vector_rate if index == 6 else matrix_rate
        first, second, new = adamw(masters[index], firsts[index], seconds[index], grads[index] * factor, rate)
        outs.extend([first, second, new])
        if index < 6:
            outs.append(new.astype(BF))
    return tuple(outs) + (loss_sum, present, grad_norm)


def solution(mesh):
    both = P(("dp", "vocab"), None)
    split = P("vocab", "dp")
    in_specs = (both, both, P(("dp", "vocab"))) + (split,) * 3 + (both,) * 18
    out_specs = (split,) * 4 + (both,) * 23 + (P(),) * 3
    step = functools.partial(body, mesh.shape["dp"], mesh.shape["vocab"])
    return jax.shard_map(step, mesh=mesh, in_specs=in_specs, out_specs=out_specs, check_vma=False)
```

```python
import functools

import jax
import jax.numpy as jnp
import numpy as np
from jax import lax
from jax.experimental import pallas as pl
from jax.experimental.pallas import tpu as pltpu
from jax.sharding import PartitionSpec as P

D = 768
HEADS = 12
HD = 64
FF = 3072
NSPEC = 8
NVEC = 14
STEP = 10
VREAL = 4101
MESH = pl.DeviceIdType.MESH
BF = jnp.bfloat16
F32 = jnp.float32

norm_eps = 1e-05
clip_limit = 0.01
matrix_rate = 0.06
vector_rate = 0.5
decay_rate = 0.01
adam_eps = 1e-08
floor_value = -1e30

VEC_AT = 3 * D
OUT_AT = VEC_AT + 256
UP_AT = OUT_AT + D
TRANS_AT = UP_AT + FF
JOIN = TRANS_AT + D
JOIN_PARTS = (
    (0, 1280),
    (1280, 1280),
    (OUT_AT, 768),
    (UP_AT, 1536),
    (UP_AT + 1536, 1536),
    (TRANS_AT, 768),
)
VMEM_LIMIT = 63 * 2**20


T_PARTS = 9
LATE = 256
DOWN_PARTS = ((LATE, 256), (LATE + 256, D - LATE - 256))
R_LATE = 128
R_DOWN_PARTS = ((R_LATE, 256), (R_LATE + 256, D - R_LATE - 256))
GATHER_X = "yxxxxyyyxxyyxyxyxx"
REDUCE_X = "xxyyyxxyxxyyxxyxxy"
CORE, X, Y = range(3)


def padded(rows):
    return -(-rows // 128) * 128


def part_cols(wide):
    return wide // T_PARTS if wide % (128 * T_PARTS) == 0 else wide


def token_of(column, block, n_vocab, wide, xp):
    piece = part_cols(wide)
    inside = column % (piece * n_vocab)
    row = column // (piece * n_vocab) * piece + inside % piece
    return xp.where(row < block, inside // piece * block + row, -1)


class Place:
    def __init__(self, n_vocab):
        dp = lax.axis_index("dp")
        z = lax.axis_index("vocab")
        core = lax.rem(dp, 2)
        bit_x = lax.rem(lax.div(dp, 2), 2)
        bit_y = lax.div(dp, 4)
        self.dp, self.z, self.core, self.n_vocab = dp, z, core, n_vocab
        self.step_core = 1 - 2 * core
        self.step_x = 2 - 4 * bit_x
        self.step_y = 4 - 8 * bit_y

    def across(self, which):
        return self.dp + (self.step_core, self.step_x, self.step_y)[which]

    def device(self, which):
        return (self.across(which), self.z)

    def along(self, k):
        return lax.rem(self.z + k, self.n_vocab)

    def greet(self, n_dp):
        self.hail(n_dp)
        self.hear(n_dp)

    def hail(self, n_dp):
        barrier = pltpu.get_barrier_semaphore()
        for k in range(1, n_dp):
            other = lax.rem(self.dp + k, n_dp)
            pl.semaphore_signal(barrier, inc=1, device_id=(other, self.z), device_id_type=MESH)
        for k in range(1, self.n_vocab):
            pl.semaphore_signal(barrier, inc=1, device_id=(self.dp, self.along(k)), device_id_type=MESH)

    def hear(self, n_dp):
        pl.semaphore_wait(pltpu.get_barrier_semaphore(), n_dp + self.n_vocab - 2)


def remote(src, dst, send, recv, device):
    return pltpu.make_async_remote_copy(
        src_ref=src, dst_ref=dst, send_sem=send, recv_sem=recv, device_id=device, device_id_type=MESH
    )


def block_view(ref, stride, offset, rows, first, width):
    def view(index):
        return ref.at[pl.ds(pl.multiple_of(index * stride + offset, 16), rows), pl.ds(first, width)]

    return view


class TileSum:
    def __init__(self, place, n_dp, r):
        self.place, self.n_dp, self.r = place, n_dp, r

    def z_copies(self):
        place, r = self.place, self.r
        return [
            remote(
                r.tiles.at[0], r.tile_ring.at[place.z], r.tile_send.at[k - 1], r.tile_recv.at[k - 1],
                (place.dp, place.along(k)),
            )
            for k in range(1, place.n_vocab)
        ]

    def dp_copies(self):
        place, r, base = self.place, self.r, self.place.n_vocab - 1
        return [
            remote(
                r.tiles.at[1], r.tile_land.at[place.dp], r.tile_send.at[base + k - 1],
                r.tile_recv.at[base + k - 1], (lax.rem(place.dp + k, self.n_dp), place.z),
            )
            for k in range(1, self.n_dp)
        ]

    def begin(self, value):
        self.r.tiles[0] = value
        self.r.tile_ring[self.place.z] = value
        for copy in self.z_copies():
            copy.start()

    def go_on(self):
        for copy in self.z_copies():
            copy.wait()
        value = self.r.tile_ring[0]
        for k in range(1, self.place.n_vocab):
            value = value + self.r.tile_ring[k]
        self.r.tiles[1] = value
        self.r.tile_land[self.place.dp] = value
        for copy in self.dp_copies():
            copy.start()

    def total(self):
        for copy in self.dp_copies():
            copy.wait()
        value = self.r.tile_land[0]
        for k in range(1, self.n_dp):
            value = value + self.r.tile_land[k]
        return value


class Sender:
    def __init__(self):
        self.started = []

    def go(self, copy):
        copy.start()
        self.started.append(copy)

    def finish(self):
        for copy in self.started:
            copy.wait_send()


def dot_low(left, right):
    return jnp.dot(left, right, preferred_element_type=F32)


def dot_left(left, right):
    return lax.dot_general(left, right, (((0,), (0,)), ((), ())), preferred_element_type=F32)


def dot_right(left, right):
    return lax.dot_general(left, right, (((1,), (1,)), ((), ())), preferred_element_type=F32)


def norm_forward(value, gain, shift):
    mean = jnp.mean(value, axis=-1, keepdims=True)
    centered = value - mean
    inverse = lax.rsqrt(jnp.mean(centered * centered, axis=-1, keepdims=True) + norm_eps)
    normal = centered * inverse
    return normal * gain + shift, normal, inverse


def norm_backward(gradient, normal, inverse, gain):
    gain_gradient = jnp.sum(gradient * normal, axis=0)
    shift_gradient = jnp.sum(gradient, axis=0)
    scaled = gradient * gain
    inner = jnp.mean(scaled, axis=-1, keepdims=True) + normal * jnp.mean(
        scaled * normal, axis=-1, keepdims=True
    )
    return inverse * (scaled - inner), gain_gradient, shift_gradient


def gelu(value):
    return 0.5 * value * (1.0 + lax.erf(value * 0.7071067811865476))


def gelu_slope(value):
    cdf = 0.5 * (1.0 + lax.erf(value * 0.7071067811865476))
    return cdf + value * jnp.exp(-0.5 * value * value) * 0.3989422804014327


def rows_dot(left, right):
    return jnp.dot(left, right, preferred_element_type=F32)


def norm_rows(value):
    mean = jnp.mean(value, axis=-1, keepdims=True)
    centered = value - mean
    inverse = lax.rsqrt(jnp.mean(centered * centered, axis=-1, keepdims=True) + norm_eps)
    return centered * inverse, inverse


def norm_rows_backward(gradient, normal, inverse, gain):
    scaled = gradient * gain
    inner = jnp.mean(scaled, axis=-1, keepdims=True) + normal * jnp.mean(
        scaled * normal, axis=-1, keepdims=True
    )
    return inverse * (scaled - inner)


def column_sum(value):
    return jnp.sum(value, axis=0, keepdims=True)


def gelu_both(value):
    cdf = 0.5 * (1.0 + lax.erf(value * 0.7071067811865476))
    slope = cdf + value * jnp.exp(-0.5 * value * value) * 0.3989422804014327
    return value * cdf, slope


def aligned(start, size, to=128):
    return pl.ds(pl.multiple_of(start, to), size)


class Refs:
    def __init__(self, names, refs):
        for name, ref in zip(names, refs, strict=True):
            setattr(self, name, ref)


def join_pieces():
    spans = ((0, 3 * D), (VEC_AT, NVEC), (OUT_AT, D), (UP_AT, FF), (TRANS_AT, D))
    pieces = []
    for first, width in JOIN_PARTS:
        for low in (first, first + width // 2):
            high = low + width // 2
            for matrix, (start, size) in enumerate(spans):
                a, b = max(low, start), min(high, start + size)
                if a < b:
                    pieces.append((matrix, a - start, a, b - a))
    return pieces


def packed_at(column):
    for first, width in JOIN_PARTS:
        half = width // 2
        if first <= column < first + width:
            side, inside = divmod(column - first, half)
            return side, first // 2 + inside
    raise ValueError


class Gather:
    def __init__(self, place, r):
        self.place, self.r, self.sender = place, r, Sender()
        n_vocab = place.n_vocab
        self.t_rows, self.t_cols = r.table_t.shape
        self.rows = r.packed.shape[0] // 2
        self.d_rows = r.down_low.shape[0]
        piece = self.t_cols // T_PARTS
        rows = self.rows
        self.chunks = []
        self.z_moves = []
        for q in range(T_PARTS):
            first = piece * n_vocab * q
            where = (
                aligned(place.dp * self.t_rows, self.t_rows, 16),
                aligned(first + place.z * piece, piece),
            )
            view = block_view(r.table, self.t_rows, 0, self.t_rows, first, n_vocab * piece)
            self.chunks.append((view, None))
            self.z_moves.append((r.table_t.at[:, pl.ds(piece * q, piece)], r.table.at[where]))
        for part in JOIN_PARTS[:-1]:
            self.add_part(*part)
        d_rows = self.d_rows
        for first, width in DOWN_PARTS:
            dst = r.down.at[aligned((place.dp * n_vocab + place.z) * d_rows, d_rows, 16), pl.ds(first, width)]
            view = block_view(r.down, d_rows * n_vocab, 0, d_rows * n_vocab, first, width)
            self.chunks.append((view, None))
            self.z_moves.append((r.down_low.at[:, pl.ds(first, width)], dst))
        self.add_part(*JOIN_PARTS[-1])
        self.late = len(self.chunks)

    def add_part(self, first, width):
        place, r, rows = self.place, self.r, self.rows
        cols = pl.ds(first // 2, width // 2)
        view = block_view(r.join, rows * place.n_vocab, 0, rows * place.n_vocab, first, width)
        assemble = functools.partial(self.assemble, first, width)
        self.chunks.append((view, assemble))
        self.z_moves.append((r.packed.at[:, cols], r.stage.at[place.z, :, cols]))

    def place_own(self):
        for src, dst in self.z_moves[:T_PARTS]:
            dst[...] = src[...]

    def place_packed(self):
        self.r.stage[self.place.z] = self.r.packed[...]

    def place_down(self):
        place, r, d_rows = self.place, self.r, self.d_rows
        r.down[aligned((place.dp * place.n_vocab + place.z) * d_rows, d_rows, 16), :] = r.down_low[...]

    def z_copies(self, slot):
        place, r = self.place, self.r
        src, dst = self.z_moves[slot]
        return [
            remote(src, dst, r.z_send.at[slot, k - 1], r.z_recv.at[slot, k - 1], (place.dp, place.along(k)))
            for k in range(1, place.n_vocab)
        ]

    def along_z(self, *slots):
        for slot in slots:
            for copy in self.z_copies(slot):
                self.sender.go(copy)

    def assemble(self, first, width):
        place, r, rows = self.place, self.r, self.rows
        half = width // 2
        at = first // 2
        lefts, rights = [], []
        for k in range(place.n_vocab):
            piece = r.stage[k, :, at : at + half].astype(F32)
            lefts.append(piece[:rows])
            rights.append(piece[rows:])
        where = aligned(place.dp * rows * place.n_vocab, rows * place.n_vocab, 16)
        r.join[where, first : first + half] = jnp.concatenate(lefts, axis=0).astype(BF)
        r.join[where, first + half : first + width] = jnp.concatenate(rights, axis=0).astype(BF)

    def move(self, i, k, arriving):
        place, r = self.place, self.r
        if i == self.late:
            d_rows = self.d_rows
            if k < 3:
                view = block_view(
                    r.down, d_rows * place.n_vocab, place.z * d_rows, d_rows, 0, LATE
                )
            else:
                view = block_view(r.down, d_rows * place.n_vocab, 0, d_rows * place.n_vocab, 0, LATE)
        else:
            view = self.chunks[i][0]
        one, two = self.directions(i)
        own, a, b = place.dp, place.across(one), place.across(two)
        ab = a + b - own
        if k < 3:
            block = (a, b, ab)[k] if arriving else (own, own, a)[k]
            which = (one, two, two)[k]
        else:
            block = (own, a, b, ab)[k - 3] + (place.step_core if arriving else 0)
            which = CORE
        return remote(view(block), view(block), r.d_send.at[i, k], r.d_recv.at[i, k], place.device(which))

    def directions(self, i):
        return (X, Y) if GATHER_X[i] == "x" else (Y, X)

    def send(self, i, *which):
        for k in which:
            self.sender.go(self.move(i, k, False))

    def arrive(self, i, *which):
        for k in which:
            self.move(i, k, True).wait_recv()

    def late_copies(self, arriving):
        place, r, d_rows = self.place, self.r, self.d_rows
        one, two = self.directions(self.late)
        a, b = place.across(one), place.across(two)
        copies = []
        for j, block in enumerate((place.dp, a, b, a + b - place.dp)):
            for k in range(1, place.n_vocab):
                z = place.along(place.n_vocab - k) if arriving else place.z
                at = r.down.at[aligned((block * place.n_vocab + z) * d_rows, d_rows, 16), pl.ds(0, LATE)]
                copies.append(
                    remote(at, at, r.l_send.at[j, k - 1], r.l_recv.at[j, k - 1], (place.dp, place.along(k)))
                )
        return copies

    def after_z(self, i):
        for copy in self.z_copies(i):
            copy.wait_recv()
        if self.chunks[i][1] is not None:
            self.chunks[i][1]()
        self.send(i, 0, 1, 3)

    def after_one(self, i):
        self.arrive(i, 0)
        self.send(i, 2)
        if i != self.late:
            self.send(i, 4)

    def after_two(self, i):
        self.arrive(i, 1)
        if i != self.late:
            self.send(i, 5)

    def after_both(self, i):
        self.arrive(i, 2)
        if i != self.late:
            self.send(i, 6)
        else:
            for copy in self.late_copies(False):
                self.sender.go(copy)
            self.along_z(*range(Z_TAIL, Z_SLOTS))

    def after_late(self, i):
        for copy in self.late_copies(True):
            copy.wait_recv()
        self.send(i, 3, 4, 5, 6)

    def go_on(self, steps):
        for kind, i in steps:
            (self.after_z, self.after_one, self.after_two, self.after_both, self.after_late)[kind](i)

    def need(self, *which):
        for i in which:
            self.arrive(i, 3, 4, 5, 6)


N_CHUNKS = T_PARTS + len(JOIN_PARTS) + len(DOWN_PARTS) + 1
Z_SLOTS = N_CHUNKS - 1
GATHER_PLAN = (
    (
        (2, 17), (1, 17), (0, 0), (0, 1), (1, 0), (0, 2), (0, 3), (0, 4), (2, 0), (3, 17), (1, 1), (0, 5),
        (1, 2), (0, 6), (0, 7), (1, 3), (0, 8), (2, 1), (2, 2), (2, 3), (2, 4), (1, 4), (3, 0), (3, 1), (1, 5),
        (0, 9), (2, 5), (2, 6), (3, 2), (2, 7), (1, 6),
    ),
    (
        (1, 8), (1, 7), (0, 10), (0, 11), (3, 5), (2, 8), (3, 3), (3, 4), (1, 9),
    ),
    (
        (0, 12), (3, 6), (3, 7), (2, 9), (3, 8),
    ),
    (
        (2, 10), (1, 10), (2, 11), (1, 11), (4, 17), (1, 12), (3, 9), (3, 10), (0, 13), (2, 12),
    ),
    (
        (0, 14), (3, 11),
    ),
    (
        (0, 15), (2, 13), (3, 12),
    ),
    (
        (1, 14), (1, 13), (0, 16),
    ),
    (
        (2, 15), (2, 14),
    ),
    (
        (1, 15),
    ),
    (
        (3, 13),
    ),
    (
        (3, 14), (1, 16),
    ),
    (
        (2, 16), (3, 15), (3, 16),
    ),
    (),
    (),
)
Z_TAIL = T_PARTS + 4


N_FORWARD_IN = 11


def saved_shapes(rows, d_rows, tokens, picked, t_cols_all):
    return dict(
        join=((rows, JOIN), BF),
        down=((d_rows, D), BF),
        normal0=((tokens, D), BF),
        inverse0=((tokens, 1), F32),
        x0_low=((tokens, D), BF),
        keys=((tokens, D), BF),
        values=((tokens, D), BF),
        query=((picked, D), BF),
        x0_rows=((picked, D), BF),
        att=((picked, D), BF),
        normal1=((picked, D), F32),
        inverse1=((picked, 1), F32),
        x1_low=((picked, D), BF),
        hidden=((picked, FF), BF),
        slope=((picked, FF), BF),
        x2_low=((picked, D), BF),
        d_trans=((picked, D), BF),
        d_two=((picked, D), F32),
        d_logits=((picked, t_cols_all), BF),
        latent=((picked, D), BF),
        g_vec=((16, D), F32),
        vec=((16, D), F32),
        col_ids=((tokens, 1), jnp.int32),
        spots=((picked, 1), jnp.int32),
    )


def tile_scratch(n_dp, n_vocab):
    dma = pltpu.SemaphoreType.DMA
    return dict(
        tiles=pltpu.VMEM((2, 8, 128), F32),
        tile_land=pltpu.VMEM((n_dp, 8, 128), F32),
        tile_ring=pltpu.VMEM((n_vocab, 8, 128), F32),
        tile_send=dma((n_dp + n_vocab - 2,)),
        tile_recv=dma((n_dp + n_vocab - 2,)),
    )


def whole_part(value, by):
    return jnp.floor((value + 0.5) * (1.0 / by))


def forward_kernel(n_dp, n_vocab, names, out_names, *refs):
    r = Refs(names, refs[:N_FORWARD_IN] + refs[N_FORWARD_IN + len(out_names) + 2 :])
    out = Refs(out_names, refs[N_FORWARD_IN : N_FORWARD_IN + len(out_names)])
    counts_out, loss_out = refs[N_FORWARD_IN + len(out_names) : N_FORWARD_IN + len(out_names) + 2]
    seqs, seq_len = r.tokens.shape
    tokens = seqs * seq_len
    picked = r.spots.shape[0]
    slots = picked // seqs
    block = r.table_in.shape[1]
    place = Place(n_vocab)

    def prepare_table():
        full = block // 128 * 128
        r.table_t[:, :full] = r.table_in[:, :full].astype(BF)
        if full < r.table_t.shape[1]:
            r.table_rest[...] = jnp.zeros_like(r.table_rest)
            r.table_rest[:, : block - full] = r.table_in[:, full:]
            r.table_t[:, full:] = r.table_rest[...].astype(BF)

    def prepare_packed():
        r.vec_rest[...] = jnp.zeros_like(r.vec_rest)
        rows = r.packed.shape[0] // 2
        r.vec_rows[...] = jnp.zeros_like(r.vec_rows)
        r.vec_rows[:NVEC, :rows] = r.vectors[...]
        r.vec_rest[:, :16] = r.vec_rows[...].T[:rows, :]
        sources = (r.qkv_w, r.vec_rest, r.out_w, r.up_w, r.trans_w)
        spans = ((0, 3 * D), (VEC_AT, OUT_AT - VEC_AT), (OUT_AT, D), (UP_AT, FF), (TRANS_AT, D))

        def read(low, high):
            found = []
            for source, (start, size) in zip(sources, spans, strict=True):
                a, b = max(low, start), min(high, start + size)
                if a < b:
                    found.append(source[:, a - start : b - start])
            return found[0] if len(found) == 1 else jnp.concatenate(found, axis=1)

        for first, width in JOIN_PARTS:
            half = width // 2
            both = jnp.concatenate([read(first, first + half), read(first + half, first + width)], axis=0)
            r.packed[:, first // 2 : first // 2 + half] = both.astype(BF)

    def prepare_ids():
        piece = part_cols(r.table_t.shape[1])
        token = r.tokens[...].astype(F32)
        owner = whole_part(token, block)
        row = token - owner * block
        part = whole_part(row, piece)
        column = part * (piece * n_vocab) + owner * piece + (row - part * piece)
        r.wide_rows[...] = jnp.full(r.wide_rows.shape, float(seq_len), F32)
        r.wide_rows[:seqs, : r.picks.shape[1]] = r.picks[...].astype(F32)
        spots = r.wide_rows[...].T
        lane = lax.broadcasted_iota(jnp.int32, (slots, 128), 1)
        masked_columns = []
        for s in range(seqs):
            rows = slice(s * slots, (s + 1) * slots)
            spot = spots[:slots, s : s + 1]
            position = lax.broadcasted_iota(jnp.int32, (slots, seq_len), 1).astype(F32)
            here = spot == position
            r.targets[rows, :] = jnp.sum(
                jnp.where(here, column[s : s + 1, :], 0.0), axis=-1, keepdims=True
            ).astype(jnp.int32)
            live = spot < float(seq_len)
            r.spots[rows, :] = jnp.where(live, spot, -1.0).astype(jnp.int32)
            kind = r.species[s] == lane
            r.own_kinds[rows, :] = jnp.where(kind & live, 1.0, 0.0)
            masked = jnp.max(jnp.where(here, 1.0, 0.0), axis=0, keepdims=True)
            masked_columns.append(jnp.where(masked > 0.0, -1.0, column[s : s + 1, :]))
        masked_columns.append(jnp.zeros((8 - seqs, seq_len), F32))
        turned = jnp.concatenate(masked_columns, axis=0).T
        for s in range(seqs):
            r.col_ids[s * seq_len : (s + 1) * seq_len, :] = turned[:, s : s + 1].astype(jnp.int32)

    saves = []

    def save(src, dst, *cols):
        if cols:
            src, dst = src.at[:, pl.ds(*cols)], dst.at[:, pl.ds(*cols)]
        copy = pltpu.make_async_copy(src, dst, r.save_sem.at[len(saves)])
        copy.start()
        saves.append(copy)

    def embed(q):
        width = r.table.shape[1] // 3
        first = q * width

        def step(i, carry):
            at = aligned(i * 256, 256)
            ids = r.col_ids[at, :]
            onehot = (ids == lax.broadcasted_iota(jnp.int32, (256, width), 1) + first).astype(BF)
            part = dot_right(onehot, r.table[:, first : first + width])
            r.embedded[at, :] = part if q == 0 else part + r.embedded[at, :]
            return carry

        lax.fori_loop(0, tokens // 256, step, 0)

    def first_norm():
        columns = r.join[:, VEC_AT : VEC_AT + 128].astype(F32).T
        r.vec[...] = columns[:16]

        def step(i, carry):
            at = aligned(i * 128, 128)
            value = jnp.where(r.col_ids[at, :] < 0, r.vec[13:14, :], r.embedded[at, :])
            normal, inverse = norm_rows(value)
            stream = normal * r.vec[0:1, :] + r.vec[1:2, :]
            high = stream.astype(BF)
            r.normal0[at, :] = normal.astype(BF)
            r.inverse0[at, :] = inverse
            r.x0_low[at, :] = high
            r.x0_rest[at, :] = (stream - high.astype(F32)).astype(BF)
            return carry

        lax.fori_loop(0, tokens // 128, step, 0)

    def project():
        def step(i, carry):
            at = aligned(i * 256, 256)
            low = r.x0_low[at, :]
            r.keys[at, :] = rows_dot(low, r.join[:, D : 2 * D]).astype(BF)
            r.values[at, :] = (rows_dot(low, r.join[:, 2 * D : 3 * D]) + r.vec[9:10, :]).astype(BF)
            return carry

        lax.fori_loop(0, tokens // 256, step, 0)
        for s in range(seqs):
            rows = slice(s * slots, (s + 1) * slots)
            seq = slice(s * seq_len, (s + 1) * seq_len)
            pick = (r.spots[rows, :] == lax.broadcasted_iota(jnp.int32, (slots, seq_len), 1)).astype(BF)
            high = rows_dot(pick, r.x0_low[seq, :])
            r.stream[rows, :] = high + rows_dot(pick, r.x0_rest[seq, :])
            r.x0_rows[rows, :] = high.astype(BF)
        r.query[...] = (rows_dot(r.x0_rows[...], r.join[:, :D]) + r.vec[8:9, :]).astype(BF)

    def attend(low, high):
        lane = lax.broadcasted_iota(jnp.int32, (slots, 128), 1)

        def step(j, carry):
            lanes = aligned(j * 128, 128)
            for s in range(seqs):
                rows = slice(s * slots, (s + 1) * slots)
                seq = slice(s * seq_len, (s + 1) * seq_len)
                q2 = r.query[rows, lanes]
                k2 = r.keys[seq, lanes]
                v2 = r.values[seq, lanes]
                parts = []
                for a in range(2):
                    mine = (lane >= HD) if a else (lane < HD)
                    scores = dot_right(jnp.where(mine, q2, jnp.zeros_like(q2)), k2) * HD ** (-0.5)
                    top = jnp.max(scores, axis=-1, keepdims=True)
                    expo = jnp.exp(scores - top)
                    total = jnp.sum(expo, axis=-1, keepdims=True)
                    parts.append(rows_dot((expo * (1.0 / total)).astype(BF), v2))
                r.att[rows, lanes] = jnp.where(lane < HD, parts[0], parts[1]).astype(BF)
            return carry

        lax.fori_loop(low, high, step, 0)

    def after_attention():
        value = r.stream[...] + (rows_dot(r.att[...], r.join[:, OUT_AT : OUT_AT + D]) + r.vec[10:11, :])
        normal, inverse = norm_rows(value)
        r.normal1[...] = normal
        r.inverse1[...] = inverse
        stream = normal * r.vec[2:3, :] + r.vec[3:4, :]
        r.stream[...] = stream
        r.x1_low[...] = stream.astype(BF)

    def feed_up(first):
        def step(j, carry):
            cols = aligned(j * 512, 512)
            act, slope = gelu_both(rows_dot(r.x1_low[...], r.join[:, aligned(UP_AT + j * 512, 512)]))
            r.hidden[:, cols] = act.astype(BF)
            r.slope[:, cols] = slope.astype(BF)
            return carry

        lax.fori_loop(3 * first, 3 * first + 3, step, 0)

    def feed_down():
        value = r.stream[...] + (rows_dot(r.hidden[...], r.down[...]) + r.vec[11:12, :])
        normal, inverse = norm_rows(value)
        r.normal2[...] = normal
        r.inverse2[...] = inverse
        r.x2_low[...] = (normal * r.vec[4:5, :] + r.vec[5:6, :]).astype(BF)

    def head(counts):
        act, slope3 = gelu_both(
            rows_dot(r.x2_low[...], r.join[:, TRANS_AT : TRANS_AT + D]) + r.vec[12:13, :]
        )
        normal3, inverse3 = norm_rows(act)
        r.stream[...] = normal3
        latent = (normal3 * r.vec[6:7, :] + r.vec[7:8, :]).astype(BF)
        r.latent[...] = latent
        steps = 6
        width = r.table.shape[1] // steps

        top = jnp.full((picked, 1), floor_value, F32)
        total = jnp.zeros((picked, 1), F32)
        hit = jnp.zeros((picked, 1), F32)
        for i in range(steps):
            cols = slice(i * width, (i + 1) * width)
            logits = rows_dot(latent, r.table[:, cols])
            logits = jnp.where(r.col_floor[:, cols] == 0.0, logits, floor_value)
            r.logits[:, cols] = logits
            column = lax.broadcasted_iota(jnp.int32, (picked, width), 1) + i * width
            hit = hit + jnp.sum(jnp.where(column == r.targets[...], logits, 0.0), axis=-1, keepdims=True)
            higher = jnp.maximum(top, jnp.max(logits, axis=-1, keepdims=True))
            total = total * jnp.exp(top - higher) + jnp.sum(jnp.exp(logits - higher), axis=-1, keepdims=True)
            top = higher
        spread = top + jnp.log(total)
        loss_rows = spread - hit
        here = counts > 0.0
        present = jnp.sum(here.astype(F32), axis=-1, keepdims=True)
        inverse = jnp.where(here, 1.0 / jnp.maximum(counts, 1.0), 0.0)
        weight = jnp.sum(r.own_kinds[...] * inverse, axis=-1, keepdims=True)
        loss_out[...] = jnp.broadcast_to(column_sum(weight * loss_rows), (8, 128))
        weight = weight / present
        d_latent = jnp.zeros((picked, D), F32)
        for i in range(steps):
            cols = slice(i * width, (i + 1) * width)
            column = lax.broadcasted_iota(jnp.int32, (picked, width), 1) + i * width
            d_logits = weight * jnp.exp(r.logits[:, cols] - spread)
            d_logits = (d_logits - jnp.where(column == r.targets[...], weight, 0.0)).astype(BF)
            r.d_logits[:, cols] = d_logits
            d_latent = d_latent + dot_right(d_logits, r.table[:, cols])
        normal3 = r.stream[...]
        r.g_vec[6:7, :] = column_sum(d_latent * normal3)
        r.g_vec[7:8, :] = column_sum(d_latent)
        d_act = norm_rows_backward(d_latent, normal3, inverse3, r.vec[6:7, :])
        d_trans = (d_act * slope3).astype(BF)
        r.d_trans[...] = d_trans
        r.g_vec[12:13, :] = column_sum(d_trans.astype(F32))
        d_two = dot_right(d_trans, r.join[:, TRANS_AT : TRANS_AT + D])
        normal2 = r.normal2[...]
        r.g_vec[4:5, :] = column_sum(d_two * normal2)
        r.g_vec[5:6, :] = column_sum(d_two)
        r.d_two[...] = norm_rows_backward(d_two, normal2, r.inverse2[...], r.vec[4:5, :])

    gather = Gather(place, r)
    place.hail(n_dp)
    prepare_table()
    place.hear(n_dp)
    gather.along_z(0)
    r.down_low[...] = r.down_w[...].astype(BF)
    gather.place_down()
    gather.send(gather.late, 0, 1)
    gather.along_z(*range(1, T_PARTS))
    gather.place_own()
    plan = iter(GATHER_PLAN)
    first = next(plan)
    gather.go_on(first[:3])
    prepare_packed()
    gather.place_packed()
    gather.along_z(*range(T_PARTS, Z_TAIL))
    gather.go_on(first[3:24])
    prepare_ids()
    r.g_vec[...] = jnp.zeros_like(r.g_vec)
    counting = TileSum(place, n_dp, r)
    counting.begin(jnp.broadcast_to(column_sum(r.own_kinds[...]), (8, 128)))
    gather.go_on(first[24:])
    thirds = T_PARTS // 3
    for q in range(3):
        gather.need(*range(thirds * q, thirds * q + thirds))
        embed(q)
        gather.go_on(next(plan))
    at = T_PARTS
    gather.need(at, at + 1)
    first_norm()
    save(r.vec, out.vec)
    save(r.col_ids, out.col_ids)
    save(r.spots, out.spots)
    save(r.normal0, out.normal0)
    save(r.inverse0, out.inverse0)
    save(r.x0_low, out.x0_low)
    save(r.join, out.join, 0, OUT_AT)
    gather.go_on(next(plan))
    project()
    save(r.keys, out.keys)
    save(r.values, out.values)
    save(r.query, out.query)
    save(r.x0_rows, out.x0_rows)
    counting.go_on()
    gather.go_on(next(plan))
    for pair in range(0, HEADS // 2, 2):
        attend(pair, pair + 2)
        gather.go_on(next(plan))
    save(r.att, out.att)
    gather.need(at + 2)
    after_attention()
    save(r.normal1, out.normal1)
    save(r.inverse1, out.inverse1)
    save(r.x1_low, out.x1_low)
    gather.go_on(next(plan))
    for part in range(2):
        gather.need(at + 3 + part)
        feed_up(part)
        gather.go_on(next(plan))
    save(r.join, out.join, OUT_AT, TRANS_AT - OUT_AT)
    save(r.hidden, out.hidden)
    save(r.slope, out.slope)
    counts = counting.total()
    counts_out[...] = counts
    gather.need(at + 5, at + 6, gather.late)
    feed_down()
    save(r.down, out.down)
    save(r.x2_low, out.x2_low)
    gather.go_on(next(plan))
    gather.need(at + 7)
    save(r.join, out.join, TRANS_AT, D)
    head(counts[0:1, :])
    gather.go_on(next(plan))
    for src, dst in (
        (r.d_trans, out.d_trans), (r.d_two, out.d_two), (r.d_logits, out.d_logits), (r.latent, out.latent),
        (r.g_vec, out.g_vec),
    ):
        save(src, dst)
    gather.sender.finish()
    for copy in saves:
        copy.wait()


def forward(inputs, n_dp, n_vocab):
    rows = inputs["qkv_w"].shape[0]
    columns, block = inputs["table_in"].shape
    wide = padded(block)
    d_rows = inputs["down_w"].shape[0]
    seqs, seq_len = inputs["tokens"].shape
    tokens, picked = seqs * seq_len, seqs * 128
    table_shape = (D, wide * n_vocab)
    shapes = saved_shapes(rows * n_dp * n_vocab, d_rows * n_dp * n_vocab, tokens, picked, wide * n_vocab)
    dma = pltpu.SemaphoreType.DMA
    scratch = {name: pltpu.VMEM(*shape) for name, shape in shapes.items()}
    scratch.update(
        table=pltpu.VMEM(table_shape, BF),
        table_t=pltpu.VMEM((columns, wide), BF),
        table_rest=pltpu.VMEM((columns, 128), F32),
        vec_rows=pltpu.VMEM((16, 128), F32),
        packed=pltpu.VMEM((2 * rows, JOIN // 2), BF),
        vec_rest=pltpu.VMEM((rows, OUT_AT - VEC_AT), F32),
        down_low=pltpu.VMEM((d_rows, D), BF),
        wide_rows=pltpu.VMEM((8, 128), F32),
        targets=pltpu.VMEM((picked, 1), jnp.int32),
        own_kinds=pltpu.VMEM((picked, 128), F32),
        stage=pltpu.VMEM((n_vocab, 2 * rows, JOIN // 2), BF),
        embedded=pltpu.VMEM((tokens, D), F32),
        x0_rest=pltpu.VMEM((tokens, D), BF),
        stream=pltpu.VMEM((picked, D), F32),
        normal2=pltpu.VMEM((picked, D), F32),
        inverse2=pltpu.VMEM((picked, 1), F32),
        logits=pltpu.VMEM((picked, wide * n_vocab), F32),
        z_send=dma((Z_SLOTS, n_vocab - 1)),
        z_recv=dma((Z_SLOTS, n_vocab - 1)),
        l_send=dma((4, n_vocab - 1)),
        l_recv=dma((4, n_vocab - 1)),
        d_send=dma((N_CHUNKS, 7)),
        d_recv=dma((N_CHUNKS, 7)),
        save_sem=dma((len(shapes) + 2,)),
        **tile_scratch(n_dp, n_vocab),
    )
    vmem = pl.BlockSpec(memory_space=pltpu.VMEM)
    anywhere = pl.BlockSpec(memory_space=pl.ANY)
    tile = jax.ShapeDtypeStruct((8, 128), F32)
    names = tuple(inputs) + tuple(scratch)
    smem = pl.BlockSpec(memory_space=pltpu.SMEM)
    outs = pl.pallas_call(
        functools.partial(forward_kernel, n_dp, n_vocab, names, tuple(shapes)),
        out_shape=tuple(jax.ShapeDtypeStruct(*shape) for shape in shapes.values()) + (tile, tile),
        in_specs=[smem if name == "species" else vmem for name in inputs],
        out_specs=(anywhere,) * len(shapes) + (vmem, vmem),
        scratch_shapes=list(scratch.values()),
        compiler_params=pltpu.CompilerParams(
            collective_id=0, has_side_effects=True, vmem_limit_bytes=VMEM_LIMIT
        ),
    )(*inputs.values())
    return dict(zip(shapes, outs[:-2], strict=True)), outs[-2], outs[-1]


JOINED, DOWN, TABLE = range(3)
REDUCE_ORDER = (
    (JOINED, 5), (JOINED, 3), (JOINED, 4), (DOWN, -1), (DOWN, 0), (DOWN, 1), (JOINED, 2), (JOINED, 0), (JOINED, 1),
) + tuple((TABLE, j) for j in range(T_PARTS))


REDUCE_PLAN = (
    (
        (0, 0),
    ),
    (
        (0, 1), (1, 0),
    ),
    (
        (0, 2),
    ),
    (
        (0, 3), (0, 4), (1, 1),
    ),
    (
        (0, 5),
    ),
    (
        (0, 6), (2, 0), (1, 2),
    ),
    (),
    (
        (3, 0),
    ),
    (
        (1, 5),
    ),
    (),
    (
        (2, 1),
    ),
    (),
    (),
    (
        (2, 2),
    ),
    (
        (1, 3), (1, 4),
    ),
    (),
    (
        (3, 1), (2, 5),
    ),
    (
        (1, 6),
    ),
    (),
    (
        (0, 7), (0, 8),
    ),
    (
        (3, 2), (4, 3),
    ),
    (
        (0, 9), (2, 4),
    ),
    (
        (0, 10),
    ),
    (
        (0, 11), (1, 7),
    ),
    (
        (0, 12), (1, 8), (2, 6),
    ),
    (
        (0, 13), (3, 5),
    ),
    (
        (0, 14), (2, 3),
    ),
    (
        (0, 15), (3, 4),
    ),
    (
        (0, 16),
    ),
    (
        (0, 17),
    ),
    (
        (2, 7), (1, 10), (2, 8), (3, 3), (1, 9), (3, 6), (3, 7), (2, 10), (1, 11), (1, 12), (2, 9), (3, 8),
        (1, 13), (3, 10), (1, 14), (2, 11), (2, 12), (3, 9), (1, 15), (1, 17), (2, 13), (2, 14), (3, 11),
        (3, 12), (1, 16), (2, 15), (2, 17), (3, 14), (3, 13), (3, 15), (2, 16), (3, 17), (3, 16),
    ),
)


class Reduce:
    def __init__(self, place, r, t_cols, from_core, from_two, from_one):
        self.place, self.r, self.sender = place, r, Sender()
        self.from_core, self.from_two, self.from_one = from_core, from_two, from_one
        n_vocab = place.n_vocab
        rows = r.join_out.shape[0] // 2
        d_rows = r.down_out.shape[0]
        t_rows = r.table_out.shape[0]
        piece = t_cols // T_PARTS
        self.rows, self.d_rows, self.t_rows, self.piece = rows, d_rows, t_rows, piece
        self.chunks = []
        for kind, j in REDUCE_ORDER:
            if kind == JOINED:
                first, width = JOIN_PARTS[j]
                view = block_view(r.join, rows * n_vocab, 0, rows * n_vocab, first, width)
            elif kind == DOWN:
                first, width = R_DOWN_PARTS[j] if j >= 0 else (0, R_LATE)
                view = block_view(r.down, d_rows * n_vocab, 0, d_rows * n_vocab, first, width)
            else:
                view = block_view(r.table, t_rows, 0, t_rows, n_vocab * piece * j, n_vocab * piece)
            narrow = view
            if (kind, j) == (DOWN, -1):
                narrow = block_view(r.down, d_rows * n_vocab, place.z * d_rows, d_rows, 0, R_LATE)
            self.chunks.append(((kind, j), view, narrow))
        self.jobs = {}

    def blocks(self, i):
        place = self.place
        one, two = (X, Y) if REDUCE_X[i] == "x" else (Y, X)
        own, a, b = place.dp, place.across(one), place.across(two)
        return one, two, (own, a, b, a + b - own)

    def add_into(self, target, *sources):
        def step(i, carry):
            at = aligned(i * 16, 16, 16)
            if len(sources) == 1:
                target[at, :] = target[at, :] + sources[0][at, :]
            else:
                total = target[at, :].astype(F32)
                for source in sources:
                    total = total + source[at, :].astype(F32)
                target[at, :] = total.astype(BF)
            return carry

        lax.fori_loop(0, target.shape[0] // 16, step, 0)

    def to_core(self, i, k):
        _, _, blocks = self.blocks(i)
        block = blocks[k] + self.place.step_core
        r, place = self.r, self.place
        return remote(
            self.chunks[i][1](block), self.from_core[i].at[k], r.d_send.at[i, k], r.d_recv.at[i, k],
            place.device(CORE),
        )

    def to_two(self, i, k):
        _, two, blocks = self.blocks(i)
        r, place = self.r, self.place
        return remote(
            self.chunks[i][2](blocks[2 + k]), self.from_two[i].at[k], r.d_send.at[i, 4 + k],
            r.d_recv.at[i, 4 + k], place.device(two),
        )

    def to_one(self, i):
        one, _, blocks = self.blocks(i)
        r, place = self.r, self.place
        return remote(
            self.chunks[i][2](blocks[1]), self.from_one[i], r.d_send.at[i, 6], r.d_recv.at[i, 6],
            place.device(one),
        )

    def late_copies(self, i):
        place, r, d_rows = self.place, self.r, self.d_rows
        _, _, blocks = self.blocks(i)
        copies = []
        for j, block in enumerate(blocks):
            for k in range(1, place.n_vocab):
                row = (block * place.n_vocab + place.along(k)) * d_rows
                copies.append(
                    remote(
                        r.down.at[aligned(row, d_rows, 16), pl.ds(0, R_LATE)], r.z_late.at[j, k - 1],
                        r.l_send.at[j, k - 1], r.l_recv.at[j, k - 1], (place.dp, place.along(k)),
                    )
                )
        return copies

    def z_copies(self, slot, src_of, dst_of):
        place, r = self.place, self.r
        return [
            remote(
                src_of(place.along(k)), dst_of(k - 1), r.z_send.at[slot, k - 1], r.z_recv.at[slot, k - 1],
                (place.dp, place.along(k)),
            )
            for k in range(1, place.n_vocab)
        ]

    def pack(self, first, width):
        r, rows, n_vocab = self.r, self.rows, self.place.n_vocab
        half = width // 2
        at = first // 2
        where = aligned(self.place.dp * rows * n_vocab, rows * n_vocab, 16)
        block = r.join[where, first : first + width].astype(F32)
        for k in range(n_vocab):
            piece = block[k * rows : (k + 1) * rows]
            r.packed[k, :, at : at + half] = jnp.concatenate([piece[:, :half], piece[:, half:]], axis=0).astype(BF)

    def along_z(self, i):
        place, r = self.place, self.r
        kind, j = self.chunks[i][0]
        slot = len(self.jobs)
        if kind == JOINED:
            first, width = JOIN_PARTS[j]
            self.pack(first, width)
            cols = pl.ds(first // 2, width // 2)
            copies = self.z_copies(slot, lambda to: r.packed.at[to, :, cols], lambda k: r.z_join.at[k, :, cols])
        elif kind == DOWN:
            first, width = R_DOWN_PARTS[j]
            cols = pl.ds(first, width)
            d_rows, n_vocab = self.d_rows, place.n_vocab
            copies = self.z_copies(
                slot,
                lambda to: r.down.at[aligned((place.dp * n_vocab + to) * d_rows, d_rows, 16), cols],
                lambda k: r.z_down.at[k, :, pl.ds(first - R_LATE, width)],
            )
        else:
            piece, q = self.piece, j
            copies = self.z_copies(
                slot,
                lambda to: r.table.at[
                    aligned(place.dp * self.t_rows, self.t_rows, 16),
                    aligned(q * piece * place.n_vocab + to * piece, piece),
                ],
                lambda k: r.z_table.at[k, :, pl.ds(q * piece, piece)],
            )
        for copy in copies:
            self.sender.go(copy)
        self.jobs[i] = copies

    def is_late(self, i):
        return self.chunks[i][0] == (DOWN, -1)

    def go_on(self, steps):
        for stage, i in steps:
            (self.start, self.after_core, self.after_two, self.after_one, self.after_late)[stage](i)

    def start(self, i):
        for k in range(4):
            self.sender.go(self.to_core(i, k))

    def after_core(self, i):
        view = self.chunks[i][1]
        _, _, blocks = self.blocks(i)
        for k in (2, 3, 0, 1):
            self.to_core(i, k).wait_recv()
            self.add_into(view(blocks[k]), self.from_core[i].at[k])
            if k == 3 and not self.is_late(i):
                self.send_two(i)
        if self.is_late(i):
            for copy in self.late_copies(i):
                self.sender.go(copy)

    def after_late(self, i):
        narrow = self.chunks[i][2]
        _, _, blocks = self.blocks(i)
        for copy in self.late_copies(i):
            copy.wait_recv()
        for j in (2, 3, 0, 1):
            parts = [self.r.z_late.at[j, k] for k in range(self.place.n_vocab - 1)]
            self.add_into(narrow(blocks[j]), *parts)
            if j == 3:
                self.send_two(i)

    def send_two(self, i):
        for k in range(2):
            self.sender.go(self.to_two(i, k))

    def after_two(self, i):
        narrow = self.chunks[i][2]
        _, _, blocks = self.blocks(i)
        self.to_two(i, 1).wait_recv()
        self.add_into(narrow(blocks[1]), self.from_two[i].at[1])
        self.sender.go(self.to_one(i))
        self.to_two(i, 0).wait_recv()
        self.add_into(narrow(blocks[0]), self.from_two[i].at[0])

    def after_one(self, i):
        self.to_one(i).wait_recv()
        self.add_into(self.chunks[i][2](self.place.dp), self.from_one[i])
        if not self.is_late(i):
            self.along_z(i)

    def collect(self):
        place, r = self.place, self.r
        n_vocab = place.n_vocab

        def total(own, parts, out, cols):
            whole = own.astype(F32)
            for part in parts:
                whole = whole + part.astype(F32)
            out[:, cols] = whole
            return jnp.sum(column_sum(whole * whole), axis=-1, keepdims=True)

        square = jnp.zeros((1, 1), F32)
        rows = aligned((place.dp * n_vocab + place.z) * self.d_rows, self.d_rows, 16)
        square += total(r.down[rows, :R_LATE], (), r.down_out, slice(0, R_LATE))
        for i, ((kind, j), _, _) in enumerate(self.chunks):
            if self.is_late(i):
                continue
            for copy in self.jobs[i]:
                copy.wait_recv()
            if kind == JOINED:
                first, width = JOIN_PARTS[j]
                cols = slice(first // 2, first // 2 + width // 2)
                own = r.packed[place.z, :, cols]
                parts = [r.z_join[k, :, cols] for k in range(n_vocab - 1)]
                square += total(own, parts, r.join_out, cols)
            elif kind == DOWN:
                first, width = R_DOWN_PARTS[j]
                low = first - R_LATE
                parts = [r.z_down[k, :, low : low + width] for k in range(n_vocab - 1)]
                own = r.down[rows, first : first + width]
                square += total(own, parts, r.down_out, slice(first, first + width))
            else:
                q = j
                cols = slice(q * self.piece, (q + 1) * self.piece)
                t_rows = aligned(place.dp * self.t_rows, self.t_rows, 16)
                own = r.table[t_rows, aligned(q * self.piece * n_vocab + place.z * self.piece, self.piece)]
                parts = [r.z_table[k, :, cols] for k in range(n_vocab - 1)]
                square += total(own, parts, r.table_out, cols)
        return square


def backward_kernel(n_dp, n_vocab, in_names, names, *refs):
    given = Refs(in_names, refs[: len(in_names)])
    scratch = refs[len(in_names) :]
    n_chunks = len(REDUCE_ORDER)
    lands, scratch = scratch[-3 * n_chunks :], scratch[: -3 * n_chunks]
    r = Refs(names, scratch)
    tokens = given.col_ids.shape[0]
    picked = given.spots.shape[0]
    seqs = 2
    seq_len, slots = tokens // seqs, picked // seqs
    wide = r.table.shape[1]

    def keys_at(s):
        return r.table.at[pl.ds(0, seq_len), pl.ds(s * D, D)]

    def values_at(s):
        return r.table.at[pl.ds(0, seq_len), pl.ds((2 + s) * D, D)]

    hidden = r.table.at[pl.ds(seq_len, picked), pl.ds(0, FF)]
    query = r.table.at[pl.ds(seq_len, picked), pl.ds(FF, D)]
    x0_rows = r.table.at[pl.ds(seq_len, picked), pl.ds(FF + D, D)]
    half = FF // 2
    slopes = [r.table.at[pl.ds(s * picked, picked), pl.ds(4 * D, half)] for s in range(2)]
    count = [0]

    def load(*pairs):
        copies = []
        for src, dst in pairs:
            copies.append(pltpu.make_async_copy(src, dst, r.load_sem.at[count[0]]))
            copies[-1].start()
            count[0] += 1
        return copies

    def seq_pairs(src, dst):
        return [(src.at[pl.ds(s * seq_len, seq_len), :], dst(s)) for s in range(seqs)]

    def need(*groups):
        for copies in groups:
            for copy in copies:
                copy.wait()

    up_cols, low_cols = pl.ds(UP_AT, FF), pl.ds(0, UP_AT)
    got_trans = load((given.x2_low, r.x2_low), (given.d_trans, r.d_trans))
    got_feed = load(
        (given.d_two, r.stream), (given.x1_low, r.x1_low),
        *[(given.slope.at[:, pl.ds(s * half, half)], slopes[s]) for s in range(2)],
        (given.join.at[:, up_cols], r.join.at[:, up_cols]), (given.down, r.down),
    )
    got_hidden = load((given.hidden, hidden))
    got_out = load(
        (given.normal1, r.normal1), (given.att, r.att), (given.join.at[:, low_cols], r.join.at[:, low_cols])
    )
    got_att = load(
        *seq_pairs(given.values, values_at), *seq_pairs(given.keys, keys_at), (given.query, query)
    )
    got_first = load((given.x0_rows, x0_rows), (given.x0_low, r.x0_low), (given.normal0, r.normal0))
    got_head = load((given.d_logits, r.d_logits))

    place = Place(n_vocab)
    place.greet(n_dp)
    reduce = Reduce(
        place, r, wide // n_vocab, lands[:n_chunks], lands[n_chunks : 2 * n_chunks], lands[2 * n_chunks :]
    )
    r.g_vec[...] = given.g_vec[...]

    def gain(i):
        return given.vec[i : i + 1, :]

    def put(first, width, value):
        r.join[:, first : first + width] = value.astype(BF)

    need(got_trans)
    put(TRANS_AT, D, dot_left(r.x2_low[...], r.d_trans[...]))
    plan = iter(REDUCE_PLAN)
    reduce.go_on(next(plan))

    need(got_feed)
    d_ffn = r.stream[...].astype(BF)
    r.d_rows_low[...] = d_ffn
    r.g_vec[11:12, :] = column_sum(d_ffn.astype(F32))

    def feed(part):
        def step(j, carry):
            cols = aligned(j * D, D)
            up_at = aligned(UP_AT + part * half + j * D, D)
            d_act = dot_right(r.d_rows_low[...], r.down[aligned(part * half + j * D, D), :])
            d_hidden = (d_act * slopes[part][:, cols].astype(F32)).astype(BF)
            r.stream[...] += dot_right(d_hidden, r.join[:, up_at])
            r.join[:, up_at] = dot_left(r.x1_low[...], d_hidden).astype(BF)
            return carry

        lax.fori_loop(0, half // D, step, 0)

    feed(0)
    reduce.go_on(next(plan))
    feed(1)
    reduce.go_on(next(plan))
    need(got_hidden)

    def feed_down(first, width):
        def step(j, carry):
            rows = aligned(j * D, D)
            cols = slice(first, first + width)
            r.down[rows, cols] = dot_left(hidden[:, rows], r.d_rows_low[:, cols]).astype(BF)
            return carry

        lax.fori_loop(0, FF // D, step, 0)

    first = R_LATE + R_DOWN_PARTS[0][1]
    feed_down(0, first)
    reduce.go_on(next(plan))
    feed_down(first, D - first)
    reduce.go_on(next(plan))

    need(got_out)
    d_one = r.stream[...]
    normal1 = r.normal1[...]
    r.g_vec[2:3, :] = column_sum(d_one * normal1)
    r.g_vec[3:4, :] = column_sum(d_one)
    d_one = norm_rows_backward(d_one, normal1, given.inverse1[...], gain(2))
    r.stream[...] = d_one
    d_proj = d_one.astype(BF)
    r.g_vec[10:11, :] = column_sum(d_proj.astype(F32))
    r.x2_low[...] = dot_right(d_proj, r.join[:, OUT_AT : OUT_AT + D]).astype(BF)
    put(OUT_AT, D, dot_left(r.att[...], d_proj))
    got_latent = load((given.latent, r.att))
    reduce.go_on(next(plan))

    need(got_att)
    lane = lax.broadcasted_iota(jnp.int32, (slots, 128), 1)

    def attend(j, carry):
        lanes = aligned(j * 128, 128)
        for s in range(seqs):
            rows = slice(s * slots, (s + 1) * slots)
            q2 = query[rows, lanes]
            g2 = r.x2_low[rows, lanes]
            k2 = keys_at(s)[:, lanes]
            v2 = values_at(s)[:, lanes]
            d_q, d_k, d_v = [], None, None
            for a in range(2):
                mine = (lane >= HD) if a else (lane < HD)
                q1 = jnp.where(mine, q2, jnp.zeros_like(q2))
                g1 = jnp.where(mine, g2, jnp.zeros_like(g2))
                scores = dot_right(q1, k2) * HD ** (-0.5)
                expo = jnp.exp(scores - jnp.max(scores, axis=-1, keepdims=True))
                probs = expo * (1.0 / jnp.sum(expo, axis=-1, keepdims=True))
                d_probs = dot_right(g1, v2)
                delta = jnp.sum(d_probs * probs, axis=-1, keepdims=True)
                d_scores = (probs * (d_probs - delta)).astype(BF)
                d_q.append(rows_dot(d_scores, k2))
                more_k = dot_left(d_scores, q1)
                more_v = dot_left(probs.astype(BF), g1)
                d_k = more_k if d_k is None else d_k + more_k
                d_v = more_v if d_v is None else d_v + more_v
            r.d_trans[rows, lanes] = (jnp.where(lane < HD, d_q[0], d_q[1]) * HD ** (-0.5)).astype(BF)
            keys_at(s)[:, lanes] = (d_k * HD ** (-0.5)).astype(BF)
            values_at(s)[:, lanes] = d_v.astype(BF)
        return carry

    for pair in range(HEADS // 2):
        lax.fori_loop(pair, pair + 1, attend, 0)
        reduce.go_on(next(plan))

    need(got_first)
    d_query = r.d_trans[...]
    r.g_vec[8:9, :] = column_sum(d_query.astype(F32))
    d_rows = r.stream[...] + dot_right(d_query, r.join[:, :D])
    high = d_rows.astype(BF)
    r.d_rows_low[...] = high
    r.x1_low[...] = (d_rows - high.astype(F32)).astype(BF)
    put(0, D, dot_left(x0_rows[...], d_query))
    for i in (0, 1, 9, 13):
        r.g_vec[i : i + 1, :] = jnp.zeros((1, D), F32)

    reduce.go_on(next(plan))

    for s in range(seqs):

        def step(i, carry, s=s):
            inside = aligned(i * 256, 256)
            at = aligned(s * seq_len + i * 256, 256)
            d_v = values_at(s)[inside, :]
            r.g_vec[9:10, :] += column_sum(d_v.astype(F32))
            d_zero = dot_right(keys_at(s)[inside, :], r.join[:, D : 2 * D])
            d_zero = d_zero + dot_right(d_v, r.join[:, 2 * D : 3 * D])
            column = lax.broadcasted_iota(jnp.int32, (slots, 256), 1) + i * 256
            rows = slice(s * slots, (s + 1) * slots)
            pick = (given.spots[rows, :] == column).astype(BF)
            d_zero = d_zero + (dot_left(pick, r.d_rows_low[rows, :]) + dot_left(pick, r.x1_low[rows, :]))
            normal = r.normal0[at, :].astype(F32)
            r.g_vec[0:1, :] += column_sum(d_zero * normal)
            r.g_vec[1:2, :] += column_sum(d_zero)
            d_emb = norm_rows_backward(d_zero, normal, given.inverse0[at, :], gain(0)).astype(BF)
            r.g_vec[13:14, :] += column_sum(jnp.where(given.col_ids[at, :] < 0, d_emb.astype(F32), 0.0))
            r.normal0[at, :] = d_emb
            return carry

        for i in range(seq_len // 256):
            lax.fori_loop(i, i + 1, step, 0)
            reduce.go_on(next(plan))

    def weigh(i, carry):
        cols = aligned(i * 256, 256)
        for part, source in ((1, keys_at), (2, values_at)):
            value = sum(
                dot_left(r.x0_low[s * seq_len : (s + 1) * seq_len, :], source(s)[:, cols]) for s in range(seqs)
            )
            r.join[:, aligned(part * D + i * 256, 256)] = value.astype(BF)
        return carry

    lax.fori_loop(0, 2, weigh, 0)
    reduce.go_on(next(plan))
    lax.fori_loop(2, D // 256, weigh, 0)
    reduce.go_on(next(plan))
    columns = jnp.concatenate([r.g_vec[...], jnp.zeros((112, D), F32)], axis=0).T
    put(VEC_AT, 128, columns)
    put(VEC_AT + 128, 128, jnp.zeros((D, 128), F32))
    reduce.go_on(next(plan))

    need(got_head, got_latent)
    r.flipped[:, :tokens] = r.normal0[...].T
    r.flipped[:, tokens:] = r.att[...].T
    reduce.go_on(next(plan))
    width = wide // T_PARTS
    for j in range(T_PARTS):
        cols = slice(j * width, (j + 1) * width)
        column = lax.broadcasted_iota(jnp.int32, (tokens, width), 1) + j * width
        onehot = (given.col_ids[...] == column).astype(BF)
        value = rows_dot(r.flipped[:, :tokens], onehot) + rows_dot(r.flipped[:, tokens:], r.d_logits[:, cols])
        r.table[:, cols] = value.astype(BF)
        reduce.go_on(next(plan))
    reduce.go_on(next(plan))
    square = reduce.collect()
    row = lax.broadcasted_iota(jnp.int32, (8, 128), 0)
    summing = TileSum(place, n_dp, r)
    summing.begin(jnp.where(row == 0, square, given.loss[...]))
    summing.go_on()
    r.tile_out[...] = summing.total()
    reduce.sender.finish()


def backward(saved, loss, n_dp, n_vocab):
    rows = saved["join"].shape[0] // (n_dp * n_vocab)
    d_rows = saved["down"].shape[0] // (n_dp * n_vocab)
    t_rows = D // n_dp
    t_cols = saved["d_logits"].shape[1] // n_vocab
    tokens, picked = saved["col_ids"].shape[0], saved["spots"].shape[0]
    core_shapes, far_shapes = [], []
    for kind, j in REDUCE_ORDER:
        if kind == JOINED:
            shape = (rows * n_vocab, JOIN_PARTS[j][1])
        elif kind == DOWN:
            shape = (d_rows * n_vocab, R_DOWN_PARTS[j][1] if j >= 0 else R_LATE)
        else:
            shape = (t_rows, t_cols * n_vocab // T_PARTS)
        core_shapes.append((4,) + shape)
        far_shapes.append((d_rows, R_LATE) if (kind, j) == (DOWN, -1) else shape)
    inputs = dict(saved, loss=loss)
    inputs.pop("x0_rest", None)
    outs = dict(
        join_out=(2 * rows, JOIN // 2), down_out=(d_rows, D), table_out=(t_rows, t_cols), tile_out=(8, 128)
    )
    dma = pltpu.SemaphoreType.DMA
    rows_low = pltpu.VMEM((picked, D), BF)
    tokens_low = pltpu.VMEM((tokens, D), BF)
    scratch = dict(
        join=pltpu.VMEM(saved["join"].shape, BF),
        down=pltpu.VMEM(saved["down"].shape, BF),
        table=pltpu.VMEM((D, t_cols * n_vocab), BF),
        normal0=tokens_low,
        x0_low=tokens_low,
        att=rows_low,
        x1_low=rows_low,
        x2_low=rows_low,
        d_trans=rows_low,
        d_rows_low=rows_low,
        normal1=pltpu.VMEM((picked, D), F32),
        stream=pltpu.VMEM((picked, D), F32),
        d_logits=pltpu.VMEM(saved["d_logits"].shape, BF),
        g_vec=pltpu.VMEM((16, D), F32),
        flipped=pltpu.VMEM((D, tokens + picked), BF),
        packed=pltpu.VMEM((n_vocab, 2 * rows, JOIN // 2), BF),
        z_join=pltpu.VMEM((n_vocab - 1, 2 * rows, JOIN // 2), BF),
        z_down=pltpu.VMEM((n_vocab - 1, d_rows, D - R_LATE), BF),
        z_late=pltpu.VMEM((4, n_vocab - 1, d_rows, R_LATE), BF),
        z_table=pltpu.VMEM((n_vocab - 1, t_rows, t_cols), BF),
        load_sem=dma((len(saved) + 4,)),
        z_send=dma((Z_SLOTS, n_vocab - 1)),
        z_recv=dma((Z_SLOTS, n_vocab - 1)),
        l_send=dma((4, n_vocab - 1)),
        l_recv=dma((4, n_vocab - 1)),
        d_send=dma((N_CHUNKS, 7)),
        d_recv=dma((N_CHUNKS, 7)),
        **tile_scratch(n_dp, n_vocab),
    )
    lands = [pltpu.VMEM(shape, BF) for shape in core_shapes]
    lands += [pltpu.VMEM((2,) + shape, BF) for shape in far_shapes]
    lands += [pltpu.VMEM(shape, BF) for shape in far_shapes]
    vmem = pl.BlockSpec(memory_space=pltpu.VMEM)
    anywhere = pl.BlockSpec(memory_space=pl.ANY)
    near = set(dict(vec=0, g_vec=0, inverse0=0, inverse1=0, col_ids=0, spots=0, loss=0))
    return pl.pallas_call(
        functools.partial(backward_kernel, n_dp, n_vocab, tuple(inputs), tuple(outs) + tuple(scratch)),
        out_shape=tuple(jax.ShapeDtypeStruct(shape, F32) for shape in outs.values()),
        in_specs=[vmem if name in near else anywhere for name in inputs],
        out_specs=(vmem,) * len(outs),
        scratch_shapes=list(scratch.values()) + lands,
        compiler_params=pltpu.CompilerParams(
            collective_id=1, has_side_effects=True, vmem_limit_bytes=VMEM_LIMIT
        ),
    )(*inputs.values())


def update_kernel(n_state, *refs):
    tile, counts, g_join, g_down, g_table = refs[:5]
    states = refs[5 : 5 + 3 * n_state]
    outs = refs[5 + 3 * n_state : 5 + 7 * n_state]
    loss_out, present_out, norm_out = refs[5 + 7 * n_state :]
    norm = jnp.sqrt(tile[0:1, 0:1])
    factor = jnp.minimum(1.0, clip_limit / (norm + 1e-06))
    norm_out[0] = jnp.max(norm)
    loss_out[0] = jnp.max(tile[1:2, 0:1])
    present_out[0] = jnp.sum((counts[0:1, :] > 0.0).astype(F32))

    def advance(index, cols, gradient, rate):
        weight, first, second = (ref[:, cols] for ref in states[3 * index : 3 * index + 3])
        first, second, new = adamw(weight, first, second, gradient * factor, rate)
        targets = outs[4 * index : 4 * index + 4]
        targets[0][:, cols] = first
        targets[1][:, cols] = second
        targets[2][:, cols] = new
        targets[3][:, cols] = new.astype(targets[3].dtype)

    every = slice(None)
    block = states[0].shape[1]
    full = block // 128 * 128
    advance(0, slice(0, full), g_table[:, :full], matrix_rate)
    if full < block:
        advance(0, slice(full, block), g_table[:, full:block], matrix_rate)
    rows = g_join.shape[0] // 2
    for matrix, first, column, width in join_pieces():
        side, at = packed_at(column)
        if matrix == 1:
            square = jnp.concatenate([g_join[side * rows : (side + 1) * rows, at : at + 128], jnp.zeros((128 - rows, 128), F32)], axis=0)
            advance(2, every, square.T[:width, :rows], vector_rate)
        else:
            gradient = g_join[side * rows : (side + 1) * rows, at : at + width]
            advance(1 + matrix, slice(first, first + width), gradient, matrix_rate)
    advance(6, every, g_down[...], matrix_rate)


def update(tile, counts, g_join, g_down, g_table, states):
    vmem = pl.BlockSpec(memory_space=pltpu.VMEM)
    smem = pl.BlockSpec(memory_space=pltpu.SMEM)
    shapes = []
    for index, (weight, _, _) in enumerate(states):
        shapes += [jax.ShapeDtypeStruct(weight.shape, F32)] * 3
        shapes.append(jax.ShapeDtypeStruct(weight.shape, F32 if index == 2 else BF))
    flat = [array for state in states for array in state]
    scalars = [jax.ShapeDtypeStruct((1,), F32)] * 3
    return pl.pallas_call(
        functools.partial(update_kernel, len(states)),
        out_shape=tuple(shapes + scalars),
        in_specs=[vmem] * (5 + len(flat)),
        out_specs=(vmem,) * len(shapes) + (smem,) * 3,
        compiler_params=pltpu.CompilerParams(vmem_limit_bytes=VMEM_LIMIT),
    )(tile, counts, g_join, g_down, g_table, *flat)


def species_counts(picks, species, seq_len):
    live = (picks < seq_len).astype(F32)
    kinds = jnp.arange(NSPEC, dtype=jnp.int32)
    return jnp.sum((species[:, None] == kinds[None, :]).astype(F32) * jnp.sum(live, axis=1)[:, None], axis=0)


def local_step(tokens, picks, species, counts, join, down, table_t, col_id):
    seqs, seq_len = tokens.shape
    slots = picks.shape[1]
    w_qkv = join[:, : 3 * D]
    vec = join[:, VEC_AT : VEC_AT + NVEC].astype(F32)
    w_out = join[:, OUT_AT : OUT_AT + D]
    w_up = join[:, UP_AT : UP_AT + FF]
    w_trans = join[:, TRANS_AT : TRANS_AT + D]

    masked = jnp.any(picks[:, :, None] == jnp.arange(seq_len, dtype=jnp.int32)[None, None, :], axis=1)
    masked_flat = masked.reshape(-1)
    live = (picks < seq_len).reshape(-1)
    spot = jnp.minimum(picks, seq_len - 1)
    row_index = (spot + jnp.arange(seqs, dtype=jnp.int32)[:, None] * seq_len).reshape(-1)
    target = jnp.take_along_axis(tokens, spot, axis=1).reshape(-1)
    row_species = jnp.broadcast_to(species[:, None], picks.shape).reshape(-1)

    inputs = jnp.where(masked, -2, tokens).reshape(-1)
    onehot = (inputs[:, None] == col_id[None, :]).astype(BF)
    embedded = jnp.where(masked_flat[:, None], vec[:, 13], dot_right(onehot, table_t))
    stream_zero, normal0, inverse0 = norm_forward(embedded, vec[:, 0], vec[:, 1])
    x0_low = stream_zero.astype(BF)
    keys = dot_low(x0_low, w_qkv[:, D : 2 * D]).astype(BF)
    values = (dot_low(x0_low, w_qkv[:, 2 * D :]) + vec[:, 9]).astype(BF)
    x0_rows = stream_zero[row_index]
    x0_rows_low = x0_rows.astype(BF)
    query = (dot_low(x0_rows_low, w_qkv[:, :D]) + vec[:, 8]).astype(BF)
    q4 = query.reshape(seqs, slots, HEADS, HD)
    k4 = keys.reshape(seqs, seq_len, HEADS, HD)
    v4 = values.reshape(seqs, seq_len, HEADS, HD)
    scores = jnp.einsum("sqhd,skhd->shqk", q4, k4, preferred_element_type=F32) * HD ** (-0.5)
    probs = jax.nn.softmax(scores, axis=-1)
    probs_low = probs.astype(BF)
    att = jnp.einsum("shqk,skhd->sqhd", probs_low, v4, preferred_element_type=F32)
    att_low = att.reshape(-1, D).astype(BF)
    stream_one, normal1, inverse1 = norm_forward(
        x0_rows + dot_low(att_low, w_out) + vec[:, 10], vec[:, 2], vec[:, 3]
    )
    x1_low = stream_one.astype(BF)
    hidden = dot_low(x1_low, w_up)
    hidden_low = gelu(hidden).astype(BF)
    stream_two, normal2, inverse2 = norm_forward(
        stream_one + dot_low(hidden_low, down) + vec[:, 11], vec[:, 4], vec[:, 5]
    )
    picked_low = stream_two.astype(BF)
    trans = dot_low(picked_low, w_trans) + vec[:, 12]
    latent, normal3, inverse3 = norm_forward(gelu(trans), vec[:, 6], vec[:, 7])
    latent_low = latent.astype(BF)
    logits = dot_low(latent_low, table_t)
    logits = jnp.where(((col_id >= 0) & (col_id < VREAL))[None, :], logits, floor_value)
    top = jnp.max(logits, axis=-1, keepdims=True)
    expo = jnp.exp(logits - top)
    total = jnp.sum(expo, axis=-1, keepdims=True)
    is_target = col_id[None, :] == target[:, None]
    hit = jnp.sum(jnp.where(is_target, logits, 0.0), axis=-1)
    loss_rows = (top + jnp.log(total))[:, 0] - hit
    kinds = jnp.arange(NSPEC, dtype=jnp.int32)
    own = ((row_species[:, None] == kinds[None, :]) & live[:, None]).astype(F32)
    species_loss = jnp.sum(own * loss_rows[:, None], axis=0)
    present_mask = counts > 0
    present = jnp.sum(present_mask.astype(F32))
    inverse = jnp.where(present_mask, 1.0 / jnp.maximum(counts, 1.0), 0.0) / present
    weight = jnp.sum(own * inverse[None, :], axis=-1)
    loss_part = jnp.sum(jnp.where(present_mask, species_loss / jnp.maximum(counts, 1.0), 0.0))
    d_logits = (weight[:, None] * (expo / total - is_target.astype(F32))).astype(BF)

    d_latent = dot_right(d_logits, table_t)
    d_act, d6, d7 = norm_backward(d_latent, normal3, inverse3, vec[:, 6])
    d_trans = (d_act * gelu_slope(trans)).astype(BF)
    g_trans = dot_left(picked_low, d_trans)
    d12 = jnp.sum(d_trans.astype(F32), axis=0)
    d_two, d4, d5 = norm_backward(dot_right(d_trans, w_trans), normal2, inverse2, vec[:, 4])
    d_ffn = d_two.astype(BF)
    d11 = jnp.sum(d_ffn.astype(F32), axis=0)
    g_down = dot_left(hidden_low, d_ffn)
    d_hidden = (dot_right(d_ffn, down) * gelu_slope(hidden)).astype(BF)
    g_up = dot_left(x1_low, d_hidden)
    d_one, d2, d3 = norm_backward(d_two + dot_right(d_hidden, w_up), normal1, inverse1, vec[:, 2])
    d_proj = d_one.astype(BF)
    d10 = jnp.sum(d_proj.astype(F32), axis=0)
    g_out = dot_left(att_low, d_proj)
    d_att = dot_right(d_proj, w_out).astype(BF).reshape(seqs, slots, HEADS, HD)
    d_probs = jnp.einsum("sqhd,skhd->shqk", d_att, v4, preferred_element_type=F32)
    delta = jnp.sum(d_probs * probs, axis=-1, keepdims=True)
    d_scores = (probs * (d_probs - delta)).astype(BF)
    d_q = jnp.einsum("shqk,skhd->sqhd", d_scores, k4, preferred_element_type=F32) * HD ** (-0.5)
    d_k = jnp.einsum("shqk,sqhd->skhd", d_scores, q4, preferred_element_type=F32) * HD ** (-0.5)
    d_v = jnp.einsum("shqk,sqhd->skhd", probs_low, d_att, preferred_element_type=F32)
    d_q = d_q.reshape(-1, D).astype(BF)
    d_k = d_k.reshape(-1, D).astype(BF)
    d_v = d_v.reshape(-1, D).astype(BF)
    d8 = jnp.sum(d_q.astype(F32), axis=0)
    d9 = jnp.sum(d_v.astype(F32), axis=0)
    g_q = dot_left(x0_rows_low, d_q)
    g_k = dot_left(x0_low, d_k)
    g_v = dot_left(x0_low, d_v)
    d_rows = d_one + dot_right(d_q, w_qkv[:, :D])
    d_zero = dot_right(d_k, w_qkv[:, D : 2 * D]) + dot_right(d_v, w_qkv[:, 2 * D :])
    d_zero = d_zero.at[row_index].add(jnp.where(live[:, None], d_rows, 0.0))
    d_emb, d0, d1 = norm_backward(d_zero, normal0, inverse0, vec[:, 0])
    d_emb_low = d_emb.astype(BF)
    d13 = jnp.sum(jnp.where(masked_flat[:, None], d_emb_low.astype(F32), 0.0), axis=0)
    g_table = dot_left(latent_low, d_logits) + dot_left(d_emb_low, onehot)
    g_vec = jnp.stack([d0, d1, d2, d3, d4, d5, d6, d7, d8, d9, d10, d11, d12, d13], axis=1)
    g_vec = jnp.pad(g_vec, ((0, 0), (0, OUT_AT - VEC_AT - NVEC)))
    g_join = jnp.concatenate([g_q, g_k, g_v, g_vec, g_out, g_up, g_trans], axis=1)
    return loss_part, present, g_join.astype(BF), g_down.astype(BF), g_table.astype(BF)


def adamw(weight, first, second, gradient, rate):
    first = 0.5 * first + 0.5 * gradient
    second = 0.5 * second + 0.5 * gradient * gradient
    fix = 1.0 - 0.5**STEP
    step = first / fix / (jnp.sqrt(second / fix) + adam_eps)
    return (first, second, weight - rate * (step + decay_rate * weight))


def body(
    n_dp, n_vocab, tokens, picks, species,
    table, table_m, table_v, qkv_w, qkv_m, qkv_v, out_w, out_m, out_v, up_w, up_m, up_v,
    down_w, down_m, down_v, trans_w, trans_m, trans_v, vectors, vectors_m, vectors_v,
):
    block, columns = table.shape
    wide = padded(block)
    rows = qkv_w.shape[0]
    seqs, seq_len = tokens.shape
    both = ("dp", "vocab")
    own_kernels = n_dp == 8 and n_vocab * rows % 16 == 0 and rows % 8 == 0 and columns % 16 == 0 and seqs == 2
    own_kernels = own_kernels and part_cols(wide) * T_PARTS == wide
    if own_kernels:
        column = np.arange(wide * n_vocab)
        token = np.array(token_of(column, block, n_vocab, wide, np))
        col_floor = np.where((token >= 0) & (token < VREAL), 0.0, floor_value).astype(np.float32)[None, :]
        inputs = dict(
            table_in=table.T, down_w=down_w, qkv_w=qkv_w, vectors=vectors.T, out_w=out_w, up_w=up_w, trans_w=trans_w,
            tokens=tokens, picks=picks, species=species, col_floor=jnp.asarray(col_floor),
        )
        saved, counts, loss = forward(inputs, n_dp, n_vocab)
        g_join, g_down, g_table, tile = backward(saved, loss, n_dp, n_vocab)
        states = (
            (table.T, table_m.T, table_v.T), (qkv_w, qkv_m, qkv_v), (vectors.T, vectors_m.T, vectors_v.T),
            (out_w, out_m, out_v), (up_w, up_m, up_v), (trans_w, trans_m, trans_v), (down_w, down_m, down_v),
        )
        new = list(update(tile, counts, g_join, g_down, g_table, states))
        for index in (0, 2):
            new[4 * index : 4 * index + 4] = [array.T for array in new[4 * index : 4 * index + 4]]
        order = (0, 1, 3, 4, 6, 5)
        outs = [new[4 * index + part] for index in order for part in range(4)] + new[8:11]
        return tuple(outs) + tuple(array.reshape(()) for array in new[28:])
    col_token = token_of(jnp.arange(wide * n_vocab, dtype=jnp.int32), block, n_vocab, wide, jnp)
    joined = jnp.concatenate(
        [qkv_w, jnp.pad(vectors, ((0, 0), (0, OUT_AT - VEC_AT - NVEC))), out_w, up_w, trans_w], axis=1
    ).astype(BF)
    down_low = down_w.astype(BF)
    table_t = jnp.pad(table.T.astype(BF), ((0, 0), (0, wide - block)))
    counts = species_counts(picks, species, seq_len)
    piece = part_cols(wide)
    parts = wide // piece
    join_all = lax.all_gather(joined, both, axis=0, tiled=True)
    down_all = lax.all_gather(down_low, both, axis=0, tiled=True)
    table_all = lax.all_gather(table_t, "dp", axis=0, tiled=True).reshape(D, parts, 1, piece)
    table_all = lax.all_gather(table_all, "vocab", axis=2, tiled=True).reshape(D, wide * n_vocab)
    counts = lax.psum(counts, both)
    loss, present, g_join, g_down, g_table = local_step(
        tokens, picks, species, counts, join_all, down_all, table_all, col_token
    )
    g_join = lax.psum_scatter(g_join.astype(F32), both, scatter_dimension=0, tiled=True)
    g_down = lax.psum_scatter(g_down.astype(F32), both, scatter_dimension=0, tiled=True)
    g_table = lax.psum_scatter(g_table, "dp", scatter_dimension=0, tiled=True)
    g_table = g_table.reshape(columns, parts, n_vocab, piece)
    g_table = lax.psum_scatter(g_table, "vocab", scatter_dimension=2, tiled=True)
    g_table = g_table.reshape(columns, wide).astype(F32)
    square = jnp.sum(g_join * g_join) + jnp.sum(g_down * g_down) + jnp.sum(g_table * g_table)
    square, loss_sum = lax.psum((square, loss), both)
    grad_norm = jnp.sqrt(square)
    factor = jnp.minimum(1.0, clip_limit / (grad_norm + 1e-06))
    grads = (
        g_table[:, :block].T, g_join[:, : 3 * D], g_join[:, OUT_AT : OUT_AT + D], g_join[:, UP_AT : UP_AT + FF],
        g_down, g_join[:, TRANS_AT:], g_join[:, VEC_AT : VEC_AT + NVEC],
    )
    masters = (table, qkv_w, out_w, up_w, down_w, trans_w, vectors)
    firsts = (table_m, qkv_m, out_m, up_m, down_m, trans_m, vectors_m)
    seconds = (table_v, qkv_v, out_v, up_v, down_v, trans_v, vectors_v)
    outs = []
    for index in range(7):
        rate = vector_rate if index == 6 else matrix_rate
        first, second, new = adamw(masters[index], firsts[index], seconds[index], grads[index] * factor, rate)
        outs.extend([first, second, new])
        if index < 6:
            outs.append(new.astype(BF))
    return tuple(outs) + (loss_sum, present, grad_norm)


def solution(mesh):
    both = P(("dp", "vocab"), None)
    split = P("vocab", "dp")
    in_specs = (both, both, P(("dp", "vocab"))) + (split,) * 3 + (both,) * 18
    out_specs = (split,) * 4 + (both,) * 23 + (P(),) * 3
    step = functools.partial(body, mesh.shape["dp"], mesh.shape["vocab"])
    return jax.shard_map(step, mesh=mesh, in_specs=in_specs, out_specs=out_specs, check_vma=False)
```

```python
import functools

import jax
import jax.numpy as jnp
import numpy as np
from jax import lax
from jax.experimental import pallas as pl
from jax.experimental.pallas import tpu as pltpu
from jax.sharding import PartitionSpec as P

D = 768
HEADS = 12
HD = 64
FF = 3072
NSPEC = 8
NVEC = 14
STEP = 10
VREAL = 4101
MESH = pl.DeviceIdType.MESH
BF = jnp.bfloat16
F32 = jnp.float32

norm_eps = 1e-05
clip_limit = 0.01
matrix_rate = 0.06
vector_rate = 0.5
decay_rate = 0.01
adam_eps = 1e-08
floor_value = -1e30

VEC_AT = 3 * D
OUT_AT = VEC_AT + 256
UP_AT = OUT_AT + D
TRANS_AT = UP_AT + FF
JOIN = TRANS_AT + D
JOIN_PARTS = (
    (0, 1280),
    (1280, 1280),
    (OUT_AT, 768),
    (UP_AT, 1536),
    (UP_AT + 1536, 1536),
    (TRANS_AT, 768),
)
VMEM_LIMIT = 63 * 2**20


T_PARTS = 9
LATE = 256
DOWN_PARTS = ((LATE, 256), (LATE + 256, D - LATE - 256))
R_LATE = 128
R_DOWN_PARTS = ((R_LATE, 256), (R_LATE + 256, D - R_LATE - 256))
GATHER_X = "yxxxxyyyxxyyxyxyxx"
REDUCE_X = "xxyyyxxyxxyyxxyxxy"
CORE, X, Y = range(3)


def padded(rows):
    return -(-rows // 128) * 128


def part_cols(wide):
    return wide // T_PARTS if wide % (128 * T_PARTS) == 0 else wide


def token_of(column, block, n_vocab, wide, xp):
    piece = part_cols(wide)
    inside = column % (piece * n_vocab)
    row = column // (piece * n_vocab) * piece + inside % piece
    return xp.where(row < block, inside // piece * block + row, -1)


class Place:
    def __init__(self, n_vocab):
        dp = lax.axis_index("dp")
        z = lax.axis_index("vocab")
        core = lax.rem(dp, 2)
        bit_x = lax.rem(lax.div(dp, 2), 2)
        bit_y = lax.div(dp, 4)
        self.dp, self.z, self.core, self.n_vocab = dp, z, core, n_vocab
        self.step_core = 1 - 2 * core
        self.step_x = 2 - 4 * bit_x
        self.step_y = 4 - 8 * bit_y

    def across(self, which):
        return self.dp + (self.step_core, self.step_x, self.step_y)[which]

    def device(self, which):
        return (self.across(which), self.z)

    def along(self, k):
        return lax.rem(self.z + k, self.n_vocab)

    def greet(self, n_dp):
        self.hail(n_dp)
        self.hear(n_dp)

    def hail(self, n_dp):
        barrier = pltpu.get_barrier_semaphore()
        for k in range(1, n_dp):
            other = lax.rem(self.dp + k, n_dp)
            pl.semaphore_signal(barrier, inc=1, device_id=(other, self.z), device_id_type=MESH)
        for k in range(1, self.n_vocab):
            pl.semaphore_signal(barrier, inc=1, device_id=(self.dp, self.along(k)), device_id_type=MESH)

    def hear(self, n_dp):
        pl.semaphore_wait(pltpu.get_barrier_semaphore(), n_dp + self.n_vocab - 2)


def remote(src, dst, send, recv, device):
    return pltpu.make_async_remote_copy(
        src_ref=src, dst_ref=dst, send_sem=send, recv_sem=recv, device_id=device, device_id_type=MESH
    )


def block_view(ref, stride, offset, rows, first, width):
    def view(index):
        return ref.at[pl.ds(pl.multiple_of(index * stride + offset, 16), rows), pl.ds(first, width)]

    return view


class TileSum:
    def __init__(self, place, n_dp, r):
        self.place, self.n_dp, self.r = place, n_dp, r

    def z_copies(self):
        place, r = self.place, self.r
        return [
            remote(
                r.tiles.at[0], r.tile_ring.at[place.z], r.tile_send.at[k - 1], r.tile_recv.at[k - 1],
                (place.dp, place.along(k)),
            )
            for k in range(1, place.n_vocab)
        ]

    def dp_copies(self):
        place, r, base = self.place, self.r, self.place.n_vocab - 1
        return [
            remote(
                r.tiles.at[1], r.tile_land.at[place.dp], r.tile_send.at[base + k - 1],
                r.tile_recv.at[base + k - 1], (lax.rem(place.dp + k, self.n_dp), place.z),
            )
            for k in range(1, self.n_dp)
        ]

    def begin(self, value):
        self.r.tiles[0] = value
        self.r.tile_ring[self.place.z] = value
        for copy in self.z_copies():
            copy.start()

    def go_on(self):
        for copy in self.z_copies():
            copy.wait()
        value = self.r.tile_ring[0]
        for k in range(1, self.place.n_vocab):
            value = value + self.r.tile_ring[k]
        self.r.tiles[1] = value
        self.r.tile_land[self.place.dp] = value
        for copy in self.dp_copies():
            copy.start()

    def total(self):
        for copy in self.dp_copies():
            copy.wait()
        value = self.r.tile_land[0]
        for k in range(1, self.n_dp):
            value = value + self.r.tile_land[k]
        return value


class Sender:
    def __init__(self):
        self.started = []

    def go(self, copy):
        copy.start()
        self.started.append(copy)

    def finish(self):
        for copy in self.started:
            copy.wait_send()


def dot_low(left, right):
    return jnp.dot(left, right, preferred_element_type=F32)


def dot_left(left, right):
    return lax.dot_general(left, right, (((0,), (0,)), ((), ())), preferred_element_type=F32)


def dot_right(left, right):
    return lax.dot_general(left, right, (((1,), (1,)), ((), ())), preferred_element_type=F32)


def norm_forward(value, gain, shift):
    mean = jnp.mean(value, axis=-1, keepdims=True)
    centered = value - mean
    inverse = lax.rsqrt(jnp.mean(centered * centered, axis=-1, keepdims=True) + norm_eps)
    normal = centered * inverse
    return normal * gain + shift, normal, inverse


def norm_backward(gradient, normal, inverse, gain):
    gain_gradient = jnp.sum(gradient * normal, axis=0)
    shift_gradient = jnp.sum(gradient, axis=0)
    scaled = gradient * gain
    inner = jnp.mean(scaled, axis=-1, keepdims=True) + normal * jnp.mean(
        scaled * normal, axis=-1, keepdims=True
    )
    return inverse * (scaled - inner), gain_gradient, shift_gradient


def gelu(value):
    return 0.5 * value * (1.0 + lax.erf(value * 0.7071067811865476))


def gelu_slope(value):
    cdf = 0.5 * (1.0 + lax.erf(value * 0.7071067811865476))
    return cdf + value * jnp.exp(-0.5 * value * value) * 0.3989422804014327


def rows_dot(left, right):
    return jnp.dot(left, right, preferred_element_type=F32)


def norm_rows(value):
    mean = jnp.mean(value, axis=-1, keepdims=True)
    centered = value - mean
    inverse = lax.rsqrt(jnp.mean(centered * centered, axis=-1, keepdims=True) + norm_eps)
    return centered * inverse, inverse


def norm_rows_backward(gradient, normal, inverse, gain):
    scaled = gradient * gain
    inner = jnp.mean(scaled, axis=-1, keepdims=True) + normal * jnp.mean(
        scaled * normal, axis=-1, keepdims=True
    )
    return inverse * (scaled - inner)


def column_sum(value):
    return jnp.sum(value, axis=0, keepdims=True)


def gelu_both(value):
    cdf = 0.5 * (1.0 + lax.erf(value * 0.7071067811865476))
    slope = cdf + value * jnp.exp(-0.5 * value * value) * 0.3989422804014327
    return value * cdf, slope


def aligned(start, size, to=128):
    return pl.ds(pl.multiple_of(start, to), size)


class Refs:
    def __init__(self, names, refs):
        for name, ref in zip(names, refs, strict=True):
            setattr(self, name, ref)


def join_pieces():
    spans = ((0, 3 * D), (VEC_AT, NVEC), (OUT_AT, D), (UP_AT, FF), (TRANS_AT, D))
    pieces = []
    for first, width in JOIN_PARTS:
        for low in (first, first + width // 2):
            high = low + width // 2
            for matrix, (start, size) in enumerate(spans):
                a, b = max(low, start), min(high, start + size)
                if a < b:
                    pieces.append((matrix, a - start, a, b - a))
    return pieces


def packed_at(column):
    for first, width in JOIN_PARTS:
        half = width // 2
        if first <= column < first + width:
            side, inside = divmod(column - first, half)
            return side, first // 2 + inside
    raise ValueError


class Gather:
    def __init__(self, place, r):
        self.place, self.r, self.sender = place, r, Sender()
        n_vocab = place.n_vocab
        self.t_rows, self.t_cols = r.table_t.shape
        self.rows = r.packed.shape[0] // 2
        self.d_rows = r.down_low.shape[0]
        piece = self.t_cols // T_PARTS
        rows = self.rows
        self.chunks = []
        self.z_moves = []
        for q in range(T_PARTS):
            first = piece * n_vocab * q
            where = (
                aligned(place.dp * self.t_rows, self.t_rows, 16),
                aligned(first + place.z * piece, piece),
            )
            view = block_view(r.table, self.t_rows, 0, self.t_rows, first, n_vocab * piece)
            self.chunks.append((view, None))
            self.z_moves.append((r.table_t.at[:, pl.ds(piece * q, piece)], r.table.at[where]))
        for part in JOIN_PARTS[:-1]:
            self.add_part(*part)
        d_rows = self.d_rows
        for first, width in DOWN_PARTS:
            dst = r.down.at[aligned((place.dp * n_vocab + place.z) * d_rows, d_rows, 16), pl.ds(first, width)]
            view = block_view(r.down, d_rows * n_vocab, 0, d_rows * n_vocab, first, width)
            self.chunks.append((view, None))
            self.z_moves.append((r.down_low.at[:, pl.ds(first, width)], dst))
        self.add_part(*JOIN_PARTS[-1])
        self.late = len(self.chunks)

    def add_part(self, first, width):
        place, r, rows = self.place, self.r, self.rows
        cols = pl.ds(first // 2, width // 2)
        view = block_view(r.join, rows * place.n_vocab, 0, rows * place.n_vocab, first, width)
        assemble = functools.partial(self.assemble, first, width)
        self.chunks.append((view, assemble))
        self.z_moves.append((r.packed.at[:, cols], r.stage.at[place.z, :, cols]))

    def place_own(self):
        for src, dst in self.z_moves[:T_PARTS]:
            dst[...] = src[...]

    def place_packed(self):
        self.r.stage[self.place.z] = self.r.packed[...]

    def place_down(self):
        place, r, d_rows = self.place, self.r, self.d_rows
        r.down[aligned((place.dp * place.n_vocab + place.z) * d_rows, d_rows, 16), :] = r.down_low[...]

    def z_copies(self, slot):
        place, r = self.place, self.r
        src, dst = self.z_moves[slot]
        return [
            remote(src, dst, r.z_send.at[slot, k - 1], r.z_recv.at[slot, k - 1], (place.dp, place.along(k)))
            for k in range(1, place.n_vocab)
        ]

    def along_z(self, *slots):
        for slot in slots:
            for copy in self.z_copies(slot):
                self.sender.go(copy)

    def assemble(self, first, width):
        place, r, rows = self.place, self.r, self.rows
        half = width // 2
        at = first // 2
        lefts, rights = [], []
        for k in range(place.n_vocab):
            piece = r.stage[k, :, at : at + half].astype(F32)
            lefts.append(piece[:rows])
            rights.append(piece[rows:])
        where = aligned(place.dp * rows * place.n_vocab, rows * place.n_vocab, 16)
        r.join[where, first : first + half] = jnp.concatenate(lefts, axis=0).astype(BF)
        r.join[where, first + half : first + width] = jnp.concatenate(rights, axis=0).astype(BF)

    def move(self, i, k, arriving):
        place, r = self.place, self.r
        if i == self.late:
            d_rows = self.d_rows
            if k < 3:
                view = block_view(
                    r.down, d_rows * place.n_vocab, place.z * d_rows, d_rows, 0, LATE
                )
            else:
                view = block_view(r.down, d_rows * place.n_vocab, 0, d_rows * place.n_vocab, 0, LATE)
        else:
            view = self.chunks[i][0]
        one, two = self.directions(i)
        own, a, b = place.dp, place.across(one), place.across(two)
        ab = a + b - own
        if k < 3:
            block = (a, b, ab)[k] if arriving else (own, own, a)[k]
            which = (one, two, two)[k]
        else:
            block = (own, a, b, ab)[k - 3] + (place.step_core if arriving else 0)
            which = CORE
        return remote(view(block), view(block), r.d_send.at[i, k], r.d_recv.at[i, k], place.device(which))

    def directions(self, i):
        return (X, Y) if GATHER_X[i] == "x" else (Y, X)

    def send(self, i, *which):
        for k in which:
            self.sender.go(self.move(i, k, False))

    def arrive(self, i, *which):
        for k in which:
            self.move(i, k, True).wait_recv()

    def late_copies(self, arriving):
        place, r, d_rows = self.place, self.r, self.d_rows
        one, two = self.directions(self.late)
        a, b = place.across(one), place.across(two)
        copies = []
        for j, block in enumerate((place.dp, a, b, a + b - place.dp)):
            for k in range(1, place.n_vocab):
                z = place.along(place.n_vocab - k) if arriving else place.z
                at = r.down.at[aligned((block * place.n_vocab + z) * d_rows, d_rows, 16), pl.ds(0, LATE)]
                copies.append(
                    remote(at, at, r.l_send.at[j, k - 1], r.l_recv.at[j, k - 1], (place.dp, place.along(k)))
                )
        return copies

    def after_z(self, i):
        for copy in self.z_copies(i):
            copy.wait_recv()
        if self.chunks[i][1] is not None:
            self.chunks[i][1]()
        self.send(i, 0, 1, 3)

    def after_one(self, i):
        self.arrive(i, 0)
        self.send(i, 2)
        if i != self.late:
            self.send(i, 4)

    def after_two(self, i):
        self.arrive(i, 1)
        if i != self.late:
            self.send(i, 5)

    def after_both(self, i):
        self.arrive(i, 2)
        if i != self.late:
            self.send(i, 6)
        else:
            for copy in self.late_copies(False):
                self.sender.go(copy)
            self.along_z(*range(Z_TAIL, Z_SLOTS))

    def after_late(self, i):
        for copy in self.late_copies(True):
            copy.wait_recv()
        self.send(i, 3, 4, 5, 6)

    def go_on(self, steps):
        for kind, i in steps:
            (self.after_z, self.after_one, self.after_two, self.after_both, self.after_late)[kind](i)

    def need(self, *which):
        for i in which:
            self.arrive(i, 3, 4, 5, 6)


N_CHUNKS = T_PARTS + len(JOIN_PARTS) + len(DOWN_PARTS) + 1
Z_SLOTS = N_CHUNKS - 1
GATHER_PLAN = (
    (
        (2, 17), (1, 17), (0, 0), (0, 1), (1, 0), (0, 2), (0, 3), (0, 4), (2, 0), (3, 17), (1, 1), (0, 5),
        (1, 2), (0, 6), (0, 7), (1, 3), (0, 8), (2, 1), (2, 2), (2, 3), (2, 4), (1, 4), (3, 0), (3, 1), (1, 5),
        (0, 9), (2, 5), (2, 6), (3, 2), (2, 7), (1, 6),
    ),
    (
        (1, 8), (1, 7), (0, 10), (0, 11), (3, 5), (2, 8), (3, 3), (3, 4), (1, 9),
    ),
    (
        (0, 12), (3, 6), (3, 7), (2, 9), (3, 8),
    ),
    (
        (2, 10), (1, 10), (2, 11), (1, 11), (4, 17), (1, 12), (3, 9), (3, 10), (0, 13), (2, 12),
    ),
    (
        (0, 14), (3, 11),
    ),
    (
        (0, 15), (2, 13), (3, 12),
    ),
    (
        (1, 14), (1, 13), (0, 16),
    ),
    (
        (2, 15), (2, 14),
    ),
    (
        (1, 15),
    ),
    (
        (3, 13),
    ),
    (
        (3, 14), (1, 16),
    ),
    (
        (2, 16), (3, 15), (3, 16),
    ),
    (),
    (),
)
Z_TAIL = T_PARTS + 4


N_FORWARD_IN = 11


def saved_shapes(rows, d_rows, tokens, picked, t_cols_all):
    return dict(
        join=((rows, JOIN), BF),
        down=((d_rows, D), BF),
        normal0=((tokens, D), BF),
        inverse0=((tokens, 1), F32),
        x0_low=((tokens, D), BF),
        keys=((tokens, D), BF),
        values=((tokens, D), BF),
        query=((picked, D), BF),
        x0_rows=((picked, D), BF),
        att=((picked, D), BF),
        normal1=((picked, D), F32),
        inverse1=((picked, 1), F32),
        x1_low=((picked, D), BF),
        hidden=((picked, FF), BF),
        slope=((picked, FF), BF),
        x2_low=((picked, D), BF),
        d_trans=((picked, D), BF),
        d_two=((picked, D), F32),
        d_logits=((picked, t_cols_all), BF),
        latent=((picked, D), BF),
        g_vec=((16, D), F32),
        vec=((16, D), F32),
        col_ids=((tokens, 1), jnp.int32),
        spots=((picked, 1), jnp.int32),
    )


def tile_scratch(n_dp, n_vocab):
    dma = pltpu.SemaphoreType.DMA
    return dict(
        tiles=pltpu.VMEM((2, 8, 128), F32),
        tile_land=pltpu.VMEM((n_dp, 8, 128), F32),
        tile_ring=pltpu.VMEM((n_vocab, 8, 128), F32),
        tile_send=dma((n_dp + n_vocab - 2,)),
        tile_recv=dma((n_dp + n_vocab - 2,)),
    )


def whole_part(value, by):
    return jnp.floor((value + 0.5) * (1.0 / by))


def forward_kernel(n_dp, n_vocab, names, out_names, *refs):
    r = Refs(names, refs[:N_FORWARD_IN] + refs[N_FORWARD_IN + len(out_names) + 2 :])
    out = Refs(out_names, refs[N_FORWARD_IN : N_FORWARD_IN + len(out_names)])
    counts_out, loss_out = refs[N_FORWARD_IN + len(out_names) : N_FORWARD_IN + len(out_names) + 2]
    seqs, seq_len = r.tokens.shape
    tokens = seqs * seq_len
    picked = r.spots.shape[0]
    slots = picked // seqs
    block = r.table_in.shape[1]
    place = Place(n_vocab)

    def prepare_table():
        full = block // 128 * 128
        r.table_t[:, :full] = r.table_in[:, :full].astype(BF)
        if full < r.table_t.shape[1]:
            r.table_rest[...] = jnp.zeros_like(r.table_rest)
            r.table_rest[:, : block - full] = r.table_in[:, full:]
            r.table_t[:, full:] = r.table_rest[...].astype(BF)

    def prepare_packed():
        r.vec_rest[...] = jnp.zeros_like(r.vec_rest)
        rows = r.packed.shape[0] // 2
        r.vec_rows[...] = jnp.zeros_like(r.vec_rows)
        r.vec_rows[:NVEC, :rows] = r.vectors[...]
        r.vec_rest[:, :16] = r.vec_rows[...].T[:rows, :]
        sources = (r.qkv_w, r.vec_rest, r.out_w, r.up_w, r.trans_w)
        spans = ((0, 3 * D), (VEC_AT, OUT_AT - VEC_AT), (OUT_AT, D), (UP_AT, FF), (TRANS_AT, D))

        def read(low, high):
            found = []
            for source, (start, size) in zip(sources, spans, strict=True):
                a, b = max(low, start), min(high, start + size)
                if a < b:
                    found.append(source[:, a - start : b - start])
            return found[0] if len(found) == 1 else jnp.concatenate(found, axis=1)

        for first, width in JOIN_PARTS:
            half = width // 2
            both = jnp.concatenate([read(first, first + half), read(first + half, first + width)], axis=0)
            r.packed[:, first // 2 : first // 2 + half] = both.astype(BF)

    def prepare_ids():
        piece = part_cols(r.table_t.shape[1])
        token = r.tokens[...].astype(F32)
        owner = whole_part(token, block)
        row = token - owner * block
        part = whole_part(row, piece)
        column = part * (piece * n_vocab) + owner * piece + (row - part * piece)
        r.wide_rows[...] = jnp.full(r.wide_rows.shape, float(seq_len), F32)
        r.wide_rows[:seqs, : r.picks.shape[1]] = r.picks[...].astype(F32)
        spots = r.wide_rows[...].T
        lane = lax.broadcasted_iota(jnp.int32, (slots, 128), 1)
        masked_columns = []
        for s in range(seqs):
            rows = slice(s * slots, (s + 1) * slots)
            spot = spots[:slots, s : s + 1]
            position = lax.broadcasted_iota(jnp.int32, (slots, seq_len), 1).astype(F32)
            here = spot == position
            r.targets[rows, :] = jnp.sum(
                jnp.where(here, column[s : s + 1, :], 0.0), axis=-1, keepdims=True
            ).astype(jnp.int32)
            live = spot < float(seq_len)
            r.spots[rows, :] = jnp.where(live, spot, -1.0).astype(jnp.int32)
            kind = r.species[s] == lane
            r.own_kinds[rows, :] = jnp.where(kind & live, 1.0, 0.0)
            masked = jnp.max(jnp.where(here, 1.0, 0.0), axis=0, keepdims=True)
            masked_columns.append(jnp.where(masked > 0.0, -1.0, column[s : s + 1, :]))
        masked_columns.append(jnp.zeros((8 - seqs, seq_len), F32))
        turned = jnp.concatenate(masked_columns, axis=0).T
        for s in range(seqs):
            r.col_ids[s * seq_len : (s + 1) * seq_len, :] = turned[:, s : s + 1].astype(jnp.int32)

    saves = []

    def save(src, dst, *cols):
        if cols:
            src, dst = src.at[:, pl.ds(*cols)], dst.at[:, pl.ds(*cols)]
        copy = pltpu.make_async_copy(src, dst, r.save_sem.at[len(saves)])
        copy.start()
        saves.append(copy)

    def embed(q):
        width = r.table.shape[1] // 3
        first = q * width

        def step(i, carry):
            at = aligned(i * 256, 256)
            ids = r.col_ids[at, :]
            onehot = (ids == lax.broadcasted_iota(jnp.int32, (256, width), 1) + first).astype(BF)
            part = dot_right(onehot, r.table[:, first : first + width])
            r.embedded[at, :] = part if q == 0 else part + r.embedded[at, :]
            return carry

        lax.fori_loop(0, tokens // 256, step, 0)

    def first_norm():
        columns = r.join[:, VEC_AT : VEC_AT + 128].astype(F32).T
        r.vec[...] = columns[:16]

        def step(i, carry):
            at = aligned(i * 128, 128)
            value = jnp.where(r.col_ids[at, :] < 0, r.vec[13:14, :], r.embedded[at, :])
            normal, inverse = norm_rows(value)
            stream = normal * r.vec[0:1, :] + r.vec[1:2, :]
            high = stream.astype(BF)
            r.normal0[at, :] = normal.astype(BF)
            r.inverse0[at, :] = inverse
            r.x0_low[at, :] = high
            r.x0_rest[at, :] = (stream - high.astype(F32)).astype(BF)
            return carry

        lax.fori_loop(0, tokens // 128, step, 0)

    def project():
        def step(i, carry):
            at = aligned(i * 256, 256)
            low = r.x0_low[at, :]
            r.keys[at, :] = rows_dot(low, r.join[:, D : 2 * D]).astype(BF)
            r.values[at, :] = (rows_dot(low, r.join[:, 2 * D : 3 * D]) + r.vec[9:10, :]).astype(BF)
            return carry

        lax.fori_loop(0, tokens // 256, step, 0)
        for s in range(seqs):
            rows = slice(s * slots, (s + 1) * slots)
            seq = slice(s * seq_len, (s + 1) * seq_len)
            pick = (r.spots[rows, :] == lax.broadcasted_iota(jnp.int32, (slots, seq_len), 1)).astype(BF)
            high = rows_dot(pick, r.x0_low[seq, :])
            r.stream[rows, :] = high + rows_dot(pick, r.x0_rest[seq, :])
            r.x0_rows[rows, :] = high.astype(BF)
        r.query[...] = (rows_dot(r.x0_rows[...], r.join[:, :D]) + r.vec[8:9, :]).astype(BF)

    def attend(low, high):
        lane = lax.broadcasted_iota(jnp.int32, (slots, 128), 1)

        def step(j, carry):
            lanes = aligned(j * 128, 128)
            for s in range(seqs):
                rows = slice(s * slots, (s + 1) * slots)
                seq = slice(s * seq_len, (s + 1) * seq_len)
                q2 = r.query[rows, lanes]
                k2 = r.keys[seq, lanes]
                v2 = r.values[seq, lanes]
                parts = []
                for a in range(2):
                    mine = (lane >= HD) if a else (lane < HD)
                    scores = dot_right(jnp.where(mine, q2, jnp.zeros_like(q2)), k2) * HD ** (-0.5)
                    top = jnp.max(scores, axis=-1, keepdims=True)
                    expo = jnp.exp(scores - top)
                    total = jnp.sum(expo, axis=-1, keepdims=True)
                    parts.append(rows_dot((expo * (1.0 / total)).astype(BF), v2))
                r.att[rows, lanes] = jnp.where(lane < HD, parts[0], parts[1]).astype(BF)
            return carry

        lax.fori_loop(low, high, step, 0)

    def after_attention():
        value = r.stream[...] + (rows_dot(r.att[...], r.join[:, OUT_AT : OUT_AT + D]) + r.vec[10:11, :])
        normal, inverse = norm_rows(value)
        r.normal1[...] = normal
        r.inverse1[...] = inverse
        stream = normal * r.vec[2:3, :] + r.vec[3:4, :]
        r.stream[...] = stream
        r.x1_low[...] = stream.astype(BF)

    def feed_up(first):
        def step(j, carry):
            cols = aligned(j * 512, 512)
            act, slope = gelu_both(rows_dot(r.x1_low[...], r.join[:, aligned(UP_AT + j * 512, 512)]))
            r.hidden[:, cols] = act.astype(BF)
            r.slope[:, cols] = slope.astype(BF)
            return carry

        lax.fori_loop(3 * first, 3 * first + 3, step, 0)

    def feed_down():
        value = r.stream[...] + (rows_dot(r.hidden[...], r.down[...]) + r.vec[11:12, :])
        normal, inverse = norm_rows(value)
        r.normal2[...] = normal
        r.inverse2[...] = inverse
        r.x2_low[...] = (normal * r.vec[4:5, :] + r.vec[5:6, :]).astype(BF)

    def head(counts):
        act, slope3 = gelu_both(
            rows_dot(r.x2_low[...], r.join[:, TRANS_AT : TRANS_AT + D]) + r.vec[12:13, :]
        )
        normal3, inverse3 = norm_rows(act)
        r.stream[...] = normal3
        latent = (normal3 * r.vec[6:7, :] + r.vec[7:8, :]).astype(BF)
        r.latent[...] = latent
        save(r.latent, out.latent)
        steps = 6
        width = r.table.shape[1] // steps

        top = jnp.full((picked, 1), floor_value, F32)
        total = jnp.zeros((picked, 1), F32)
        hit = jnp.zeros((picked, 1), F32)
        for i in range(steps):
            cols = slice(i * width, (i + 1) * width)
            logits = rows_dot(latent, r.table[:, cols])
            logits = jnp.where(r.col_floor[:, cols] == 0.0, logits, floor_value)
            r.logits[:, cols] = logits
            column = lax.broadcasted_iota(jnp.int32, (picked, width), 1) + i * width
            hit = hit + jnp.sum(jnp.where(column == r.targets[...], logits, 0.0), axis=-1, keepdims=True)
            higher = jnp.maximum(top, jnp.max(logits, axis=-1, keepdims=True))
            total = total * jnp.exp(top - higher) + jnp.sum(jnp.exp(logits - higher), axis=-1, keepdims=True)
            top = higher
        spread = top + jnp.log(total)
        loss_rows = spread - hit
        here = counts > 0.0
        present = jnp.sum(here.astype(F32), axis=-1, keepdims=True)
        inverse = jnp.where(here, 1.0 / jnp.maximum(counts, 1.0), 0.0)
        weight = jnp.sum(r.own_kinds[...] * inverse, axis=-1, keepdims=True)
        loss_out[...] = jnp.broadcast_to(column_sum(weight * loss_rows), (8, 128))
        weight = weight / present
        d_latent = jnp.zeros((picked, D), F32)
        for i in range(steps):
            cols = slice(i * width, (i + 1) * width)
            column = lax.broadcasted_iota(jnp.int32, (picked, width), 1) + i * width
            d_logits = weight * jnp.exp(r.logits[:, cols] - spread)
            d_logits = (d_logits - jnp.where(column == r.targets[...], weight, 0.0)).astype(BF)
            r.d_logits[:, cols] = d_logits
            save(r.d_logits, out.d_logits, i * width, width)
            d_latent = d_latent + dot_right(d_logits, r.table[:, cols])
        normal3 = r.stream[...]
        r.g_vec[6:7, :] = column_sum(d_latent * normal3)
        r.g_vec[7:8, :] = column_sum(d_latent)
        d_act = norm_rows_backward(d_latent, normal3, inverse3, r.vec[6:7, :])
        d_trans = (d_act * slope3).astype(BF)
        r.d_trans[...] = d_trans
        r.g_vec[12:13, :] = column_sum(d_trans.astype(F32))
        d_two = dot_right(d_trans, r.join[:, TRANS_AT : TRANS_AT + D])
        normal2 = r.normal2[...]
        r.g_vec[4:5, :] = column_sum(d_two * normal2)
        r.g_vec[5:6, :] = column_sum(d_two)
        r.d_two[...] = norm_rows_backward(d_two, normal2, r.inverse2[...], r.vec[4:5, :])

    gather = Gather(place, r)
    place.hail(n_dp)
    prepare_table()
    place.hear(n_dp)
    gather.along_z(0)
    r.down_low[...] = r.down_w[...].astype(BF)
    gather.place_down()
    gather.send(gather.late, 0, 1)
    gather.along_z(*range(1, T_PARTS))
    gather.place_own()
    plan = iter(GATHER_PLAN)
    first = next(plan)
    gather.go_on(first[:3])
    prepare_packed()
    gather.place_packed()
    gather.along_z(*range(T_PARTS, Z_TAIL))
    gather.go_on(first[3:24])
    prepare_ids()
    r.g_vec[...] = jnp.zeros_like(r.g_vec)
    counting = TileSum(place, n_dp, r)
    counting.begin(jnp.broadcast_to(column_sum(r.own_kinds[...]), (8, 128)))
    gather.go_on(first[24:])
    thirds = T_PARTS // 3
    for q in range(3):
        gather.need(*range(thirds * q, thirds * q + thirds))
        embed(q)
        gather.go_on(next(plan))
    at = T_PARTS
    gather.need(at, at + 1)
    first_norm()
    save(r.vec, out.vec)
    save(r.col_ids, out.col_ids)
    save(r.spots, out.spots)
    save(r.normal0, out.normal0)
    save(r.inverse0, out.inverse0)
    save(r.x0_low, out.x0_low)
    save(r.join, out.join, 0, OUT_AT)
    gather.go_on(next(plan))
    project()
    save(r.keys, out.keys)
    save(r.values, out.values)
    save(r.query, out.query)
    save(r.x0_rows, out.x0_rows)
    counting.go_on()
    gather.go_on(next(plan))
    for pair in range(0, HEADS // 2, 2):
        attend(pair, pair + 2)
        gather.go_on(next(plan))
    save(r.att, out.att)
    gather.need(at + 2)
    after_attention()
    save(r.normal1, out.normal1)
    save(r.inverse1, out.inverse1)
    save(r.x1_low, out.x1_low)
    gather.go_on(next(plan))
    for part in range(2):
        gather.need(at + 3 + part)
        feed_up(part)
        gather.go_on(next(plan))
    save(r.join, out.join, OUT_AT, TRANS_AT - OUT_AT)
    save(r.hidden, out.hidden)
    save(r.slope, out.slope)
    counts = counting.total()
    counts_out[...] = counts
    gather.need(at + 5, at + 6, gather.late)
    feed_down()
    save(r.down, out.down)
    save(r.x2_low, out.x2_low)
    gather.go_on(next(plan))
    gather.need(at + 7)
    save(r.join, out.join, TRANS_AT, D)
    head(counts[0:1, :])
    gather.go_on(next(plan))
    for src, dst in (
        (r.d_trans, out.d_trans), (r.d_two, out.d_two), (r.g_vec, out.g_vec),
    ):
        save(src, dst)
    gather.sender.finish()
    for copy in saves:
        copy.wait()


def forward(inputs, n_dp, n_vocab):
    rows = inputs["qkv_w"].shape[0]
    columns, block = inputs["table_in"].shape
    wide = padded(block)
    d_rows = inputs["down_w"].shape[0]
    seqs, seq_len = inputs["tokens"].shape
    tokens, picked = seqs * seq_len, seqs * 128
    table_shape = (D, wide * n_vocab)
    shapes = saved_shapes(rows * n_dp * n_vocab, d_rows * n_dp * n_vocab, tokens, picked, wide * n_vocab)
    dma = pltpu.SemaphoreType.DMA
    scratch = {name: pltpu.VMEM(*shape) for name, shape in shapes.items()}
    scratch.update(
        table=pltpu.VMEM(table_shape, BF),
        table_t=pltpu.VMEM((columns, wide), BF),
        table_rest=pltpu.VMEM((columns, 128), F32),
        vec_rows=pltpu.VMEM((16, 128), F32),
        packed=pltpu.VMEM((2 * rows, JOIN // 2), BF),
        vec_rest=pltpu.VMEM((rows, OUT_AT - VEC_AT), F32),
        down_low=pltpu.VMEM((d_rows, D), BF),
        wide_rows=pltpu.VMEM((8, 128), F32),
        targets=pltpu.VMEM((picked, 1), jnp.int32),
        own_kinds=pltpu.VMEM((picked, 128), F32),
        stage=pltpu.VMEM((n_vocab, 2 * rows, JOIN // 2), BF),
        embedded=pltpu.VMEM((tokens, D), F32),
        x0_rest=pltpu.VMEM((tokens, D), BF),
        stream=pltpu.VMEM((picked, D), F32),
        normal2=pltpu.VMEM((picked, D), F32),
        inverse2=pltpu.VMEM((picked, 1), F32),
        logits=pltpu.VMEM((picked, wide * n_vocab), F32),
        z_send=dma((Z_SLOTS, n_vocab - 1)),
        z_recv=dma((Z_SLOTS, n_vocab - 1)),
        l_send=dma((4, n_vocab - 1)),
        l_recv=dma((4, n_vocab - 1)),
        d_send=dma((N_CHUNKS, 7)),
        d_recv=dma((N_CHUNKS, 7)),
        save_sem=dma((len(shapes) + 8,)),
        **tile_scratch(n_dp, n_vocab),
    )
    vmem = pl.BlockSpec(memory_space=pltpu.VMEM)
    anywhere = pl.BlockSpec(memory_space=pl.ANY)
    tile = jax.ShapeDtypeStruct((8, 128), F32)
    names = tuple(inputs) + tuple(scratch)
    smem = pl.BlockSpec(memory_space=pltpu.SMEM)
    outs = pl.pallas_call(
        functools.partial(forward_kernel, n_dp, n_vocab, names, tuple(shapes)),
        out_shape=tuple(jax.ShapeDtypeStruct(*shape) for shape in shapes.values()) + (tile, tile),
        in_specs=[smem if name == "species" else vmem for name in inputs],
        out_specs=(anywhere,) * len(shapes) + (vmem, vmem),
        scratch_shapes=list(scratch.values()),
        compiler_params=pltpu.CompilerParams(
            collective_id=0, has_side_effects=True, vmem_limit_bytes=VMEM_LIMIT
        ),
    )(*inputs.values())
    return dict(zip(shapes, outs[:-2], strict=True)), outs[-2], outs[-1]


JOINED, DOWN, TABLE = range(3)
REDUCE_ORDER = (
    (JOINED, 5), (JOINED, 3), (JOINED, 4), (DOWN, -1), (DOWN, 0), (DOWN, 1), (JOINED, 2), (JOINED, 0), (JOINED, 1),
) + tuple((TABLE, j) for j in range(T_PARTS))


REDUCE_PLAN = (
    (
        (0, 0),
    ),
    (
        (0, 1), (1, 0),
    ),
    (
        (0, 2),
    ),
    (
        (0, 3), (0, 4), (1, 1),
    ),
    (
        (0, 5),
    ),
    (
        (0, 6), (2, 0), (1, 2),
    ),
    (),
    (
        (3, 0),
    ),
    (
        (1, 5),
    ),
    (),
    (
        (2, 1),
    ),
    (),
    (),
    (
        (2, 2),
    ),
    (
        (1, 3), (1, 4),
    ),
    (),
    (
        (3, 1), (2, 5),
    ),
    (
        (1, 6),
    ),
    (),
    (
        (0, 7), (0, 8),
    ),
    (
        (3, 2), (4, 3),
    ),
    (
        (0, 9), (2, 4),
    ),
    (
        (0, 10),
    ),
    (
        (0, 11), (1, 7),
    ),
    (
        (0, 12), (1, 8), (2, 6),
    ),
    (
        (0, 13), (3, 5),
    ),
    (
        (0, 14), (2, 3),
    ),
    (
        (0, 15), (3, 4),
    ),
    (
        (0, 16),
    ),
    (
        (0, 17),
    ),
    (
        (2, 7), (1, 10), (2, 8), (3, 3), (1, 9), (3, 6), (3, 7), (2, 10), (1, 11), (1, 12), (2, 9), (3, 8),
        (1, 13), (3, 10), (1, 14), (2, 11), (2, 12), (3, 9), (1, 15), (1, 17), (2, 13), (2, 14), (3, 11),
        (3, 12), (1, 16), (2, 15), (2, 17), (3, 14), (3, 13), (3, 15), (2, 16), (3, 17), (3, 16),
    ),
)


class Reduce:
    def __init__(self, place, r, t_cols, from_core, from_two, from_one):
        self.place, self.r, self.sender = place, r, Sender()
        self.from_core, self.from_two, self.from_one = from_core, from_two, from_one
        n_vocab = place.n_vocab
        rows = r.join_out.shape[0] // 2
        d_rows = r.down_out.shape[0]
        t_rows = r.table_out.shape[0]
        piece = t_cols // T_PARTS
        self.rows, self.d_rows, self.t_rows, self.piece = rows, d_rows, t_rows, piece
        self.chunks = []
        for kind, j in REDUCE_ORDER:
            if kind == JOINED:
                first, width = JOIN_PARTS[j]
                view = block_view(r.join, rows * n_vocab, 0, rows * n_vocab, first, width)
            elif kind == DOWN:
                first, width = R_DOWN_PARTS[j] if j >= 0 else (0, R_LATE)
                view = block_view(r.down, d_rows * n_vocab, 0, d_rows * n_vocab, first, width)
            else:
                view = block_view(r.table, t_rows, 0, t_rows, n_vocab * piece * j, n_vocab * piece)
            narrow = view
            if (kind, j) == (DOWN, -1):
                narrow = block_view(r.down, d_rows * n_vocab, place.z * d_rows, d_rows, 0, R_LATE)
            self.chunks.append(((kind, j), view, narrow))
        self.jobs = {}

    def blocks(self, i):
        place = self.place
        one, two = (X, Y) if REDUCE_X[i] == "x" else (Y, X)
        own, a, b = place.dp, place.across(one), place.across(two)
        return one, two, (own, a, b, a + b - own)

    def add_into(self, target, *sources):
        def step(i, carry):
            at = aligned(i * 16, 16, 16)
            if len(sources) == 1:
                target[at, :] = target[at, :] + sources[0][at, :]
            else:
                total = target[at, :].astype(F32)
                for source in sources:
                    total = total + source[at, :].astype(F32)
                target[at, :] = total.astype(BF)
            return carry

        lax.fori_loop(0, target.shape[0] // 16, step, 0)

    def to_core(self, i, k):
        _, _, blocks = self.blocks(i)
        block = blocks[k] + self.place.step_core
        r, place = self.r, self.place
        return remote(
            self.chunks[i][1](block), self.from_core[i].at[k], r.d_send.at[i, k], r.d_recv.at[i, k],
            place.device(CORE),
        )

    def to_two(self, i, k):
        _, two, blocks = self.blocks(i)
        r, place = self.r, self.place
        return remote(
            self.chunks[i][2](blocks[2 + k]), self.from_two[i].at[k], r.d_send.at[i, 4 + k],
            r.d_recv.at[i, 4 + k], place.device(two),
        )

    def to_one(self, i):
        one, _, blocks = self.blocks(i)
        r, place = self.r, self.place
        return remote(
            self.chunks[i][2](blocks[1]), self.from_one[i], r.d_send.at[i, 6], r.d_recv.at[i, 6],
            place.device(one),
        )

    def late_copies(self, i):
        place, r, d_rows = self.place, self.r, self.d_rows
        _, _, blocks = self.blocks(i)
        copies = []
        for j, block in enumerate(blocks):
            for k in range(1, place.n_vocab):
                row = (block * place.n_vocab + place.along(k)) * d_rows
                copies.append(
                    remote(
                        r.down.at[aligned(row, d_rows, 16), pl.ds(0, R_LATE)], r.z_late.at[j, k - 1],
                        r.l_send.at[j, k - 1], r.l_recv.at[j, k - 1], (place.dp, place.along(k)),
                    )
                )
        return copies

    def z_copies(self, slot, src_of, dst_of):
        place, r = self.place, self.r
        return [
            remote(
                src_of(place.along(k)), dst_of(k - 1), r.z_send.at[slot, k - 1], r.z_recv.at[slot, k - 1],
                (place.dp, place.along(k)),
            )
            for k in range(1, place.n_vocab)
        ]

    def pack(self, first, width):
        r, rows, n_vocab = self.r, self.rows, self.place.n_vocab
        half = width // 2
        at = first // 2
        where = aligned(self.place.dp * rows * n_vocab, rows * n_vocab, 16)
        block = r.join[where, first : first + width].astype(F32)
        for k in range(n_vocab):
            piece = block[k * rows : (k + 1) * rows]
            r.packed[k, :, at : at + half] = jnp.concatenate([piece[:, :half], piece[:, half:]], axis=0).astype(BF)

    def along_z(self, i):
        place, r = self.place, self.r
        kind, j = self.chunks[i][0]
        slot = len(self.jobs)
        if kind == JOINED:
            first, width = JOIN_PARTS[j]
            self.pack(first, width)
            cols = pl.ds(first // 2, width // 2)
            copies = self.z_copies(slot, lambda to: r.packed.at[to, :, cols], lambda k: r.z_join.at[k, :, cols])
        elif kind == DOWN:
            first, width = R_DOWN_PARTS[j]
            cols = pl.ds(first, width)
            d_rows, n_vocab = self.d_rows, place.n_vocab
            copies = self.z_copies(
                slot,
                lambda to: r.down.at[aligned((place.dp * n_vocab + to) * d_rows, d_rows, 16), cols],
                lambda k: r.z_down.at[k, :, pl.ds(first - R_LATE, width)],
            )
        else:
            piece, q = self.piece, j
            copies = self.z_copies(
                slot,
                lambda to: r.table.at[
                    aligned(place.dp * self.t_rows, self.t_rows, 16),
                    aligned(q * piece * place.n_vocab + to * piece, piece),
                ],
                lambda k: r.z_table.at[k, :, pl.ds(q * piece, piece)],
            )
        for copy in copies:
            self.sender.go(copy)
        self.jobs[i] = copies

    def is_late(self, i):
        return self.chunks[i][0] == (DOWN, -1)

    def go_on(self, steps):
        for stage, i in steps:
            (self.start, self.after_core, self.after_two, self.after_one, self.after_late)[stage](i)

    def start(self, i):
        for k in range(4):
            self.sender.go(self.to_core(i, k))

    def after_core(self, i):
        view = self.chunks[i][1]
        _, _, blocks = self.blocks(i)
        for k in (2, 3, 0, 1):
            self.to_core(i, k).wait_recv()
            self.add_into(view(blocks[k]), self.from_core[i].at[k])
            if k == 3 and not self.is_late(i):
                self.send_two(i)
        if self.is_late(i):
            for copy in self.late_copies(i):
                self.sender.go(copy)

    def after_late(self, i):
        narrow = self.chunks[i][2]
        _, _, blocks = self.blocks(i)
        for copy in self.late_copies(i):
            copy.wait_recv()
        for j in (2, 3, 0, 1):
            parts = [self.r.z_late.at[j, k] for k in range(self.place.n_vocab - 1)]
            self.add_into(narrow(blocks[j]), *parts)
            if j == 3:
                self.send_two(i)

    def send_two(self, i):
        for k in range(2):
            self.sender.go(self.to_two(i, k))

    def after_two(self, i):
        narrow = self.chunks[i][2]
        _, _, blocks = self.blocks(i)
        self.to_two(i, 1).wait_recv()
        self.add_into(narrow(blocks[1]), self.from_two[i].at[1])
        self.sender.go(self.to_one(i))
        self.to_two(i, 0).wait_recv()
        self.add_into(narrow(blocks[0]), self.from_two[i].at[0])

    def after_one(self, i):
        self.to_one(i).wait_recv()
        self.add_into(self.chunks[i][2](self.place.dp), self.from_one[i])
        if not self.is_late(i):
            self.along_z(i)

    def collect(self):
        place, r = self.place, self.r
        n_vocab = place.n_vocab

        def total(own, parts, out, cols):
            whole = own.astype(F32)
            for part in parts:
                whole = whole + part.astype(F32)
            out[:, cols] = whole
            return jnp.sum(column_sum(whole * whole), axis=-1, keepdims=True)

        square = jnp.zeros((1, 1), F32)
        rows = aligned((place.dp * n_vocab + place.z) * self.d_rows, self.d_rows, 16)
        square += total(r.down[rows, :R_LATE], (), r.down_out, slice(0, R_LATE))
        for i, ((kind, j), _, _) in enumerate(self.chunks):
            if self.is_late(i):
                continue
            for copy in self.jobs[i]:
                copy.wait_recv()
            if kind == JOINED:
                first, width = JOIN_PARTS[j]
                cols = slice(first // 2, first // 2 + width // 2)
                own = r.packed[place.z, :, cols]
                parts = [r.z_join[k, :, cols] for k in range(n_vocab - 1)]
                square += total(own, parts, r.join_out, cols)
            elif kind == DOWN:
                first, width = R_DOWN_PARTS[j]
                low = first - R_LATE
                parts = [r.z_down[k, :, low : low + width] for k in range(n_vocab - 1)]
                own = r.down[rows, first : first + width]
                square += total(own, parts, r.down_out, slice(first, first + width))
            else:
                q = j
                cols = slice(q * self.piece, (q + 1) * self.piece)
                t_rows = aligned(place.dp * self.t_rows, self.t_rows, 16)
                own = r.table[t_rows, aligned(q * self.piece * n_vocab + place.z * self.piece, self.piece)]
                parts = [r.z_table[k, :, cols] for k in range(n_vocab - 1)]
                square += total(own, parts, r.table_out, cols)
        return square


def backward_kernel(n_dp, n_vocab, in_names, names, *refs):
    given = Refs(in_names, refs[: len(in_names)])
    scratch = refs[len(in_names) :]
    n_chunks = len(REDUCE_ORDER)
    lands, scratch = scratch[-3 * n_chunks :], scratch[: -3 * n_chunks]
    r = Refs(names, scratch)
    tokens = given.col_ids.shape[0]
    picked = given.spots.shape[0]
    seqs = 2
    seq_len, slots = tokens // seqs, picked // seqs
    wide = r.table.shape[1]

    def keys_at(s):
        return r.table.at[pl.ds(0, seq_len), pl.ds(s * D, D)]

    def values_at(s):
        return r.table.at[pl.ds(0, seq_len), pl.ds((2 + s) * D, D)]

    hidden = r.table.at[pl.ds(seq_len, picked), pl.ds(0, FF)]
    query = r.table.at[pl.ds(seq_len, picked), pl.ds(FF, D)]
    x0_rows = r.table.at[pl.ds(seq_len, picked), pl.ds(FF + D, D)]
    half = FF // 2
    slopes = [r.table.at[pl.ds(s * picked, picked), pl.ds(4 * D, half)] for s in range(2)]
    count = [0]

    def load(*pairs):
        copies = []
        for src, dst in pairs:
            copies.append(pltpu.make_async_copy(src, dst, r.load_sem.at[count[0]]))
            copies[-1].start()
            count[0] += 1
        return copies

    def seq_pairs(src, dst):
        return [(src.at[pl.ds(s * seq_len, seq_len), :], dst(s)) for s in range(seqs)]

    def need(*groups):
        for copies in groups:
            for copy in copies:
                copy.wait()

    up_cols, low_cols = pl.ds(UP_AT, FF), pl.ds(0, UP_AT)
    got_trans = load((given.x2_low, r.x2_low), (given.d_trans, r.d_trans))
    got_feed = load(
        (given.d_two, r.stream), (given.x1_low, r.x1_low),
        *[(given.slope.at[:, pl.ds(s * half, half)], slopes[s]) for s in range(2)],
        (given.join.at[:, up_cols], r.join.at[:, up_cols]), (given.down, r.down),
    )
    got_hidden = load((given.hidden, hidden))
    got_out = load(
        (given.normal1, r.normal1), (given.att, r.att), (given.join.at[:, low_cols], r.join.at[:, low_cols])
    )
    got_att = load(
        *seq_pairs(given.values, values_at), *seq_pairs(given.keys, keys_at), (given.query, query)
    )
    got_first = load((given.x0_rows, x0_rows), (given.x0_low, r.x0_low), (given.normal0, r.normal0))
    got_head = load((given.d_logits, r.d_logits))

    place = Place(n_vocab)
    place.greet(n_dp)
    reduce = Reduce(
        place, r, wide // n_vocab, lands[:n_chunks], lands[n_chunks : 2 * n_chunks], lands[2 * n_chunks :]
    )
    r.g_vec[...] = given.g_vec[...]

    def gain(i):
        return given.vec[i : i + 1, :]

    def put(first, width, value):
        r.join[:, first : first + width] = value.astype(BF)

    need(got_trans)
    put(TRANS_AT, D, dot_left(r.x2_low[...], r.d_trans[...]))
    plan = iter(REDUCE_PLAN)
    reduce.go_on(next(plan))

    need(got_feed)
    d_ffn = r.stream[...].astype(BF)
    r.d_rows_low[...] = d_ffn
    r.g_vec[11:12, :] = column_sum(d_ffn.astype(F32))

    def feed(part):
        def step(j, carry):
            cols = aligned(j * D, D)
            up_at = aligned(UP_AT + part * half + j * D, D)
            d_act = dot_right(r.d_rows_low[...], r.down[aligned(part * half + j * D, D), :])
            d_hidden = (d_act * slopes[part][:, cols].astype(F32)).astype(BF)
            r.stream[...] += dot_right(d_hidden, r.join[:, up_at])
            r.join[:, up_at] = dot_left(r.x1_low[...], d_hidden).astype(BF)
            return carry

        lax.fori_loop(0, half // D, step, 0)

    feed(0)
    reduce.go_on(next(plan))
    feed(1)
    reduce.go_on(next(plan))
    need(got_hidden)

    def feed_down(first, width):
        def step(j, carry):
            rows = aligned(j * D, D)
            cols = slice(first, first + width)
            r.down[rows, cols] = dot_left(hidden[:, rows], r.d_rows_low[:, cols]).astype(BF)
            return carry

        lax.fori_loop(0, FF // D, step, 0)

    first = R_LATE + R_DOWN_PARTS[0][1]
    feed_down(0, first)
    reduce.go_on(next(plan))
    feed_down(first, D - first)
    reduce.go_on(next(plan))

    need(got_out)
    d_one = r.stream[...]
    normal1 = r.normal1[...]
    r.g_vec[2:3, :] = column_sum(d_one * normal1)
    r.g_vec[3:4, :] = column_sum(d_one)
    d_one = norm_rows_backward(d_one, normal1, given.inverse1[...], gain(2))
    r.stream[...] = d_one
    d_proj = d_one.astype(BF)
    r.g_vec[10:11, :] = column_sum(d_proj.astype(F32))
    r.x2_low[...] = dot_right(d_proj, r.join[:, OUT_AT : OUT_AT + D]).astype(BF)
    put(OUT_AT, D, dot_left(r.att[...], d_proj))
    got_latent = load((given.latent, r.att))
    reduce.go_on(next(plan))

    need(got_att)
    lane = lax.broadcasted_iota(jnp.int32, (slots, 128), 1)

    def attend(j, carry):
        lanes = aligned(j * 128, 128)
        for s in range(seqs):
            rows = slice(s * slots, (s + 1) * slots)
            q2 = query[rows, lanes]
            g2 = r.x2_low[rows, lanes]
            k2 = keys_at(s)[:, lanes]
            v2 = values_at(s)[:, lanes]
            d_q, d_k, d_v = [], None, None
            for a in range(2):
                mine = (lane >= HD) if a else (lane < HD)
                q1 = jnp.where(mine, q2, jnp.zeros_like(q2))
                g1 = jnp.where(mine, g2, jnp.zeros_like(g2))
                scores = dot_right(q1, k2) * HD ** (-0.5)
                expo = jnp.exp(scores - jnp.max(scores, axis=-1, keepdims=True))
                probs = expo * (1.0 / jnp.sum(expo, axis=-1, keepdims=True))
                d_probs = dot_right(g1, v2)
                delta = jnp.sum(d_probs * probs, axis=-1, keepdims=True)
                d_scores = (probs * (d_probs - delta)).astype(BF)
                d_q.append(rows_dot(d_scores, k2))
                more_k = dot_left(d_scores, q1)
                more_v = dot_left(probs.astype(BF), g1)
                d_k = more_k if d_k is None else d_k + more_k
                d_v = more_v if d_v is None else d_v + more_v
            r.d_trans[rows, lanes] = (jnp.where(lane < HD, d_q[0], d_q[1]) * HD ** (-0.5)).astype(BF)
            keys_at(s)[:, lanes] = (d_k * HD ** (-0.5)).astype(BF)
            values_at(s)[:, lanes] = d_v.astype(BF)
        return carry

    for pair in range(HEADS // 2):
        lax.fori_loop(pair, pair + 1, attend, 0)
        reduce.go_on(next(plan))

    need(got_first)
    d_query = r.d_trans[...]
    r.g_vec[8:9, :] = column_sum(d_query.astype(F32))
    d_rows = r.stream[...] + dot_right(d_query, r.join[:, :D])
    high = d_rows.astype(BF)
    r.d_rows_low[...] = high
    r.x1_low[...] = (d_rows - high.astype(F32)).astype(BF)
    put(0, D, dot_left(x0_rows[...], d_query))
    for i in (0, 1, 9, 13):
        r.g_vec[i : i + 1, :] = jnp.zeros((1, D), F32)

    reduce.go_on(next(plan))

    for s in range(seqs):

        def step(i, carry, s=s):
            inside = aligned(i * 256, 256)
            at = aligned(s * seq_len + i * 256, 256)
            d_v = values_at(s)[inside, :]
            r.g_vec[9:10, :] += column_sum(d_v.astype(F32))
            d_zero = dot_right(keys_at(s)[inside, :], r.join[:, D : 2 * D])
            d_zero = d_zero + dot_right(d_v, r.join[:, 2 * D : 3 * D])
            column = lax.broadcasted_iota(jnp.int32, (slots, 256), 1) + i * 256
            rows = slice(s * slots, (s + 1) * slots)
            pick = (given.spots[rows, :] == column).astype(BF)
            d_zero = d_zero + (dot_left(pick, r.d_rows_low[rows, :]) + dot_left(pick, r.x1_low[rows, :]))
            normal = r.normal0[at, :].astype(F32)
            r.g_vec[0:1, :] += column_sum(d_zero * normal)
            r.g_vec[1:2, :] += column_sum(d_zero)
            d_emb = norm_rows_backward(d_zero, normal, given.inverse0[at, :], gain(0)).astype(BF)
            r.g_vec[13:14, :] += column_sum(jnp.where(given.col_ids[at, :] < 0, d_emb.astype(F32), 0.0))
            r.normal0[at, :] = d_emb
            return carry

        for i in range(seq_len // 256):
            lax.fori_loop(i, i + 1, step, 0)
            reduce.go_on(next(plan))

    def weigh(i, carry):
        cols = aligned(i * 256, 256)
        for part, source in ((1, keys_at), (2, values_at)):
            value = sum(
                dot_left(r.x0_low[s * seq_len : (s + 1) * seq_len, :], source(s)[:, cols]) for s in range(seqs)
            )
            r.join[:, aligned(part * D + i * 256, 256)] = value.astype(BF)
        return carry

    lax.fori_loop(0, 2, weigh, 0)
    reduce.go_on(next(plan))
    lax.fori_loop(2, D // 256, weigh, 0)
    reduce.go_on(next(plan))
    columns = jnp.concatenate([r.g_vec[...], jnp.zeros((112, D), F32)], axis=0).T
    put(VEC_AT, 128, columns)
    put(VEC_AT + 128, 128, jnp.zeros((D, 128), F32))
    reduce.go_on(next(plan))

    need(got_head, got_latent)
    r.flipped[:, :tokens] = r.normal0[...].T
    r.flipped[:, tokens:] = r.att[...].T
    reduce.go_on(next(plan))
    width = wide // T_PARTS
    for j in range(T_PARTS):
        cols = slice(j * width, (j + 1) * width)
        column = lax.broadcasted_iota(jnp.int32, (tokens, width), 1) + j * width
        onehot = (given.col_ids[...] == column).astype(BF)
        value = rows_dot(r.flipped[:, :tokens], onehot) + rows_dot(r.flipped[:, tokens:], r.d_logits[:, cols])
        r.table[:, cols] = value.astype(BF)
        reduce.go_on(next(plan))
    reduce.go_on(next(plan))
    square = reduce.collect()
    row = lax.broadcasted_iota(jnp.int32, (8, 128), 0)
    summing = TileSum(place, n_dp, r)
    summing.begin(jnp.where(row == 0, square, given.loss[...]))
    summing.go_on()
    r.tile_out[...] = summing.total()
    reduce.sender.finish()


def backward(saved, loss, n_dp, n_vocab):
    rows = saved["join"].shape[0] // (n_dp * n_vocab)
    d_rows = saved["down"].shape[0] // (n_dp * n_vocab)
    t_rows = D // n_dp
    t_cols = saved["d_logits"].shape[1] // n_vocab
    tokens, picked = saved["col_ids"].shape[0], saved["spots"].shape[0]
    core_shapes, far_shapes = [], []
    for kind, j in REDUCE_ORDER:
        if kind == JOINED:
            shape = (rows * n_vocab, JOIN_PARTS[j][1])
        elif kind == DOWN:
            shape = (d_rows * n_vocab, R_DOWN_PARTS[j][1] if j >= 0 else R_LATE)
        else:
            shape = (t_rows, t_cols * n_vocab // T_PARTS)
        core_shapes.append((4,) + shape)
        far_shapes.append((d_rows, R_LATE) if (kind, j) == (DOWN, -1) else shape)
    inputs = dict(saved, loss=loss)
    inputs.pop("x0_rest", None)
    outs = dict(
        join_out=(2 * rows, JOIN // 2), down_out=(d_rows, D), table_out=(t_rows, t_cols), tile_out=(8, 128)
    )
    dma = pltpu.SemaphoreType.DMA
    rows_low = pltpu.VMEM((picked, D), BF)
    tokens_low = pltpu.VMEM((tokens, D), BF)
    scratch = dict(
        join=pltpu.VMEM(saved["join"].shape, BF),
        down=pltpu.VMEM(saved["down"].shape, BF),
        table=pltpu.VMEM((D, t_cols * n_vocab), BF),
        normal0=tokens_low,
        x0_low=tokens_low,
        att=rows_low,
        x1_low=rows_low,
        x2_low=rows_low,
        d_trans=rows_low,
        d_rows_low=rows_low,
        normal1=pltpu.VMEM((picked, D), F32),
        stream=pltpu.VMEM((picked, D), F32),
        d_logits=pltpu.VMEM(saved["d_logits"].shape, BF),
        g_vec=pltpu.VMEM((16, D), F32),
        flipped=pltpu.VMEM((D, tokens + picked), BF),
        packed=pltpu.VMEM((n_vocab, 2 * rows, JOIN // 2), BF),
        z_join=pltpu.VMEM((n_vocab - 1, 2 * rows, JOIN // 2), BF),
        z_down=pltpu.VMEM((n_vocab - 1, d_rows, D - R_LATE), BF),
        z_late=pltpu.VMEM((4, n_vocab - 1, d_rows, R_LATE), BF),
        z_table=pltpu.VMEM((n_vocab - 1, t_rows, t_cols), BF),
        load_sem=dma((len(saved) + 4,)),
        z_send=dma((Z_SLOTS, n_vocab - 1)),
        z_recv=dma((Z_SLOTS, n_vocab - 1)),
        l_send=dma((4, n_vocab - 1)),
        l_recv=dma((4, n_vocab - 1)),
        d_send=dma((N_CHUNKS, 7)),
        d_recv=dma((N_CHUNKS, 7)),
        **tile_scratch(n_dp, n_vocab),
    )
    lands = [pltpu.VMEM(shape, BF) for shape in core_shapes]
    lands += [pltpu.VMEM((2,) + shape, BF) for shape in far_shapes]
    lands += [pltpu.VMEM(shape, BF) for shape in far_shapes]
    vmem = pl.BlockSpec(memory_space=pltpu.VMEM)
    anywhere = pl.BlockSpec(memory_space=pl.ANY)
    near = set(dict(vec=0, g_vec=0, inverse0=0, inverse1=0, col_ids=0, spots=0, loss=0))
    return pl.pallas_call(
        functools.partial(backward_kernel, n_dp, n_vocab, tuple(inputs), tuple(outs) + tuple(scratch)),
        out_shape=tuple(jax.ShapeDtypeStruct(shape, F32) for shape in outs.values()),
        in_specs=[vmem if name in near else anywhere for name in inputs],
        out_specs=(vmem,) * len(outs),
        scratch_shapes=list(scratch.values()) + lands,
        compiler_params=pltpu.CompilerParams(
            collective_id=1, has_side_effects=True, vmem_limit_bytes=VMEM_LIMIT
        ),
    )(*inputs.values())


def update_kernel(n_state, *refs):
    tile, counts, g_join, g_down, g_table = refs[:5]
    states = refs[5 : 5 + 3 * n_state]
    outs = refs[5 + 3 * n_state : 5 + 7 * n_state]
    loss_out, present_out, norm_out = refs[5 + 7 * n_state :]
    norm = jnp.sqrt(tile[0:1, 0:1])
    factor = jnp.minimum(1.0, clip_limit / (norm + 1e-06))
    norm_out[0] = jnp.max(norm)
    loss_out[0] = jnp.max(tile[1:2, 0:1])
    present_out[0] = jnp.sum((counts[0:1, :] > 0.0).astype(F32))

    def advance(index, cols, gradient, rate):
        weight, first, second = (ref[:, cols] for ref in states[3 * index : 3 * index + 3])
        first, second, new = adamw(weight, first, second, gradient * factor, rate)
        targets = outs[4 * index : 4 * index + 4]
        targets[0][:, cols] = first
        targets[1][:, cols] = second
        targets[2][:, cols] = new
        targets[3][:, cols] = new.astype(targets[3].dtype)

    every = slice(None)
    block = states[0].shape[1]
    full = block // 128 * 128
    advance(0, slice(0, full), g_table[:, :full], matrix_rate)
    if full < block:
        advance(0, slice(full, block), g_table[:, full:block], matrix_rate)
    rows = g_join.shape[0] // 2
    for matrix, first, column, width in join_pieces():
        side, at = packed_at(column)
        if matrix == 1:
            square = jnp.concatenate([g_join[side * rows : (side + 1) * rows, at : at + 128], jnp.zeros((128 - rows, 128), F32)], axis=0)
            advance(2, every, square.T[:width, :rows], vector_rate)
        else:
            gradient = g_join[side * rows : (side + 1) * rows, at : at + width]
            advance(1 + matrix, slice(first, first + width), gradient, matrix_rate)
    advance(6, every, g_down[...], matrix_rate)


def update(tile, counts, g_join, g_down, g_table, states):
    vmem = pl.BlockSpec(memory_space=pltpu.VMEM)
    smem = pl.BlockSpec(memory_space=pltpu.SMEM)
    shapes = []
    for index, (weight, _, _) in enumerate(states):
        shapes += [jax.ShapeDtypeStruct(weight.shape, F32)] * 3
        shapes.append(jax.ShapeDtypeStruct(weight.shape, F32 if index == 2 else BF))
    flat = [array for state in states for array in state]
    scalars = [jax.ShapeDtypeStruct((1,), F32)] * 3
    return pl.pallas_call(
        functools.partial(update_kernel, len(states)),
        out_shape=tuple(shapes + scalars),
        in_specs=[vmem] * (5 + len(flat)),
        out_specs=(vmem,) * len(shapes) + (smem,) * 3,
        compiler_params=pltpu.CompilerParams(vmem_limit_bytes=VMEM_LIMIT),
    )(tile, counts, g_join, g_down, g_table, *flat)


def species_counts(picks, species, seq_len):
    live = (picks < seq_len).astype(F32)
    kinds = jnp.arange(NSPEC, dtype=jnp.int32)
    return jnp.sum((species[:, None] == kinds[None, :]).astype(F32) * jnp.sum(live, axis=1)[:, None], axis=0)


def local_step(tokens, picks, species, counts, join, down, table_t, col_id):
    seqs, seq_len = tokens.shape
    slots = picks.shape[1]
    w_qkv = join[:, : 3 * D]
    vec = join[:, VEC_AT : VEC_AT + NVEC].astype(F32)
    w_out = join[:, OUT_AT : OUT_AT + D]
    w_up = join[:, UP_AT : UP_AT + FF]
    w_trans = join[:, TRANS_AT : TRANS_AT + D]

    masked = jnp.any(picks[:, :, None] == jnp.arange(seq_len, dtype=jnp.int32)[None, None, :], axis=1)
    masked_flat = masked.reshape(-1)
    live = (picks < seq_len).reshape(-1)
    spot = jnp.minimum(picks, seq_len - 1)
    row_index = (spot + jnp.arange(seqs, dtype=jnp.int32)[:, None] * seq_len).reshape(-1)
    target = jnp.take_along_axis(tokens, spot, axis=1).reshape(-1)
    row_species = jnp.broadcast_to(species[:, None], picks.shape).reshape(-1)

    inputs = jnp.where(masked, -2, tokens).reshape(-1)
    onehot = (inputs[:, None] == col_id[None, :]).astype(BF)
    embedded = jnp.where(masked_flat[:, None], vec[:, 13], dot_right(onehot, table_t))
    stream_zero, normal0, inverse0 = norm_forward(embedded, vec[:, 0], vec[:, 1])
    x0_low = stream_zero.astype(BF)
    keys = dot_low(x0_low, w_qkv[:, D : 2 * D]).astype(BF)
    values = (dot_low(x0_low, w_qkv[:, 2 * D :]) + vec[:, 9]).astype(BF)
    x0_rows = stream_zero[row_index]
    x0_rows_low = x0_rows.astype(BF)
    query = (dot_low(x0_rows_low, w_qkv[:, :D]) + vec[:, 8]).astype(BF)
    q4 = query.reshape(seqs, slots, HEADS, HD)
    k4 = keys.reshape(seqs, seq_len, HEADS, HD)
    v4 = values.reshape(seqs, seq_len, HEADS, HD)
    scores = jnp.einsum("sqhd,skhd->shqk", q4, k4, preferred_element_type=F32) * HD ** (-0.5)
    probs = jax.nn.softmax(scores, axis=-1)
    probs_low = probs.astype(BF)
    att = jnp.einsum("shqk,skhd->sqhd", probs_low, v4, preferred_element_type=F32)
    att_low = att.reshape(-1, D).astype(BF)
    stream_one, normal1, inverse1 = norm_forward(
        x0_rows + dot_low(att_low, w_out) + vec[:, 10], vec[:, 2], vec[:, 3]
    )
    x1_low = stream_one.astype(BF)
    hidden = dot_low(x1_low, w_up)
    hidden_low = gelu(hidden).astype(BF)
    stream_two, normal2, inverse2 = norm_forward(
        stream_one + dot_low(hidden_low, down) + vec[:, 11], vec[:, 4], vec[:, 5]
    )
    picked_low = stream_two.astype(BF)
    trans = dot_low(picked_low, w_trans) + vec[:, 12]
    latent, normal3, inverse3 = norm_forward(gelu(trans), vec[:, 6], vec[:, 7])
    latent_low = latent.astype(BF)
    logits = dot_low(latent_low, table_t)
    logits = jnp.where(((col_id >= 0) & (col_id < VREAL))[None, :], logits, floor_value)
    top = jnp.max(logits, axis=-1, keepdims=True)
    expo = jnp.exp(logits - top)
    total = jnp.sum(expo, axis=-1, keepdims=True)
    is_target = col_id[None, :] == target[:, None]
    hit = jnp.sum(jnp.where(is_target, logits, 0.0), axis=-1)
    loss_rows = (top + jnp.log(total))[:, 0] - hit
    kinds = jnp.arange(NSPEC, dtype=jnp.int32)
    own = ((row_species[:, None] == kinds[None, :]) & live[:, None]).astype(F32)
    species_loss = jnp.sum(own * loss_rows[:, None], axis=0)
    present_mask = counts > 0
    present = jnp.sum(present_mask.astype(F32))
    inverse = jnp.where(present_mask, 1.0 / jnp.maximum(counts, 1.0), 0.0) / present
    weight = jnp.sum(own * inverse[None, :], axis=-1)
    loss_part = jnp.sum(jnp.where(present_mask, species_loss / jnp.maximum(counts, 1.0), 0.0))
    d_logits = (weight[:, None] * (expo / total - is_target.astype(F32))).astype(BF)

    d_latent = dot_right(d_logits, table_t)
    d_act, d6, d7 = norm_backward(d_latent, normal3, inverse3, vec[:, 6])
    d_trans = (d_act * gelu_slope(trans)).astype(BF)
    g_trans = dot_left(picked_low, d_trans)
    d12 = jnp.sum(d_trans.astype(F32), axis=0)
    d_two, d4, d5 = norm_backward(dot_right(d_trans, w_trans), normal2, inverse2, vec[:, 4])
    d_ffn = d_two.astype(BF)
    d11 = jnp.sum(d_ffn.astype(F32), axis=0)
    g_down = dot_left(hidden_low, d_ffn)
    d_hidden = (dot_right(d_ffn, down) * gelu_slope(hidden)).astype(BF)
    g_up = dot_left(x1_low, d_hidden)
    d_one, d2, d3 = norm_backward(d_two + dot_right(d_hidden, w_up), normal1, inverse1, vec[:, 2])
    d_proj = d_one.astype(BF)
    d10 = jnp.sum(d_proj.astype(F32), axis=0)
    g_out = dot_left(att_low, d_proj)
    d_att = dot_right(d_proj, w_out).astype(BF).reshape(seqs, slots, HEADS, HD)
    d_probs = jnp.einsum("sqhd,skhd->shqk", d_att, v4, preferred_element_type=F32)
    delta = jnp.sum(d_probs * probs, axis=-1, keepdims=True)
    d_scores = (probs * (d_probs - delta)).astype(BF)
    d_q = jnp.einsum("shqk,skhd->sqhd", d_scores, k4, preferred_element_type=F32) * HD ** (-0.5)
    d_k = jnp.einsum("shqk,sqhd->skhd", d_scores, q4, preferred_element_type=F32) * HD ** (-0.5)
    d_v = jnp.einsum("shqk,sqhd->skhd", probs_low, d_att, preferred_element_type=F32)
    d_q = d_q.reshape(-1, D).astype(BF)
    d_k = d_k.reshape(-1, D).astype(BF)
    d_v = d_v.reshape(-1, D).astype(BF)
    d8 = jnp.sum(d_q.astype(F32), axis=0)
    d9 = jnp.sum(d_v.astype(F32), axis=0)
    g_q = dot_left(x0_rows_low, d_q)
    g_k = dot_left(x0_low, d_k)
    g_v = dot_left(x0_low, d_v)
    d_rows = d_one + dot_right(d_q, w_qkv[:, :D])
    d_zero = dot_right(d_k, w_qkv[:, D : 2 * D]) + dot_right(d_v, w_qkv[:, 2 * D :])
    d_zero = d_zero.at[row_index].add(jnp.where(live[:, None], d_rows, 0.0))
    d_emb, d0, d1 = norm_backward(d_zero, normal0, inverse0, vec[:, 0])
    d_emb_low = d_emb.astype(BF)
    d13 = jnp.sum(jnp.where(masked_flat[:, None], d_emb_low.astype(F32), 0.0), axis=0)
    g_table = dot_left(latent_low, d_logits) + dot_left(d_emb_low, onehot)
    g_vec = jnp.stack([d0, d1, d2, d3, d4, d5, d6, d7, d8, d9, d10, d11, d12, d13], axis=1)
    g_vec = jnp.pad(g_vec, ((0, 0), (0, OUT_AT - VEC_AT - NVEC)))
    g_join = jnp.concatenate([g_q, g_k, g_v, g_vec, g_out, g_up, g_trans], axis=1)
    return loss_part, present, g_join.astype(BF), g_down.astype(BF), g_table.astype(BF)


def adamw(weight, first, second, gradient, rate):
    first = 0.5 * first + 0.5 * gradient
    second = 0.5 * second + 0.5 * gradient * gradient
    fix = 1.0 - 0.5**STEP
    step = first / fix / (jnp.sqrt(second / fix) + adam_eps)
    return (first, second, weight - rate * (step + decay_rate * weight))


def body(
    n_dp, n_vocab, tokens, picks, species,
    table, table_m, table_v, qkv_w, qkv_m, qkv_v, out_w, out_m, out_v, up_w, up_m, up_v,
    down_w, down_m, down_v, trans_w, trans_m, trans_v, vectors, vectors_m, vectors_v,
):
    block, columns = table.shape
    wide = padded(block)
    rows = qkv_w.shape[0]
    seqs, seq_len = tokens.shape
    both = ("dp", "vocab")
    own_kernels = n_dp == 8 and n_vocab * rows % 16 == 0 and rows % 8 == 0 and columns % 16 == 0 and seqs == 2
    own_kernels = own_kernels and part_cols(wide) * T_PARTS == wide
    if own_kernels:
        column = np.arange(wide * n_vocab)
        token = np.array(token_of(column, block, n_vocab, wide, np))
        col_floor = np.where((token >= 0) & (token < VREAL), 0.0, floor_value).astype(np.float32)[None, :]
        inputs = dict(
            table_in=table.T, down_w=down_w, qkv_w=qkv_w, vectors=vectors.T, out_w=out_w, up_w=up_w, trans_w=trans_w,
            tokens=tokens, picks=picks, species=species, col_floor=jnp.asarray(col_floor),
        )
        saved, counts, loss = forward(inputs, n_dp, n_vocab)
        g_join, g_down, g_table, tile = backward(saved, loss, n_dp, n_vocab)
        states = (
            (table.T, table_m.T, table_v.T), (qkv_w, qkv_m, qkv_v), (vectors.T, vectors_m.T, vectors_v.T),
            (out_w, out_m, out_v), (up_w, up_m, up_v), (trans_w, trans_m, trans_v), (down_w, down_m, down_v),
        )
        new = list(update(tile, counts, g_join, g_down, g_table, states))
        for index in (0, 2):
            new[4 * index : 4 * index + 4] = [array.T for array in new[4 * index : 4 * index + 4]]
        order = (0, 1, 3, 4, 6, 5)
        outs = [new[4 * index + part] for index in order for part in range(4)] + new[8:11]
        return tuple(outs) + tuple(array.reshape(()) for array in new[28:])
    col_token = token_of(jnp.arange(wide * n_vocab, dtype=jnp.int32), block, n_vocab, wide, jnp)
    joined = jnp.concatenate(
        [qkv_w, jnp.pad(vectors, ((0, 0), (0, OUT_AT - VEC_AT - NVEC))), out_w, up_w, trans_w], axis=1
    ).astype(BF)
    down_low = down_w.astype(BF)
    table_t = jnp.pad(table.T.astype(BF), ((0, 0), (0, wide - block)))
    counts = species_counts(picks, species, seq_len)
    piece = part_cols(wide)
    parts = wide // piece
    join_all = lax.all_gather(joined, both, axis=0, tiled=True)
    down_all = lax.all_gather(down_low, both, axis=0, tiled=True)
    table_all = lax.all_gather(table_t, "dp", axis=0, tiled=True).reshape(D, parts, 1, piece)
    table_all = lax.all_gather(table_all, "vocab", axis=2, tiled=True).reshape(D, wide * n_vocab)
    counts = lax.psum(counts, both)
    loss, present, g_join, g_down, g_table = local_step(
        tokens, picks, species, counts, join_all, down_all, table_all, col_token
    )
    g_join = lax.psum_scatter(g_join.astype(F32), both, scatter_dimension=0, tiled=True)
    g_down = lax.psum_scatter(g_down.astype(F32), both, scatter_dimension=0, tiled=True)
    g_table = lax.psum_scatter(g_table, "dp", scatter_dimension=0, tiled=True)
    g_table = g_table.reshape(columns, parts, n_vocab, piece)
    g_table = lax.psum_scatter(g_table, "vocab", scatter_dimension=2, tiled=True)
    g_table = g_table.reshape(columns, wide).astype(F32)
    square = jnp.sum(g_join * g_join) + jnp.sum(g_down * g_down) + jnp.sum(g_table * g_table)
    square, loss_sum = lax.psum((square, loss), both)
    grad_norm = jnp.sqrt(square)
    factor = jnp.minimum(1.0, clip_limit / (grad_norm + 1e-06))
    grads = (
        g_table[:, :block].T, g_join[:, : 3 * D], g_join[:, OUT_AT : OUT_AT + D], g_join[:, UP_AT : UP_AT + FF],
        g_down, g_join[:, TRANS_AT:], g_join[:, VEC_AT : VEC_AT + NVEC],
    )
    masters = (table, qkv_w, out_w, up_w, down_w, trans_w, vectors)
    firsts = (table_m, qkv_m, out_m, up_m, down_m, trans_m, vectors_m)
    seconds = (table_v, qkv_v, out_v, up_v, down_v, trans_v, vectors_v)
    outs = []
    for index in range(7):
        rate = vector_rate if index == 6 else matrix_rate
        first, second, new = adamw(masters[index], firsts[index], seconds[index], grads[index] * factor, rate)
        outs.extend([first, second, new])
        if index < 6:
            outs.append(new.astype(BF))
    return tuple(outs) + (loss_sum, present, grad_norm)


def solution(mesh):
    both = P(("dp", "vocab"), None)
    split = P("vocab", "dp")
    in_specs = (both, both, P(("dp", "vocab"))) + (split,) * 3 + (both,) * 18
    out_specs = (split,) * 4 + (both,) * 23 + (P(),) * 3
    step = functools.partial(body, mesh.shape["dp"], mesh.shape["vocab"])
    return jax.shard_map(step, mesh=mesh, in_specs=in_specs, out_specs=out_specs, check_vma=False)
```
